32 devices in a mesh: ew: 8 (over z, y), ns: 4 (over x, core).
Axes of the slice: x: 2, y: 2, z: 4, core: 2. Of those that a mesh axis runs over, the one named last changes fastest.
Arguments:
- theta: float32 [16, 32, 1024], P(None, 'ns', 'ew'), may hold values from -6 to 6
- velocity: float32 [2, 16, 32, 1024], P(None, None, 'ns', 'ew'), may hold values from -1.2 to 1.2
- diffusivity: float32 [16, 32, 1024], P(None, 'ns', 'ew'), may hold values from 0.02 to 0.2
- land_mask: int32 [4, 8], P('ns', 'ew'), may hold values from 0 to 1, as said below
- fold_partner: int32 [8], P('ew'), may hold values from 0 to 7, as said below
- atm_flux: bfloat16 [4, 8, 6, 128], P('ns', 'ew'), may hold values from -6 to 6
- remap_src: int32 [4, 8, 4], P('ns', 'ew'), may hold values from 0 to 7, as said below
- remap_weights: bfloat16 [4, 8, 4, 128, 1024], P('ns', 'ew'), may hold values from -0.25 to 0.25
Outputs:
- theta_out: float32 [16, 32, 1024], P(None, 'ns', 'ew')
- ocean_flux: float32 [4, 8, 6, 1024], P('ns', 'ew')
The draws below stay inside these ranges and needn't reach their ends.
Inputs may be any that keep to these rules, and one draw needn't show every extreme that they name: A pairing of the block columns: fold_partner[fold_partner[e]] = e and fold_partner[e] != e. `land_mask`: the top block row is wet. `remap_src`: distinct columns of an ocean block; one of them is (its own column + 4) mod 8.
All inputs are finite; a program needn't handle non-finite values.
Results may differ from the reference program's by a relative error of at most 0.0007.
Values may be sent and summed in bfloat16 or wider, within the bound.
No kernel may reach another device: no remote copies, remote signals or barrier semaphores. Data moves between devices by JAX's collectives and lax.ppermute only.
A program may use at most 64 MiB of HBM per device.

```python
import math
import jax
import jax.numpy as jnp
from jax import lax

CX = 128
CY = 8
NZ = 16
AC = 128
NF = 6
PAIRS = 4
STEPS = 3
EWB = 8
NSB = 4
NX = 1024
NY = 32
OC = 1024


def draw_fold_partner(key, part):
    key = jax.random.fold_in(key, 12)
    first_key, second_key = jax.random.split(key)
    anchor = jax.random.randint(first_key, (), 0, EWB).astype(jnp.int32)
    half = EWB // 2
    others = jnp.concatenate([jnp.arange(1, half, dtype=jnp.int32), jnp.arange(half + 1, EWB, dtype=jnp.int32)])
    shuffled = jax.random.permutation(second_key, others).astype(jnp.int32)
    columns = ((anchor + shuffled) % EWB).astype(jnp.int32)
    left = columns[0::2]
    right = columns[1::2]
    partner = jnp.zeros((EWB,), jnp.int32)
    partner = partner.at[left].set(right).at[right].set(left)
    across = ((anchor + half) % EWB).astype(jnp.int32)
    partner = partner.at[anchor].set(across).at[across].set(anchor)
    return partner.astype(jnp.int32)


def draw_land_mask(key, part):
    key = jax.random.fold_in(key, 13)
    levels = jax.random.randint(key, (NSB, EWB), 0, 4)
    wet = (levels > 0).astype(jnp.int32)
    return wet.at[NSB - 1].set(1).astype(jnp.int32)


def draw_remap_src(key, part):
    key = jax.random.fold_in(key, 11)
    offsets = jnp.arange(EWB, dtype=jnp.int32)
    scores = jax.random.randint(key, (NSB, EWB, EWB), 0, 2 ** 20) * EWB + offsets
    scores = jnp.where(offsets == EWB // 2, 2 ** 30, scores)
    order = jnp.argsort(scores, axis=-1)[..., :PAIRS - 1].astype(jnp.int32)
    far = jnp.full((NSB, EWB, 1), EWB // 2, jnp.int32)
    chosen = jnp.concatenate([far, order], axis=-1)
    columns = jnp.arange(EWB, dtype=jnp.int32)[None, :, None] + chosen
    return (columns % EWB).astype(jnp.int32)


def block_levels(key, shape, cuts, least, largest):
    level, own = 1.0, jax.random.fold_in(key, 6)
    for axis_at, blocks in cuts:
        draws = jnp.exp(jax.random.uniform(jax.random.fold_in(own, axis_at), (blocks,), jnp.float32, least / len(cuts), largest / len(cuts)))
        level = level * jnp.repeat(draws, shape[axis_at] // blocks).reshape([-1 if axis == axis_at else 1 for axis in range(len(shape))])
    return level


def noise(rng, shape, deviation, reach, cuts=(), kind=jnp.bfloat16):
    result = deviation * jax.random.normal(rng, shape, jnp.float32)
    if cuts:
        result = result * block_levels(rng, shape, cuts, -0.22, 0.18)
    return jnp.clip(result, -reach, reach).astype(kind)


def setup_inputs(seed: int = 0) -> dict:
    arg_keys = jax.random.split(jax.random.key(seed), 9)
    return {
        "theta": noise(arg_keys[0], (NZ, NY, NX), 1.0, 6.0, ((1, 4), (2, 8)), jnp.float32),
        "velocity": noise(arg_keys[1], (2, NZ, NY, NX), 0.3, 1.2, ((2, 4), (3, 8)), jnp.float32),
        "diffusivity": jnp.clip(jnp.exp(math.log(0.2) - 2.3025851 * jax.random.uniform(arg_keys[2], (NZ, NY, NX), jnp.float32) ** block_levels(arg_keys[2], (NZ, NY, NX), ((1, 4), (2, 8)), -0.2, 0.2)), 0.02, 0.2),
        "land_mask": draw_land_mask(jax.random.fold_in(arg_keys[8], 71), 0),
        "fold_partner": draw_fold_partner(jax.random.fold_in(arg_keys[8], 71), 0),
        "atm_flux": noise(arg_keys[5], (NSB, EWB, NF, AC), 1.0, 6.0, ((0, 4), (1, 8))),
        "remap_src": draw_remap_src(jax.random.fold_in(arg_keys[8], 71), 0),
        "remap_weights": noise(arg_keys[7], (NSB, EWB, PAIRS, AC, OC), (AC * PAIRS) ** -0.5, 0.25, ((0, 4), (1, 8))),
    }


COEFS = (0.5, -0.3, 0.2, 0.4, -0.25, 0.35)


def remap_row(row):
    atm_row, src_row, weight_row = row
    picked = atm_row[src_row].astype(jnp.float32)
    return jnp.einsum("epka,epao->eko", picked, weight_row.astype(jnp.float32))


def reference(theta, velocity, diffusivity, land_mask, fold_partner, atm_flux, remap_src, remap_weights):
    ocean_flux = lax.map(remap_row, (atm_flux, remap_src, remap_weights))
    coef = jnp.array(COEFS, jnp.float32)
    combined = jnp.einsum("k,neko->neo", coef, ocean_flux)
    forcing = 0.1 * combined.reshape(NSB, EWB, CY, CX).transpose(0, 2, 1, 3).reshape(NY, NX)
    wet = jnp.repeat(jnp.repeat(land_mask.astype(jnp.float32), CY, 0), CX, 1)
    east_u = velocity[0]
    north_v = velocity[1]
    field = theta
    for step in range(STEPS):
        east = jnp.roll(field, -1, 2)
        west = jnp.roll(field, 1, 2)
        south = jnp.concatenate([jnp.zeros((NZ, 1, NX), jnp.float32), field[:, :-1, :]], 1)
        top_row = field[:, -1, :].reshape(NZ, EWB, CX)
        ghost = top_row[:, fold_partner, ::-1].reshape(NZ, 1, NX)
        north = jnp.concatenate([field[:, 1:, :], ghost], 1)
        lap = east + west + north + south - 4.0 * field
        adv = 0.5 * (east_u * (east - west) + north_v * (north - south))
        tend = diffusivity * lap - adv
        tend = tend.at[0].add(forcing)
        field = field + wet * tend
    return field, ocean_flux
```

```python
import jax
import jax.numpy as jnp
from jax import lax
from jax.experimental import pallas as pl
from jax.experimental.pallas import tpu as pltpu
from jax.sharding import PartitionSpec as P

COEFS = (0.5, -0.3, 0.2, 0.4, -0.25, 0.35)
VMEM = pl.BlockSpec(memory_space=pltpu.VMEM)
SMEM = pl.BlockSpec(memory_space=pltpu.SMEM)
HBM = pl.BlockSpec(memory_space=pltpu.HBM)
PARAMS = pltpu.CompilerParams(vmem_limit_bytes=16 * 1024 * 1024)
F32 = jnp.float32
BF16 = jnp.bfloat16
KINDS = 6
BLOCK = 16


def stencil(t, east, west, north, south, u, v, d):
    return t + d * (east + west + north + south - 4.0 * t) - 0.5 * (u * (east - west) + v * (north - south))


def split(rows, devices):
    each = -(-rows // devices)
    return each, -(-rows // each)


class Place:
    def __init__(self):
        self.count, self.block_rows = lax.axis_size("ew"), lax.axis_size("ns")
        self.devices = self.count * self.block_rows
        self.e, self.n = lax.axis_index("ew"), lax.axis_index("ns")
        self.top = self.block_rows - 1
        self.is_top = self.n == self.top
        self.has_south = self.n > 0
        self.even = lax.rem(self.n, 2) == 0
        self.east = lax.rem(self.e + 1, self.count)
        self.west = lax.rem(self.e + self.count - 1, self.count)
        self.above = jnp.minimum(self.n + 1, self.top)
        self.below = jnp.maximum(self.n - 1, 0)

    def slot(self, e, n):
        return e * self.block_rows + n


def fill(size, rows):
    parts, at = [], 0
    for index in sorted(rows):
        if index > at:
            parts.append(jnp.zeros((index - at, size), F32))
        parts.append(rows[index])
        at = index + 1
    if at < size:
        parts.append(jnp.zeros((size - at, size), F32))
    return jnp.concatenate(parts, axis=0)


def turn(field):
    return field.reshape(field.shape[0] * field.shape[1], field.shape[2]).T


def shifted(field, axis, back):
    size = field.shape[axis]
    return pltpu.roll(field, size - 1 if back else 1, axis)


def first_kernel(
    mask_ref, partner_ref, theta_hbm, vel_hbm, diff_hbm, atm_hbm, weights_hbm,
    out_ref, near_ref, far_ref, theta_ref, coef_ref, weights_ref,
    atm_ref, bulk_ref, sems,
):
    here = Place()
    copies = [
        pltpu.make_async_copy(theta_hbm, theta_ref, sems.at[0]),
        pltpu.make_async_copy(vel_hbm, coef_ref.at[pl.ds(0, 2)], sems.at[1]),
        pltpu.make_async_copy(diff_hbm, coef_ref.at[2], sems.at[2]),
        pltpu.make_async_copy(atm_hbm, atm_ref, sems.at[3]),
        pltpu.make_async_copy(weights_hbm, weights_ref, sems.at[4]),
    ]
    for copy in copies:
        copy.start()
    for copy in copies[:4]:
        copy.wait()
    levels, rows, cols = theta_ref.shape
    wet = mask_ref[0, 0].astype(F32)
    t = theta_ref[...]
    u, v, d = wet * coef_ref[0], wet * coef_ref[1], wet * coef_ref[2]
    coef_ref[0], coef_ref[1], coef_ref[2] = u, v, d
    ahead = stencil(
        t, shifted(t, 2, True), shifted(t, 2, False), shifted(t, 1, True), shifted(t, 1, False), u, v, d
    )
    last = rows - 1
    for kind, (field, row) in enumerate(((t, 0), (t, 1), (ahead, 1), (u, 0), (v, 0), (d, 0))):
        low, high = field[:, row, :], field[:, last - row, :]
        near_ref[kind] = jnp.where(here.even, high, low)
        far_ref[kind] = jnp.where(here.even, low, high)
        bulk_ref[pl.ds(kind * levels, levels), :] = high
    turned, across = turn(t), [turn(u), turn(v), turn(d)]
    lane = lax.broadcasted_iota(jnp.int32, (1, cols), 1)
    second = jnp.where(lane == 0, partner_ref[0].astype(F32), turned[1:2])
    columns = [turned[0:1], second, turned[cols - 2 : cols - 1], turned[cols - 1 : cols]]
    atm = atm_ref[...].astype(F32)
    at = 7 + atm.shape[0]
    rest = jnp.zeros((BLOCK - at, cols), F32)
    to_west = jnp.concatenate(columns + [part[0:1] for part in across] + [atm, rest], axis=0)
    to_east = jnp.concatenate(columns + [part[cols - 1 : cols] for part in across] + [atm, rest], axis=0)
    line = lax.broadcasted_iota(jnp.int32, (BLOCK, cols), 0)
    each, holders = split(KINDS * levels, here.devices)
    for target in range(here.devices):
        block = jnp.where(target // here.block_rows == here.east, to_east, to_west)
        if target < holders:
            for k in range(each):
                piece = bulk_ref[pl.ds(k * holders + target, 1), :]
                block = jnp.where(line == at + k, piece, block)
        out_ref[target] = block.astype(BF16)
    copies[4].wait()


def middle_kernel(
    mask_ref, partner_ref, src_ref, theta_ref, coef_ref, weights_ref, recv_ref, near_ref, far_ref,
    flux_ref, force_ref, next_ref, out_ref,
):
    here = Place()
    levels, rows, cols = theta_ref.shape
    fields = flux_ref.shape[0]
    wet = mask_ref[0, 0].astype(F32)

    total = None
    for pair in range(weights_ref.shape[0]):
        block = recv_ref[here.slot(src_ref[0, 0, pair], here.n)][7 : 7 + fields]
        term = jnp.dot(block, weights_ref[pair], preferred_element_type=F32)
        total = term if total is None else total + term
    force = jnp.zeros((rows, cols), F32)
    for k in range(fields):
        grid = jnp.concatenate([total[k : k + 1, r * cols : (r + 1) * cols] for r in range(rows)], axis=0)
        flux_ref[k] = grid
        force = force + COEFS[k] * grid
    force = wet * (0.1 * force)
    force_ref[...] = force

    t = theta_ref[...]
    lane = lax.broadcasted_iota(jnp.int32, t.shape, 2)
    line = lax.broadcasted_iota(jnp.int32, t.shape, 1)
    level = lax.broadcasted_iota(jnp.int32, t.shape, 0)
    from_west = recv_ref[here.slot(here.west, here.n)].astype(F32)
    from_east = recv_ref[here.slot(here.east, here.n)].astype(F32)
    folded = recv_ref[here.slot(partner_ref[0], here.n)].astype(F32)
    sides = fill(cols, {0: from_west[3:4], cols - 1: from_east[0:1]}).T.reshape(t.shape)
    corner = fill(cols, {0: folded[3:4], 1: folded[2:3], cols - 2: folded[1:2], cols - 1: folded[0:1]})
    corner = corner.T.reshape(t.shape)[:, rows - 1, :]
    above = jnp.where(here.is_top, corner, jnp.where(here.even, near_ref[0], far_ref[0]))
    below = jnp.where(here.has_south, jnp.where(here.even, far_ref[0], near_ref[0]), 0.0)
    east = jnp.where(lane == cols - 1, sides, shifted(t, 2, True))
    west = jnp.where(lane == 0, sides, shifted(t, 2, False))
    north = jnp.where(line == rows - 1, above[:, None, :], shifted(t, 1, True))
    south = jnp.where(line == 0, below[:, None, :], shifted(t, 1, False))
    t = stencil(t, east, west, north, south, coef_ref[0], coef_ref[1], coef_ref[2])
    t = t + jnp.where(level == 0, force[None], 0.0)
    next_ref[...] = t

    each, _ = split(KINDS * levels, here.devices)
    at = 7 + fields
    held = [recv_ref[here.slot(s, here.top)].astype(F32) for s in range(here.count)]
    partners = jnp.concatenate([block[1:2] for block in held], axis=0)[:, 0:1]
    routed = []
    for k in range(each):
        pick = jnp.zeros((here.count, cols), F32)
        for s in range(here.count):
            pick = jnp.where(partners == float(s), held[s][at + k : at + k + 1], pick)
        routed.append(pick)

    turned = turn(t)
    columns = [turned[0:1], turned[1:2], turned[cols - 2 : cols - 1], turned[cols - 1 : cols]]
    across = jnp.concatenate([force, jnp.zeros((cols - rows, cols), F32)], axis=0).T
    high = [force[rows - 1 : rows], force[rows - 2 : rows - 1]]
    rest = [jnp.zeros((BLOCK - 7, cols), F32)]
    low = force[0:1], force[1:2]
    line = lax.broadcasted_iota(jnp.int32, (BLOCK, cols), 0)
    base = jnp.concatenate(columns + high + [across[0:1]] + rest, axis=0)
    to_east = jnp.where(line == 6, across[cols - 1 : cols], base)
    to_below = jnp.where(line == 4, low[0], jnp.where(line == 5, low[1], base))
    for target in range(here.devices):
        e, n = target // here.block_rows, target % here.block_rows
        block = jnp.where(n == here.n - 1, to_below, jnp.where(e == here.east, to_east, base))
        for k in range(each):
            block = jnp.where(line == 7 + k, routed[k][e : e + 1], block)
        out_ref[target] = block.astype(BF16)


def last_kernel(
    partner_ref, theta_ref, coef_ref, next_ref, force_ref, first_ref, second_ref, near_ref, far_ref, result_ref
):
    here = Place()
    levels, rows, cols = theta_ref.shape
    last = rows - 1
    partner = partner_ref[0]

    def got(e, n):
        return second_ref[here.slot(e, n)].astype(F32)

    each, holders = split(KINDS * levels, here.devices)
    bulk = [second_ref[i].astype(F32)[7 : 7 + each] for i in range(holders)]
    bulk = jnp.concatenate([part[k : k + 1] for k in range(each) for part in bulk], axis=0)
    mirror = cols - 1 - lax.broadcasted_iota(jnp.int32, (KINDS * levels, cols), 1)
    bulk = jnp.take_along_axis(bulk[: KINDS * levels], mirror, axis=1)
    north, south = [], []
    for kind in range(KINDS):
        fold = bulk[kind * levels : (kind + 1) * levels]
        fold = -fold if kind in (3, 4) else fold
        near, far = near_ref[kind], far_ref[kind]
        north.append(jnp.where(here.is_top, fold, jnp.where(here.even, near, far)))
        south.append(jnp.where(here.has_south, jnp.where(here.even, far, near), 0.0))

    west, east = got(here.west, here.n), got(here.east, here.n)
    over, under = got(here.e, here.above), got(here.e, here.below)
    fold = got(partner, here.n)
    fold_east = got(lax.rem(partner + 1, here.count), here.n)
    fold_west = got(lax.rem(partner + here.count - 1, here.count), here.n)
    over_west, over_east = got(here.west, here.above), got(here.east, here.above)
    under_west, under_east = got(here.west, here.below), got(here.east, here.below)
    is_top, has_south = here.is_top, here.has_south
    ends = fill(
        cols,
        {
            0: jnp.where(is_top, fold[3:4], over[0:1]),
            1: under[0:1],
            2: jnp.where(is_top, fold_east[0:1], over_west[3:4]),
            3: under_west[3:4],
            cols - 4: under_east[0:1],
            cols - 3: jnp.where(is_top, fold_west[3:4], over_east[0:1]),
            cols - 2: under[3:4],
            cols - 1: jnp.where(is_top, fold[0:1], over[3:4]),
        },
    ).T.reshape(theta_ref.shape)
    lane = lax.broadcasted_iota(jnp.int32, (levels, cols), 1)
    level = lax.broadcasted_iota(jnp.int32, (levels, cols), 0)

    def capped(row, values, lanes):
        low = pltpu.roll(values, cols - lanes, 1) if lanes else values
        high = pltpu.roll(values, lanes, 1) if lanes else values
        return jnp.where(lane == 0, low, jnp.where(lane == cols - 1, high, row))

    def forced(row, force):
        return row + jnp.where(level == 0, force, 0.0)

    north_ends = jnp.where(is_top, ends[:, last, :], ends[:, 0, :])
    north_inner = jnp.where(is_top, ends[:, last - 1, :], ends[:, 1, :])
    south_ends, south_inner = ends[:, last, :], ends[:, last - 1, :]
    flip = cols - 1 - lax.broadcasted_iota(jnp.int32, (8, cols), 1)
    flipped = jnp.take_along_axis(fold[0:8], flip, axis=1)
    north_force = [jnp.where(is_top, flipped[k : k + 1], over[k : k + 1]) for k in (4, 5)]
    south_force = [under[4:5], under[5:6]]
    t0 = theta_ref[...]

    def rim(rows_of, inside, outward, force, edge, inner, at):
        edge_row = stencil(
            rows_of[0], shifted(rows_of[0], 1, True), shifted(rows_of[0], 1, False),
            rows_of[1] if outward else inside, inside if outward else rows_of[1], *rows_of[3:],
        )
        return capped(forced(edge_row, force[0]), edge, at), capped(forced(rows_of[2], force[1]), inner, at)

    north_one, north_two = rim(north, t0[:, last, :], True, north_force, north_ends, north_inner, 0)
    south_one, south_two = rim(south, t0[:, 0, :], False, south_force, south_ends, south_inner, 1)
    south_one, south_two = jnp.where(has_south, south_one, 0.0), jnp.where(has_south, south_two, 0.0)
    u, v, d = coef_ref[0], coef_ref[1], coef_ref[2]
    shape = t0.shape
    wide = lax.broadcasted_iota(jnp.int32, shape, 2)
    line = lax.broadcasted_iota(jnp.int32, shape, 1)
    force = jnp.where(lax.broadcasted_iota(jnp.int32, shape, 0) == 0, force_ref[...][None], 0.0)
    missing = (line == last) & (wide >= 2) & (wide < cols - 2) & is_top
    t = next_ref[...]
    t = t + jnp.where(missing, (d - 0.5 * v) * north[0][:, None, :], 0.0)

    def outer(row, beyond, inside, outward, rows_of, force_row, diagonal, lanes):
        low, high = pltpu.roll(diagonal, cols - lanes, 1), pltpu.roll(diagonal, lanes, 1)
        result = stencil(
            row, jnp.where(lane == cols - 1, high, shifted(row, 1, True)),
            jnp.where(lane == 0, low, shifted(row, 1, False)),
            beyond if outward else inside, inside if outward else beyond, *rows_of[3:],
        )
        return forced(result, force_row)

    north_next = outer(north_one, north_two, t[:, last, :], True, north, north_force[0], north_ends, 2)
    south_next = outer(south_one, south_two, t[:, 0, :], False, south, south_force[0], south_ends, 3)
    south_next = jnp.where(has_south, south_next, 0.0)

    turned = turn(t)
    first_west = first_ref[here.slot(here.west, here.n)].astype(F32)
    first_east = first_ref[here.slot(here.east, here.n)].astype(F32)
    top_west, top_east = jnp.zeros((1, cols), F32), jnp.zeros((1, cols), F32)
    for s in range(here.count):
        block = got(s, here.n)
        top_west = jnp.where(first_west[1:2, 0:1] == float(s), block[0:1], top_west)
        top_east = jnp.where(first_east[1:2, 0:1] == float(s), block[3:4], top_east)

    def pair(low, high):
        return jnp.concatenate([low, high, jnp.zeros((6, cols), F32)], axis=0)

    side = pair(west[3:4], east[0:1])
    place = lax.rem(lax.broadcasted_iota(jnp.int32, (8, cols), 1), rows)
    corner = jnp.where(
        is_top, pair(top_west, top_east), pltpu.roll(pair(over_west[3:4], over_east[0:1]), rows - 1, 1)
    )
    side_north = jnp.where(place == last, corner, shifted(side, 1, True))
    corner = pltpu.roll(pair(under_west[3:4], under_east[0:1]), cols - rows + 1, 1)
    side_south = jnp.where(place == 0, jnp.where(has_south, corner, 0.0), shifted(side, 1, False))
    side_next = stencil(
        side, pair(turned[0:1], east[1:2]), pair(west[2:3], turned[cols - 1 : cols]), side_north, side_south,
        *[pair(first_west[k : k + 1], first_east[k : k + 1]) for k in (4, 5, 6)],
    ) + pair(west[6:7], east[6:7])

    def advance(t, sides, above, below):
        return force + stencil(
            t,
            jnp.where(wide == cols - 1, sides, shifted(t, 2, True)),
            jnp.where(wide == 0, sides, shifted(t, 2, False)),
            jnp.where(line == last, above[:, None, :], shifted(t, 1, True)),
            jnp.where(line == 0, below[:, None, :], shifted(t, 1, False)),
            u, v, d,
        )

    def columns(low, high):
        return fill(cols, {0: low, cols - 1: high}).T.reshape(shape)

    t = advance(t, columns(west[3:4], east[0:1]), north_one, south_one)
    result_ref[...] = advance(t, columns(side_next[0:1], side_next[1:2]), north_next, south_next)


def exchange(blocks):
    return lax.all_to_all(blocks, ("ew", "ns"), split_axis=0, concat_axis=0, tiled=True)


def swap(rows, first):
    pairs = [(i, i + 1) for i in range(first, lax.axis_size("ns") - 1, 2)]
    return lax.ppermute(rows, "ns", pairs + [(b, a) for a, b in pairs])


def local(theta, velocity, diffusivity, land_mask, fold_partner, atm_flux, remap_src, remap_weights):
    levels, rows, cols = theta.shape
    fields = atm_flux.shape[2]
    shape = jax.ShapeDtypeStruct
    devices = lax.axis_size("ew") * lax.axis_size("ns")
    whole = shape(theta.shape, F32)
    blocks = shape((devices, BLOCK, cols), BF16)
    edge = shape((KINDS, levels, cols), F32)
    weights = remap_weights[0, 0]
    out, near, far, field, coef, weights = pl.pallas_call(
        first_kernel,
        out_shape=(blocks, edge, edge, whole, shape((3,) + theta.shape, F32), shape(weights.shape, BF16)),
        in_specs=[SMEM] * 2 + [HBM] * 5,
        out_specs=(VMEM,) * 6,
        scratch_shapes=[
            pltpu.VMEM((fields, cols), BF16),
            pltpu.VMEM((KINDS * levels, cols), F32),
            pltpu.SemaphoreType.DMA((5,)),
        ],
        compiler_params=PARAMS,
        name="first",
    )(land_mask, fold_partner, theta, velocity, diffusivity, atm_flux[0, 0], weights)
    first = exchange(out)
    near, far = swap(near, 0), swap(far, 1)
    flux, force, after, out = pl.pallas_call(
        middle_kernel,
        out_shape=(shape((fields, rows, cols), F32), shape((rows, cols), F32), whole, blocks),
        in_specs=[SMEM] * 3 + [VMEM] * 6,
        out_specs=(VMEM,) * 4,
        compiler_params=PARAMS,
        name="middle",
    )(land_mask, fold_partner, remap_src, field, coef, weights, first, near, far)
    second = exchange(out)
    field = pl.pallas_call(
        last_kernel,
        out_shape=whole,
        in_specs=[SMEM] + [VMEM] * 8,
        out_specs=VMEM,
        compiler_params=PARAMS,
        name="last",
    )(fold_partner, field, coef, after, force, first, second, near, far)
    return field, flux.reshape(1, 1, fields, rows * cols)


def solution(mesh):
    return jax.shard_map(
        local,
        mesh=mesh,
        in_specs=(
            P(None, "ns", "ew"),
            P(None, None, "ns", "ew"),
            P(None, "ns", "ew"),
            P("ns", "ew"),
            P("ew"),
            P("ns", "ew", None, None),
            P("ns", "ew", None),
            P("ns", "ew", None, None, None),
        ),
        out_specs=(P(None, "ns", "ew"), P("ns", "ew", None, None)),
        check_vma=False,
    )
```

```python
import jax
import jax.numpy as jnp
from jax import lax
from jax.experimental import pallas as pl
from jax.experimental.pallas import tpu as pltpu
from jax.sharding import PartitionSpec as P

COEFS = (0.5, -0.3, 0.2, 0.4, -0.25, 0.35)
VMEM = pl.BlockSpec(memory_space=pltpu.VMEM)
SMEM = pl.BlockSpec(memory_space=pltpu.SMEM)
HBM = pl.BlockSpec(memory_space=pltpu.HBM)
PARAMS = pltpu.CompilerParams(vmem_limit_bytes=16 * 1024 * 1024)
F32 = jnp.float32
BF16 = jnp.bfloat16
KINDS = 6
BLOCK, TILE = 16, 8
FORCE_SLOT, WET_SLOT = 4, 5


def tendency(t, east, west, north, south, u, v, d):
    return d * (east + west + north + south - 4.0 * t) - 0.5 * (u * (east - west) + v * (north - south))


def stencil(t, *others):
    return t + tendency(t, *others)


class Place:
    def __init__(self):
        self.count, self.block_rows = lax.axis_size("ew"), lax.axis_size("ns")
        self.devices = self.count * self.block_rows
        self.e, self.n = lax.axis_index("ew"), lax.axis_index("ns")
        self.top = self.block_rows - 1
        self.is_top = self.n == self.top
        self.has_south = self.n > 0
        self.even = lax.rem(self.n, 2) == 0
        self.east = lax.rem(self.e + 1, self.count)
        self.west = lax.rem(self.e + self.count - 1, self.count)
        self.above = jnp.minimum(self.n + 1, self.top)
        self.below = jnp.maximum(self.n - 1, 0)
        self.pair = jnp.where(self.even, self.n + 1, self.n - 1)
        self.other = jnp.where(self.even, self.below, self.above)
        self.half = self.count // 2

    def slot(self, e, n):
        return e * self.block_rows + n


def fill(size, rows):
    parts, at = [], 0
    for index in sorted(rows):
        if index > at:
            parts.append(jnp.zeros((index - at, size), F32))
        parts.append(rows[index])
        at = index + 1
    if at < size:
        parts.append(jnp.zeros((size - at, size), F32))
    return jnp.concatenate(parts, axis=0)


def turn(field):
    return field.reshape(field.shape[0] * field.shape[1], field.shape[2]).T


def shifted(field, axis, back):
    size = field.shape[axis]
    return pltpu.roll(field, size - 1 if back else 1, axis)


def first_kernel(
    mask_hbm, partner_hbm, src_hbm, theta_hbm, vel_hbm, diff_hbm, atm_hbm, weights_hbm,
    out_ref, theta_ref, coef_ref, weights_ref, mask_ref, partner_ref, src_ref,
    atm_ref, bulk_ref, sems,
):
    here = Place()
    pairs = [
        (theta_hbm, theta_ref), (vel_hbm, coef_ref.at[pl.ds(0, 2)]), (diff_hbm, coef_ref.at[2]),
        (atm_hbm, atm_ref), (partner_hbm, partner_ref), (mask_hbm, mask_ref), (src_hbm, src_ref),
        (weights_hbm, weights_ref),
    ]
    copies = [pltpu.make_async_copy(a, b, sems.at[i]) for i, (a, b) in enumerate(pairs)]
    for copy in copies:
        copy.start()
    for copy in copies[:5]:
        copy.wait()
    levels, rows, cols = theta_ref.shape
    t = theta_ref[...]
    u, v, d = coef_ref[0], coef_ref[1], coef_ref[2]
    tend = tendency(
        t, shifted(t, 2, True), shifted(t, 2, False), shifted(t, 1, True), shifted(t, 1, False), u, v, d
    )
    last = rows - 1
    tiles = levels // TILE
    each = KINDS * tiles
    for kind, (field, row) in enumerate(((t, 0), (t, 1), (tend, 1), (u, 0), (v, 0), (d, 0))):
        high, low = field[:, last - row, :], field[:, row, :]
        bulk_ref[pl.ds(kind * tiles, tiles)] = high.reshape(tiles, TILE, cols)
        bulk_ref[pl.ds(each + kind * tiles, tiles)] = low.reshape(tiles, TILE, cols)
    turned, across = turn(t), [turn(u), turn(v), turn(d)]
    lane = lax.broadcasted_iota(jnp.int32, (1, cols), 1)
    second = jnp.where(lane == 1, partner_ref[0, 0].astype(F32), turned[1:2])
    columns = [turned[0:1], second, turned[cols - 2 : cols - 1], turned[cols - 1 : cols]]
    atm = atm_ref[...].astype(F32)
    begin = jnp.concatenate(columns + [atm[: TILE - 4]], axis=0)
    used = atm.shape[0] - (TILE - 4) + 3
    rest = [jnp.zeros((TILE - used, cols), F32)]
    base = jnp.concatenate([atm[TILE - 4 :]] + [part[0:1] for part in across] + rest, axis=0)
    to_east = jnp.concatenate([atm[TILE - 4 :]] + [part[cols - 1 : cols] for part in across] + rest, axis=0)
    for target in range(here.devices):
        e, n = target // here.block_rows, target % here.block_rows
        order = (e % here.half) * (here.block_rows - 1) + n - (here.n < n).astype(jnp.int32)
        upward = here.even if e < here.half else jnp.logical_not(here.even)
        tile = bulk_ref[jnp.where(upward, 0, each) + jnp.minimum(order, each - 1)]
        own = jnp.where(e == here.east, to_east, base)
        out_ref[target] = jnp.concatenate([begin, jnp.where(here.n == n, own, tile)], axis=0).astype(BF16)
    for copy in copies[5:]:
        copy.wait()


def middle_kernel(
    mask_ref, partner_ref, src_ref, theta_ref, coef_ref, weights_ref, recv_ref,
    flux_ref, force_ref, next_ref, out_ref,
):
    here = Place()
    levels, rows, cols = theta_ref.shape
    fields = flux_ref.shape[0]
    last = rows - 1
    wet = mask_ref[0, 0].astype(F32)

    pairs, cells, points = weights_ref.shape
    chosen = [recv_ref[here.slot(src_ref[0, pair], here.n)][4 : 4 + fields] for pair in range(pairs)]
    weights = weights_ref[...].reshape(pairs * cells, points)
    total = jnp.dot(jnp.concatenate(chosen, axis=1), weights, preferred_element_type=F32)
    force = jnp.zeros((rows, cols), F32)
    for k in range(fields):
        grid = jnp.concatenate([total[k : k + 1, r * cols : (r + 1) * cols] for r in range(rows)], axis=0)
        flux_ref[k] = grid
        force = force + COEFS[k] * grid
    force = wet * (0.1 * force)
    force_ref[...] = force

    t = theta_ref[...]
    u, v, d = wet * coef_ref[0], wet * coef_ref[1], wet * coef_ref[2]
    lane = lax.broadcasted_iota(jnp.int32, t.shape, 2)
    line = lax.broadcasted_iota(jnp.int32, t.shape, 1)
    level = lax.broadcasted_iota(jnp.int32, t.shape, 0)

    def got(e, n):
        return recv_ref[here.slot(e, n)].astype(F32)

    sides = fill(cols, {0: got(here.west, here.n)[3:4], cols - 1: got(here.east, here.n)[0:1]}).T.reshape(t.shape)
    fold, over, under = got(partner_ref[0, 0], here.n), got(here.e, here.above), got(here.e, here.below)
    spots = (0, 1, cols - 2, cols - 1)
    beyond = {spot: jnp.where(here.is_top, fold[3 - i : 4 - i], over[i : i + 1]) for i, spot in enumerate(spots)}
    beyond.update({spot + (2 if i < 2 else -2): under[i : i + 1] for i, spot in enumerate(spots)})
    beyond = fill(cols, beyond).T.reshape(t.shape)
    flat = lax.broadcasted_iota(jnp.int32, (levels, cols), 1)
    above = jnp.where(here.is_top, beyond[:, last, :], beyond[:, 0, :])
    above = jnp.where((flat < 2) | (flat >= cols - 2), above, 0.0)
    below = beyond[:, last, :]
    below = jnp.where(
        flat < 2, pltpu.roll(below, cols - 2, 1), jnp.where(flat >= cols - 2, pltpu.roll(below, 2, 1), 0.0)
    )
    below = jnp.where(here.has_south, below, 0.0)
    east = jnp.where(lane == cols - 1, sides, shifted(t, 2, True))
    west = jnp.where(lane == 0, sides, shifted(t, 2, False))
    north = jnp.where(line == last, above[:, None, :], shifted(t, 1, True))
    south = jnp.where(line == 0, below[:, None, :], shifted(t, 1, False))
    t = stencil(t, east, west, north, south, u, v, d)
    t = t + jnp.where(level == 0, force[None], 0.0)
    next_ref[...] = t

    held = [got(m, here.top) for m in range(here.count)]
    size = -(-here.count * TILE // cols) * cols
    tiles = [block[TILE:] for block in held] + [jnp.zeros((size - here.count * TILE, cols), F32)] * (size > here.count * TILE)
    tiles = jnp.concatenate(tiles, axis=0).astype(BF16)
    partners = jnp.concatenate([jnp.broadcast_to(block[1:2, 1:2], (TILE, 1)) for block in held], axis=0)
    wanted = TILE * partners + lax.rem(lax.broadcasted_iota(jnp.int32, partners.shape, 0), TILE).astype(F32)
    pick = lax.broadcasted_iota(jnp.int32, (here.count * TILE, size), 1).astype(F32) == wanted
    folded = jnp.dot(pick.astype(F32).astype(BF16), tiles, preferred_element_type=F32)

    turned = turn(t)
    slot = lax.broadcasted_iota(jnp.int32, (rows, rows, cols), 1)
    marks = jnp.where(slot == WET_SLOT, wet, 0.0)
    marks = [jnp.where(slot == FORCE_SLOT, force[:, None, :], marks)] + [marks] * (levels // rows - 1)
    marks = jnp.concatenate(marks, axis=0).reshape(cols, cols).T
    ends = jnp.concatenate([turned[0:1], turned[cols - 1 : cols], jnp.zeros((6, cols), F32)], axis=0)
    slot = lax.rem(lax.broadcasted_iota(jnp.int32, (1, cols), 1), 8)

    def corners(shifts, mark):
        row = mark
        for index, shift in enumerate(shifts):
            moved = pltpu.roll(ends, shift % cols, 1) if shift else ends
            row = jnp.where(slot == index, moved[index // 2 : index // 2 + 1], row)
        return row

    up, down = (-last, 2 - last, 2 - last, 4 - last), (0, 0, 2, 2)
    low_mark, high_mark = marks[0:1], marks[cols - 1 : cols]
    rest = jnp.zeros((TILE - 5, cols), F32)
    high_force, low_force = [force[last : last + 1], force[last - 1 : last]], [force[0:1], force[1:2]]
    low, high = [turned[0:1], turned[1:2]], [turned[cols - 1 : cols], turned[cols - 2 : cols - 1]]
    base = jnp.concatenate([corners(up, low_mark)] + high_force + low + [rest], axis=0)
    to_east = jnp.concatenate([corners(up, high_mark)] + high_force + high + [rest], axis=0)
    to_below = jnp.concatenate([corners(down, low_mark)] + low_force + low + [rest], axis=0)
    first_half = here.e < here.half
    for target in range(here.devices):
        e, n = target // here.block_rows, target % here.block_rows
        begin = jnp.where(n == here.n - 1, to_below, jnp.where(e == here.east, to_east, base))
        pair = n + 1 if n % 2 == 0 else n - 1
        other = max(n - 1, 0) if n % 2 == 0 else min(n + 1, here.top)
        tile = got(e, jnp.where(first_half, pair, other))[TILE:]
        if n == here.top:
            tile = jnp.where(first_half, tile, folded[e * TILE : (e + 1) * TILE])
        out_ref[target] = jnp.concatenate([begin, tile], axis=0).astype(BF16)


def last_kernel(
    mask_ref, partner_ref, theta_ref, coef_ref, next_ref, force_ref, first_ref, second_ref, result_ref,
):
    here = Place()
    levels, rows, cols = theta_ref.shape
    last = rows - 1
    partner = partner_ref[0, 0]
    wet = mask_ref[0, 0].astype(F32)
    is_top, has_south = here.is_top, here.has_south

    def got(e, n):
        return second_ref[here.slot(e, n)].astype(F32)

    west, east = got(here.west, here.n), got(here.east, here.n)
    over, under = got(here.e, here.above), got(here.e, here.below)
    fold = got(partner, here.n)
    fold_east = got(lax.rem(partner + 1, here.count), here.n)[0:1]
    fold_west = got(lax.rem(partner + here.count - 1, here.count), here.n)[0:1]
    over_west, over_east = got(here.west, here.above)[0:1], got(here.east, here.above)[0:1]
    under_west, under_east = got(here.west, here.below)[0:1], got(here.east, here.below)[0:1]
    first_west = first_ref[here.slot(here.west, here.n)].astype(F32)
    first_east = first_ref[here.slot(here.east, here.n)].astype(F32)

    def mark(block):
        return block[0:1, WET_SLOT : WET_SLOT + 1]

    tiles = KINDS * levels // TILE

    def gather(begin, source):
        found = []
        for k in range(tiles):
            e, order = k // (here.block_rows - 1), k % (here.block_rows - 1)
            found.append(got(begin + e, order + (source <= order).astype(jnp.int32))[TILE:])
        return jnp.concatenate(found, axis=0)

    near, far = gather(0, here.pair), gather(here.half, here.other)
    south = jnp.where(has_south, jnp.where(here.even, far, near), 0.0)
    north = jnp.where(here.even, near, far)
    mirror = cols - 1 - lax.broadcasted_iota(jnp.int32, north.shape, 1)
    north = jnp.where(is_top, jnp.take_along_axis(north, mirror, axis=1), north)

    def kinds(bulk, wet, sign):
        t, inner, tend, u, v, d = [bulk[kind * levels : (kind + 1) * levels] for kind in range(KINDS)]
        return t, inner, inner + wet * tend, (sign * wet) * u, (sign * wet) * v, wet * d

    north = kinds(north, jnp.where(is_top, mark(fold), mark(over)), jnp.where(is_top, -1.0, 1.0))
    south = kinds(south, mark(under), 1.0)

    top_west, top_east = jnp.zeros((1, cols), F32), jnp.zeros((1, cols), F32)
    for s in range(here.count):
        row = got(s, here.n)[0:1]
        top_west = jnp.where(first_west[1:2, 1:2] == float(s), row, top_west)
        top_east = jnp.where(first_east[1:2, 1:2] == float(s), row, top_east)
    moved = [fold[0:1], over[0:1], under[0:1], fold_west, over_west, under_west, top_east]
    moved = jnp.concatenate(moved + [jnp.zeros((1, cols), F32)], axis=0)
    moved = pltpu.roll(moved, cols - 2, 1)
    ends = fill(
        cols,
        {
            0: jnp.where(is_top, moved[0:1], over[0:1]),
            1: under[0:1],
            2: jnp.where(is_top, fold_east, moved[4:5]),
            3: moved[5:6],
            cols - 4: under_east,
            cols - 3: jnp.where(is_top, moved[3:4], over_east),
            cols - 2: moved[2:3],
            cols - 1: jnp.where(is_top, fold[0:1], moved[1:2]),
        },
    ).T.reshape(theta_ref.shape)
    edges, inners = ends[:, 0, :], ends[:, 1, :]
    lane = lax.broadcasted_iota(jnp.int32, (levels, cols), 1)
    level = lax.broadcasted_iota(jnp.int32, (levels, cols), 0)

    def capped(row, values, lanes):
        low = pltpu.roll(values, cols - lanes, 1) if lanes else values
        high = pltpu.roll(values, lanes, 1) if lanes else values
        return jnp.where(lane == 0, low, jnp.where(lane == cols - 1, high, row))

    def forced(row, force):
        return row + jnp.where(level == 0, force, 0.0)

    flip = cols - 1 - lax.broadcasted_iota(jnp.int32, (8, cols), 1)
    flipped = jnp.take_along_axis(fold[:TILE], flip, axis=1)
    north_force = [jnp.where(is_top, flipped[k : k + 1], over[k : k + 1]) for k in (1, 2)]
    south_force = [under[1:2], under[2:3]]
    t0 = theta_ref[...]

    def rim(rows_of, inside, outward, force, at):
        edge_row = stencil(
            rows_of[0], shifted(rows_of[0], 1, True), shifted(rows_of[0], 1, False),
            rows_of[1] if outward else inside, inside if outward else rows_of[1], *rows_of[3:],
        )
        return capped(forced(edge_row, force[0]), edges, at), capped(forced(rows_of[2], force[1]), inners, at)

    north_one, north_two = rim(north, t0[:, last, :], True, north_force, 0)
    south_one, south_two = rim(south, t0[:, 0, :], False, south_force, 1)
    south_one, south_two = jnp.where(has_south, south_one, 0.0), jnp.where(has_south, south_two, 0.0)
    u, v, d = wet * coef_ref[0], wet * coef_ref[1], wet * coef_ref[2]
    shape = t0.shape
    wide = lax.broadcasted_iota(jnp.int32, shape, 2)
    line = lax.broadcasted_iota(jnp.int32, shape, 1)
    force = jnp.where(lax.broadcasted_iota(jnp.int32, shape, 0) == 0, force_ref[...][None], 0.0)
    inside = (wide >= 2) & (wide < cols - 2)
    t = next_ref[...]
    t = t + jnp.where((line == last) & inside, (d - 0.5 * v) * north[0][:, None, :], 0.0)
    t = t + jnp.where((line == 0) & inside, (d + 0.5 * v) * south[0][:, None, :], 0.0)

    def outer(row, beyond, inside, outward, rows_of, force_row, lanes):
        low, high = pltpu.roll(edges, cols - lanes, 1), pltpu.roll(edges, lanes, 1)
        result = stencil(
            row, jnp.where(lane == cols - 1, high, shifted(row, 1, True)),
            jnp.where(lane == 0, low, shifted(row, 1, False)),
            beyond if outward else inside, inside if outward else beyond, *rows_of[3:],
        )
        return forced(result, force_row)

    north_next = outer(north_one, north_two, t[:, last, :], True, north, north_force[0], 2)
    south_next = outer(south_one, south_two, t[:, 0, :], False, south, south_force[0], 3)
    south_next = jnp.where(has_south, south_next, 0.0)

    def pair(low, high):
        return jnp.concatenate([low, high, jnp.zeros((6, cols), F32)], axis=0)

    turned = turn(t)
    side = pair(west[3:4], east[3:4])
    along = lax.broadcasted_iota(jnp.int32, (8, cols), 1)
    place = lax.rem(along, rows)
    corner = pair(jnp.where(is_top, top_west, moved[4:5]), jnp.where(is_top, moved[6:7], over_east))
    side_north = jnp.where(place == last, pltpu.roll(corner, last, 1), shifted(side, 1, True))
    corner = jnp.where(has_south, pair(moved[5:6], under_east), 0.0)
    side_south = jnp.where(place == 0, corner, shifted(side, 1, False))
    side_force = jnp.take_along_axis(pair(west[0:1], east[0:1]), jnp.where(along < rows, 8 * along, 0) + FORCE_SLOT, axis=1)
    side_next = stencil(
        side, pair(turned[0:1], east[4:5]), pair(west[4:5], turned[cols - 1 : cols]), side_north, side_south,
        *[pair(mark(west) * first_west[k : k + 1], mark(east) * first_east[k : k + 1]) for k in range(10, 13)],
    ) + jnp.where(along < rows, side_force, 0.0)

    def advance(t, sides, above, below):
        return force + stencil(
            t,
            jnp.where(wide == cols - 1, sides, shifted(t, 2, True)),
            jnp.where(wide == 0, sides, shifted(t, 2, False)),
            jnp.where(line == last, above[:, None, :], shifted(t, 1, True)),
            jnp.where(line == 0, below[:, None, :], shifted(t, 1, False)),
            u, v, d,
        )

    def columns(low, high):
        return fill(cols, {0: low, cols - 1: high}).T.reshape(shape)

    t = advance(t, columns(west[3:4], east[3:4]), north_one, south_one)
    result_ref[...] = advance(t, columns(side_next[0:1], side_next[1:2]), north_next, south_next)


def exchange(blocks):
    return lax.all_to_all(blocks, ("ew", "ns"), split_axis=0, concat_axis=0, tiled=True)


def local(theta, velocity, diffusivity, land_mask, fold_partner, atm_flux, remap_src, remap_weights):
    levels, rows, cols = theta.shape
    fields = atm_flux.shape[2]
    shape = jax.ShapeDtypeStruct
    devices = lax.axis_size("ew") * lax.axis_size("ns")
    blocks = (devices, BLOCK, cols)
    room = 60 * 2**20 - 2 * max(0, 2 * devices * BLOCK * cols - 2**20)
    scalars = [land_mask, fold_partner.reshape(1, 1), remap_src[0]]
    weights = remap_weights[0, 0]
    out, field, coef, weights, *scalars = pl.pallas_call(
        first_kernel,
        out_shape=(
            pltpu.VMEM(blocks, BF16), pltpu.VMEM(theta.shape, F32), pltpu.VMEM((3,) + theta.shape, F32),
            pltpu.VMEM(weights.shape, BF16),
        ) + tuple(pltpu.SMEM(x.shape, x.dtype) for x in scalars),
        in_specs=[HBM] * 8,
        out_specs=(VMEM,) * 4 + (SMEM,) * 3,
        scratch_shapes=[
            pltpu.VMEM((fields, cols), BF16),
            pltpu.VMEM((2 * KINDS * levels // TILE, TILE, cols), F32),
            pltpu.SemaphoreType.DMA((8,)),
        ],
        compiler_params=pltpu.CompilerParams(vmem_limit_bytes=room),
        name="first",
    )(*scalars, theta, velocity, diffusivity, atm_flux[0, 0], weights)
    first = exchange(out)
    flux, force, after, out = pl.pallas_call(
        middle_kernel,
        out_shape=(
            shape((fields, rows, cols), F32), pltpu.VMEM((rows, cols), F32), pltpu.VMEM(theta.shape, F32),
            pltpu.VMEM(blocks, BF16),
        ),
        in_specs=[SMEM] * 3 + [VMEM] * 4,
        out_specs=(VMEM,) * 4,
        compiler_params=PARAMS,
        name="middle",
    )(*scalars, field, coef, weights, first)
    second = exchange(out)
    field = pl.pallas_call(
        last_kernel,
        out_shape=shape(theta.shape, F32),
        in_specs=[SMEM] * 2 + [VMEM] * 6,
        out_specs=VMEM,
        compiler_params=PARAMS,
        name="last",
    )(*scalars[:2], field, coef, after, force, first, second)
    return field, flux.reshape(1, 1, fields, rows * cols)


def solution(mesh):
    return jax.shard_map(
        local,
        mesh=mesh,
        in_specs=(
            P(None, "ns", "ew"),
            P(None, None, "ns", "ew"),
            P(None, "ns", "ew"),
            P("ns", "ew"),
            P("ew"),
            P("ns", "ew", None, None),
            P("ns", "ew", None),
            P("ns", "ew", None, None, None),
        ),
        out_specs=(P(None, "ns", "ew"), P("ns", "ew", None, None)),
        check_vma=False,
    )
```

```python
import jax
import jax.numpy as jnp
from jax import lax
from jax.experimental import pallas as pl
from jax.experimental.pallas import tpu as pltpu
from jax.sharding import PartitionSpec as P

COEFS = (0.5, -0.3, 0.2, 0.4, -0.25, 0.35)
VMEM = pl.BlockSpec(memory_space=pltpu.VMEM)
SMEM = pl.BlockSpec(memory_space=pltpu.SMEM)
HBM = pl.BlockSpec(memory_space=pltpu.HBM)
PARAMS = pltpu.CompilerParams(vmem_limit_bytes=16 * 1024 * 1024)
F32 = jnp.float32
BF16 = jnp.bfloat16
KINDS = 6
BLOCK, TILE = 16, 8
FORCE_SLOT, WET_SLOT = 4, 5


def tendency(t, east, west, north, south, u, v, d):
    return d * (east + west + north + south - 4.0 * t) - 0.5 * (u * (east - west) + v * (north - south))


def stencil(t, *others):
    return t + tendency(t, *others)


class Place:
    def __init__(self):
        self.count, self.block_rows = lax.axis_size("ew"), lax.axis_size("ns")
        self.devices = self.count * self.block_rows
        self.e, self.n = lax.axis_index("ew"), lax.axis_index("ns")
        self.top = self.block_rows - 1
        self.is_top = self.n == self.top
        self.has_south = self.n > 0
        self.even = lax.rem(self.n, 2) == 0
        self.east = lax.rem(self.e + 1, self.count)
        self.west = lax.rem(self.e + self.count - 1, self.count)
        self.above = jnp.minimum(self.n + 1, self.top)
        self.below = jnp.maximum(self.n - 1, 0)
        self.pair = jnp.where(self.even, self.n + 1, self.n - 1)
        self.other = jnp.where(self.even, self.below, self.above)
        self.half = self.count // 2

    def slot(self, e, n):
        return e * self.block_rows + n


def fill(size, rows):
    parts, at = [], 0
    for index in sorted(rows):
        if index > at:
            parts.append(jnp.zeros((index - at, size), F32))
        parts.append(rows[index])
        at = index + 1
    if at < size:
        parts.append(jnp.zeros((size - at, size), F32))
    return jnp.concatenate(parts, axis=0)


def turn(field):
    return field.reshape(field.shape[0] * field.shape[1], field.shape[2]).T


def shifted(field, axis, back):
    size = field.shape[axis]
    return pltpu.roll(field, size - 1 if back else 1, axis)


def first_kernel(
    partner_ref, theta_hbm, vel_hbm, diff_hbm, atm_hbm,
    out_ref, theta_ref, coef_ref,
    atm_ref, bulk_ref, sems,
):
    here = Place()
    pairs = [
        (theta_hbm, theta_ref), (vel_hbm, coef_ref.at[pl.ds(0, 2)]), (diff_hbm, coef_ref.at[2]),
        (atm_hbm, atm_ref),
    ]
    copies = [pltpu.make_async_copy(a, b, sems.at[i]) for i, (a, b) in enumerate(pairs)]
    for copy in copies:
        copy.start()
    for copy in copies:
        copy.wait()
    levels, rows, cols = theta_ref.shape
    tiles = levels // TILE
    each = KINDS * tiles
    for side, step in enumerate((-1, 1)):
        edge = rows - 1 if step < 0 else 0
        outer, t, inner = [theta_ref[:, edge + k * step, :] for k in range(3)]
        north, south = (outer, inner) if step < 0 else (inner, outer)
        coef = [coef_ref[k, :, edge + step, :] for k in range(3)]
        tend = tendency(t, shifted(t, 1, True), shifted(t, 1, False), north, south, *coef)
        for kind, field in enumerate((outer, t, tend, *[coef_ref[k, :, edge, :] for k in range(3)])):
            bulk_ref[pl.ds(side * each + kind * tiles, tiles)] = field.reshape(tiles, TILE, cols)
    turned = turn(theta_ref[...])
    lane = lax.broadcasted_iota(jnp.int32, (1, cols), 1)
    second = jnp.where(lane == 1, partner_ref[0].astype(F32), turned[1:2])
    columns = [turned[0:1], second, turned[cols - 2 : cols - 1], turned[cols - 1 : cols]]
    atm = atm_ref[...].astype(F32)
    begin = jnp.concatenate(columns + [atm[: TILE - 4]], axis=0)
    own = jnp.concatenate([atm[TILE - 4 :], jnp.zeros((2 * TILE - 4 - atm.shape[0], cols), F32)], axis=0)
    for target in range(here.devices):
        e, n = target // here.block_rows, target % here.block_rows
        order = (e % here.half) * (here.block_rows - 1) + n - (here.n < n).astype(jnp.int32)
        upward = here.even if e < here.half else jnp.logical_not(here.even)
        tile = bulk_ref[jnp.where(upward, 0, each) + jnp.minimum(order, each - 1)]
        out_ref[target] = jnp.concatenate([begin, jnp.where(here.n == n, own, tile)], axis=0).astype(BF16)

def load_kernel(src_hbm, weights_hbm, src_ref, weights_ref, sems):
    copies = [
        pltpu.make_async_copy(weights_hbm, weights_ref, sems.at[0]), pltpu.make_async_copy(src_hbm, src_ref, sems.at[1])
    ]
    for copy in copies:
        copy.start()
    for copy in copies:
        copy.wait()


def side_kernel(
    mask_ref, theta_ref, coef_ref, points_ref, columns_ref, rims_ref, start_ref
):
    levels, rows, cols = theta_ref.shape
    last = rows - 1
    wet = mask_ref[0, 0].astype(F32)
    u, v, d = wet * coef_ref[0], wet * coef_ref[1], wet * coef_ref[2]
    turned = [turn(u), turn(v), turn(d)]
    for side, at in enumerate((0, cols - 1)):
        for k in range(3):
            columns_ref[side, k : k + 1, :] = turned[k][at : at + 1]
    center, east, west, north, south = 1.0 - 4.0 * d, d - 0.5 * u, d + 0.5 * u, d - 0.5 * v, d + 0.5 * v
    for k, field in enumerate((center, east, west, north, south)):
        points_ref[k] = field
    t = theta_ref[...]
    lane = lax.broadcasted_iota(jnp.int32, t.shape, 2)
    line = lax.broadcasted_iota(jnp.int32, t.shape, 1)
    rims_ref[0] = jnp.where(lane == cols - 1, east, jnp.where(lane == 0, west, 0.0))
    rims_ref[1] = jnp.where(line == last, north, jnp.where(line == 0, south, 0.0))
    inner = center * t
    inner = inner + east * jnp.where(lane == cols - 1, 0.0, shifted(t, 2, True))
    inner = inner + west * jnp.where(lane == 0, 0.0, shifted(t, 2, False))
    inner = inner + north * jnp.where(line == last, 0.0, shifted(t, 1, True))
    inner = inner + south * jnp.where(line == 0, 0.0, shifted(t, 1, False))
    start_ref[...] = inner


def middle_kernel(
    mask_ref, partner_ref, src_ref, columns_ref, rims_ref, start_ref, weights_ref, recv_ref,
    total_ref, force_ref, next_ref, ends_ref, out_ref,
):
    here = Place()
    levels, rows, cols = start_ref.shape
    fields = total_ref.shape[0]
    last = rows - 1
    wet = mask_ref[0, 0].astype(F32)

    pairs, cells, points = weights_ref.shape
    chosen = [recv_ref[here.slot(src_ref[0, pair], here.n)][4 : 4 + fields] for pair in range(pairs)]
    weights = weights_ref[...].reshape(pairs * cells, points)
    total = jnp.dot(jnp.concatenate(chosen, axis=1), weights, preferred_element_type=F32)
    total_ref[...] = total
    force = jnp.zeros((1, points), F32)
    for k in range(fields):
        force = force + COEFS[k] * total[k : k + 1]
    force = jnp.concatenate([force[:, r * cols : (r + 1) * cols] for r in range(rows)], axis=0)
    force = wet * (0.1 * force)
    force_ref[...] = force

    shape = start_ref.shape
    line = lax.broadcasted_iota(jnp.int32, shape, 1)
    level = lax.broadcasted_iota(jnp.int32, shape, 0)

    def got(e, n):
        return recv_ref[here.slot(e, n)].astype(F32)

    sides = fill(cols, {0: got(here.west, here.n)[3:4], cols - 1: got(here.east, here.n)[0:1]}).T.reshape(shape)
    fold, over, under = got(partner_ref[0], here.n), got(here.e, here.above), got(here.e, here.below)
    spots = (0, 1, cols - 2, cols - 1)
    beyond = {spot: jnp.where(here.is_top, fold[3 - i : 4 - i], over[i : i + 1]) for i, spot in enumerate(spots)}
    beyond.update({spot + (2 if i < 2 else -2): under[i : i + 1] for i, spot in enumerate(spots)})
    beyond = fill(cols, beyond).T.reshape(shape)
    flat = lax.broadcasted_iota(jnp.int32, (levels, cols), 1)
    above = jnp.where(here.is_top, beyond[:, last, :], beyond[:, 0, :])
    above = jnp.where((flat < 2) | (flat >= cols - 2), above, 0.0)
    below = beyond[:, last, :]
    below = jnp.where(
        flat < 2, pltpu.roll(below, cols - 2, 1), jnp.where(flat >= cols - 2, pltpu.roll(below, 2, 1), 0.0)
    )
    below = jnp.where(here.has_south, below, 0.0)
    across = jnp.where(line == last, above[:, None, :], below[:, None, :])
    t = start_ref[...] + rims_ref[0] * sides + rims_ref[1] * across
    next_ref[...] = t + jnp.where(level == 0, force[None], 0.0)

    held = [got(m, here.top) for m in range(here.count)]
    size = -(-here.count * TILE // cols) * cols
    tiles = [block[TILE:] for block in held] + [jnp.zeros((size - here.count * TILE, cols), F32)] * (size > here.count * TILE)
    tiles = jnp.concatenate(tiles, axis=0).astype(BF16)
    partners = jnp.concatenate([jnp.broadcast_to(block[1:2, 1:2], (TILE, 1)) for block in held], axis=0)
    wanted = TILE * partners + lax.rem(lax.broadcasted_iota(jnp.int32, partners.shape, 0), TILE).astype(F32)
    pick = lax.broadcasted_iota(jnp.int32, (here.count * TILE, size), 1).astype(F32) == wanted
    folded = jnp.dot(pick.astype(F32).astype(BF16), tiles, preferred_element_type=F32)

    turned = turn(t) + jnp.concatenate([force, jnp.zeros((cols - rows, cols), F32)], axis=0).T
    ends = jnp.concatenate([turned[0:1], turned[cols - 1 : cols], jnp.zeros((TILE - 2, cols), F32)], axis=0)
    lane = lax.broadcasted_iota(jnp.int32, (TILE, cols), 1)
    forces = jnp.concatenate([force, jnp.zeros((cols - rows, cols), F32)], axis=0).T
    forces = jnp.concatenate([forces[0:1], forces[cols - 1 : cols], jnp.zeros((TILE - 2, cols), F32)], axis=0)
    ends_ref[...] = ends
    marks = jnp.take_along_axis(forces, lane // 8, axis=1)
    slot = lax.rem(lane, 8)
    marks = jnp.where(slot == FORCE_SLOT, marks, jnp.where(slot == WET_SLOT, wet, 0.0))
    slot = slot[0:1]

    def corners(shifts, mark):
        row = mark
        for index, shift in enumerate(shifts):
            moved = pltpu.roll(ends, shift % cols, 1) if shift else ends
            row = jnp.where(slot == index, moved[index // 2 : index // 2 + 1], row)
        return row

    up, down = (-last, 2 - last, 2 - last, 4 - last), (0, 0, 2, 2)
    low_mark, high_mark = marks[0:1], marks[1:2]
    low_coef, high_coef = columns_ref[0], columns_ref[1]
    high_force, low_force = [force[last : last + 1], force[last - 1 : last]], [force[0:1], force[1:2]]
    low, high = [turned[0:1], turned[1:2]], [turned[cols - 1 : cols], turned[cols - 2 : cols - 1]]
    base = jnp.concatenate([corners(up, low_mark)] + high_force + low + [low_coef], axis=0)
    to_east = jnp.concatenate([corners(up, high_mark)] + high_force + high + [high_coef], axis=0)
    to_below = jnp.concatenate([corners(down, low_mark)] + low_force + low + [low_coef], axis=0)
    first_half = here.e < here.half
    for target in range(here.devices):
        e, n = target // here.block_rows, target % here.block_rows
        begin = jnp.where(n == here.n - 1, to_below, jnp.where(e == here.east, to_east, base))
        pair = n + 1 if n % 2 == 0 else n - 1
        other = max(n - 1, 0) if n % 2 == 0 else min(n + 1, here.top)
        tile = got(e, jnp.where(first_half, pair, other))[TILE:]
        if n == here.top:
            tile = jnp.where(first_half, tile, folded[e * TILE : (e + 1) * TILE])
        out_ref[target] = jnp.concatenate([begin, tile], axis=0).astype(BF16)


def last_kernel(
    partner_ref, theta_ref, points_ref, total_ref, next_ref, ends_ref, force_ref, first_ref, second_ref,
    result_hbm, flux_hbm, result_ref, flux_ref, rim_ref, sems,
):
    here = Place()
    levels, rows, cols = theta_ref.shape
    last = rows - 1
    for k in range(flux_ref.shape[0]):
        for r in range(rows):
            flux_ref[k, r : r + 1, :] = total_ref[k : k + 1, r * cols : (r + 1) * cols]
    copies = [
        pltpu.make_async_copy(flux_ref, flux_hbm, sems.at[0]), pltpu.make_async_copy(result_ref, result_hbm, sems.at[1])
    ]
    copies[0].start()
    partner = partner_ref[0]
    is_top, has_south = here.is_top, here.has_south

    def got(e, n):
        return second_ref[here.slot(e, n)].astype(F32)

    west, east = got(here.west, here.n), got(here.east, here.n)
    over, under = got(here.e, here.above), got(here.e, here.below)
    fold = got(partner, here.n)
    fold_east = got(lax.rem(partner + 1, here.count), here.n)[0:1]
    fold_west = got(lax.rem(partner + here.count - 1, here.count), here.n)[0:1]
    over_west, over_east = got(here.west, here.above)[0:1], got(here.east, here.above)[0:1]
    under_west, under_east = got(here.west, here.below)[0:1], got(here.east, here.below)[0:1]
    first_west = first_ref[here.slot(here.west, here.n)].astype(F32)
    first_east = first_ref[here.slot(here.east, here.n)].astype(F32)

    def mark(block):
        return block[0:1, WET_SLOT : WET_SLOT + 1]

    tiles = KINDS * levels // TILE

    def gather(begin, source):
        found = []
        for k in range(tiles):
            e, order = k // (here.block_rows - 1), k % (here.block_rows - 1)
            found.append(got(begin + e, order + (source <= order).astype(jnp.int32))[TILE:])
        return jnp.concatenate(found, axis=0)

    near, far = gather(0, here.pair), gather(here.half, here.other)
    south = jnp.where(has_south, jnp.where(here.even, far, near), 0.0)
    north = jnp.where(here.even, near, far)
    mirror = cols - 1 - lax.broadcasted_iota(jnp.int32, north.shape, 1)
    north = jnp.where(is_top, jnp.take_along_axis(north, mirror, axis=1), north)

    def kinds(bulk, wet, sign):
        t, inner, tend, u, v, d = [bulk[kind * levels : (kind + 1) * levels] for kind in range(KINDS)]
        return t, inner, inner + wet * tend, (sign * wet) * u, (sign * wet) * v, wet * d

    north = kinds(north, jnp.where(is_top, mark(fold), mark(over)), jnp.where(is_top, -1.0, 1.0))
    south = kinds(south, mark(under), 1.0)

    top_west, top_east = jnp.zeros((1, cols), F32), jnp.zeros((1, cols), F32)
    for s in range(here.count):
        row = got(s, here.n)[0:1]
        top_west = jnp.where(first_west[1:2, 1:2] == float(s), row, top_west)
        top_east = jnp.where(first_east[1:2, 1:2] == float(s), row, top_east)
    moved = [fold[0:1], over[0:1], under[0:1], fold_west, over_west, under_west, top_east]
    moved = jnp.concatenate(moved + [jnp.zeros((1, cols), F32)], axis=0)
    moved = pltpu.roll(moved, cols - 2, 1)
    def pair(low, high):
        return jnp.concatenate([low, high, jnp.zeros((TILE - 2, cols), F32)], axis=0)

    along = lax.broadcasted_iota(jnp.int32, (TILE, cols), 1)
    place = lax.rem(along, rows)
    side = pair(west[3:4], east[3:4])
    corner = pair(jnp.where(is_top, top_west, moved[4:5]), jnp.where(is_top, moved[6:7], over_east))
    side_north = jnp.where(place == last, pltpu.roll(corner, last, 1), shifted(side, 1, True))
    corner = jnp.where(has_south, pair(moved[5:6], under_east), 0.0)
    side_south = jnp.where(place == 0, corner, shifted(side, 1, False))
    side_force = jnp.take_along_axis(pair(west[0:1], east[0:1]), jnp.where(along < rows, 8 * along, 0) + FORCE_SLOT, axis=1)
    side_next = stencil(
        side, pair(ends_ref[0:1], east[4:5]), pair(west[4:5], ends_ref[1:2]), side_north, side_south,
        *[pair(west[k : k + 1], east[k : k + 1]) for k in (5, 6, 7)],
    ) + jnp.where(along < rows, side_force, 0.0)

    listed = [
        (west[3:4], east[3:4]),
        (side_next[0:1], side_next[1:2]),
        (jnp.where(is_top, moved[0:1], over[0:1]), jnp.where(is_top, fold[0:1], moved[1:2])),
        (under[0:1], moved[2:3]),
        (jnp.where(is_top, fold_east, moved[4:5]), jnp.where(is_top, moved[3:4], over_east)),
        (moved[5:6], under_east),
    ]
    lanes = {}
    for q, (low, high) in enumerate(listed):
        lanes[2 * q], lanes[(2 * q - 1) % cols] = low, high
    rim = fill(cols, lanes).T.reshape(theta_ref.shape)
    rim_ref[...] = rim

    def listing(q, field):
        return pltpu.roll(field, cols - 2 * q, field.ndim - 1) if q else field

    edges, inners = rim_ref[:, 0, :], rim_ref[:, 1, :]
    lane = lax.broadcasted_iota(jnp.int32, (levels, cols), 1)
    level = lax.broadcasted_iota(jnp.int32, (levels, cols), 0)
    ends = (lane == 0) | (lane == cols - 1)

    def forced(row, force):
        return row + jnp.where(level == 0, force, 0.0)

    flip = cols - 1 - lax.broadcasted_iota(jnp.int32, (8, cols), 1)
    flipped = jnp.take_along_axis(fold[:TILE], flip, axis=1)
    north_force = [jnp.where(is_top, flipped[k : k + 1], over[k : k + 1]) for k in (1, 2)]
    south_force = [under[1:2], under[2:3]]

    def beyond(rows_of, inside, outward, force, q):
        edge_row = stencil(
            rows_of[0], shifted(rows_of[0], 1, True), shifted(rows_of[0], 1, False),
            rows_of[1] if outward else inside, inside if outward else rows_of[1], *rows_of[3:],
        )
        edge_row = jnp.where(ends, listing(q, edges), forced(edge_row, force[0]))
        return edge_row, jnp.where(ends, listing(q, inners), forced(rows_of[2], force[1]))

    north_one, north_two = beyond(north, theta_ref[:, last, :], True, north_force, 2)
    south_one, south_two = beyond(south, theta_ref[:, 0, :], False, south_force, 3)
    south_one, south_two = jnp.where(has_south, south_one, 0.0), jnp.where(has_south, south_two, 0.0)
    shape = theta_ref.shape
    wide = lax.broadcasted_iota(jnp.int32, shape, 2)
    line = lax.broadcasted_iota(jnp.int32, shape, 1)
    force = jnp.where(lax.broadcasted_iota(jnp.int32, shape, 0) == 0, force_ref[...][None], 0.0)
    inside = (lane >= 2) & (lane < cols - 2)
    top_row = next_ref[:, last, :] + jnp.where(inside, points_ref[3, :, last, :] * north[0], 0.0)
    bottom_row = next_ref[:, 0, :] + jnp.where(inside, points_ref[4, :, 0, :] * south[0], 0.0)
    t = jnp.where(line == last, top_row[:, None, :], jnp.where(line == 0, bottom_row[:, None, :], next_ref[...]))

    def outer(row, further, inside, outward, rows_of, force_row, diagonal):
        result = stencil(
            row, jnp.where(lane == cols - 1, diagonal, shifted(row, 1, True)),
            jnp.where(lane == 0, diagonal, shifted(row, 1, False)),
            further if outward else inside, inside if outward else further, *rows_of[3:],
        )
        return forced(result, force_row)

    north_next = outer(north_one, north_two, top_row, True, north, north_force[0], listing(4, edges))
    south_next = outer(south_one, south_two, bottom_row, False, south, south_force[0], listing(5, edges))
    south_next = jnp.where(has_south, south_next, 0.0)

    def advance(t, sides, above, below):
        east = jnp.where(wide == cols - 1, sides, shifted(t, 2, True))
        west = jnp.where(wide == 0, sides, shifted(t, 2, False))
        north = jnp.where(line == last, above[:, None, :], shifted(t, 1, True))
        south = jnp.where(line == 0, below[:, None, :], shifted(t, 1, False))
        result = force
        for k, field in enumerate((t, east, west, north, south)):
            result = result + points_ref[k] * field
        return result

    t = advance(t, rim, north_one, south_one)
    result_ref[...] = advance(t, listing(1, rim), north_next, south_next)
    copies[1].start()
    for copy in copies:
        copy.wait()


def exchange(blocks):
    return lax.all_to_all(blocks, ("ew", "ns"), split_axis=0, concat_axis=0, tiled=True)


def local(theta, velocity, diffusivity, land_mask, fold_partner, atm_flux, remap_src, remap_weights):
    levels, rows, cols = theta.shape
    fields = atm_flux.shape[2]
    shape = jax.ShapeDtypeStruct
    devices = lax.axis_size("ew") * lax.axis_size("ns")
    blocks = (devices, BLOCK, cols)
    room = 60 * 2**20 - 2 * max(0, 2 * devices * BLOCK * cols - 2**20)
    weights = remap_weights[0, 0]
    out, field, coef = pl.pallas_call(
        first_kernel,
        out_shape=(
            pltpu.VMEM(blocks, BF16), pltpu.VMEM(theta.shape, F32), pltpu.VMEM((3,) + theta.shape, F32),
        ),
        in_specs=[SMEM] + [HBM] * 4,
        out_specs=(VMEM,) * 3,
        scratch_shapes=[
            pltpu.VMEM((fields, cols), BF16),
            pltpu.VMEM((2 * KINDS * levels // TILE, TILE, cols), F32),
            pltpu.SemaphoreType.DMA((4,)),
        ],
        compiler_params=pltpu.CompilerParams(vmem_limit_bytes=room),
        name="first",
    )(fold_partner, theta, velocity, diffusivity, atm_flux[0, 0])
    first = exchange(out)
    sources, weights = pl.pallas_call(
        load_kernel,
        out_shape=(pltpu.SMEM(remap_src.shape[1:], remap_src.dtype), pltpu.VMEM(weights.shape, BF16)),
        in_specs=[HBM] * 2,
        out_specs=(SMEM, VMEM),
        scratch_shapes=[pltpu.SemaphoreType.DMA((2,))],
        compiler_params=pltpu.CompilerParams(vmem_limit_bytes=room),
        cost_estimate=pl.CostEstimate(flops=2**20, bytes_accessed=2**22, transcendentals=0),
        name="load",
    )(remap_src[0], weights)
    points, columns, rims, start = pl.pallas_call(
        side_kernel,
        out_shape=(
            pltpu.VMEM((5,) + theta.shape, F32), pltpu.VMEM((2, 3, cols), F32), pltpu.VMEM((2,) + theta.shape, F32),
            pltpu.VMEM(theta.shape, F32),
        ),
        in_specs=[SMEM, VMEM, VMEM],
        out_specs=(VMEM,) * 4,
        compiler_params=PARAMS,
        cost_estimate=pl.CostEstimate(flops=2**20, bytes_accessed=2**20, transcendentals=0),
        name="side",
    )(land_mask, field, coef)
    total, force, after, ends, out = pl.pallas_call(
        middle_kernel,
        out_shape=(
            pltpu.VMEM((fields, rows * cols), F32), pltpu.VMEM((rows, cols), F32), pltpu.VMEM(theta.shape, F32),
            pltpu.VMEM((TILE, cols), F32), pltpu.VMEM(blocks, BF16),
        ),
        in_specs=[SMEM] * 3 + [VMEM] * 5,
        out_specs=(VMEM,) * 5,
        compiler_params=PARAMS,
        name="middle",
    )(land_mask, fold_partner, sources, columns, rims, start, weights, first)
    second = exchange(out)
    field, flux = pl.pallas_call(
        last_kernel,
        out_shape=(shape(theta.shape, F32), shape((fields, rows, cols), F32)),
        in_specs=[SMEM] + [VMEM] * 8,
        out_specs=(HBM, HBM),
        scratch_shapes=[
            pltpu.VMEM(theta.shape, F32), pltpu.VMEM((fields, rows, cols), F32), pltpu.VMEM(theta.shape, F32),
            pltpu.SemaphoreType.DMA((2,)),
        ],
        compiler_params=PARAMS,
        name="last",
    )(fold_partner, field, points, total, after, ends, force, first, second)
    return field, flux.reshape(1, 1, fields, rows * cols)


def solution(mesh):
    return jax.shard_map(
        local,
        mesh=mesh,
        in_specs=(
            P(None, "ns", "ew"),
            P(None, None, "ns", "ew"),
            P(None, "ns", "ew"),
            P("ns", "ew"),
            P("ew"),
            P("ns", "ew", None, None),
            P("ns", "ew", None),
            P("ns", "ew", None, None, None),
        ),
        out_specs=(P(None, "ns", "ew"), P("ns", "ew", None, None)),
        check_vma=False,
    )
```

```python
import functools

import jax
import jax.numpy as jnp
from jax import lax
from jax.experimental import pallas as pl
from jax.experimental.pallas import tpu as pltpu
from jax.sharding import PartitionSpec as P

COEFS = (0.5, -0.3, 0.2, 0.4, -0.25, 0.35)
VMEM = pl.BlockSpec(memory_space=pltpu.VMEM)
SMEM = pl.BlockSpec(memory_space=pltpu.SMEM)
HBM = pl.BlockSpec(memory_space=pltpu.HBM)
PARAMS = pltpu.CompilerParams(vmem_limit_bytes=16 * 1024 * 1024)
F32 = jnp.float32
BF16 = jnp.bfloat16
KINDS = 6
BLOCK, TILE = 16, 8
FORCE_SLOT, WET_SLOT = 4, 5


def tendency(t, east, west, north, south, u, v, d):
    return d * (east + west + north + south - 4.0 * t) - 0.5 * (u * (east - west) + v * (north - south))


def stencil(t, *others):
    return t + tendency(t, *others)


class Place:
    def __init__(self):
        self.count, self.block_rows = lax.axis_size("ew"), lax.axis_size("ns")
        self.devices = self.count * self.block_rows
        self.e, self.n = lax.axis_index("ew"), lax.axis_index("ns")
        self.top = self.block_rows - 1
        self.is_top = self.n == self.top
        self.has_south = self.n > 0
        self.even = lax.rem(self.n, 2) == 0
        self.east = lax.rem(self.e + 1, self.count)
        self.west = lax.rem(self.e + self.count - 1, self.count)
        self.above = jnp.minimum(self.n + 1, self.top)
        self.below = jnp.maximum(self.n - 1, 0)
        self.pair = jnp.where(self.even, self.n + 1, self.n - 1)
        self.other = jnp.where(self.even, self.below, self.above)
        self.half = self.count // 2

    def slot(self, e, n):
        return n * self.count + e


def fill(size, rows):
    parts, at = [], 0
    for index in sorted(rows):
        if index > at:
            parts.append(jnp.zeros((index - at, size), F32))
        parts.append(rows[index])
        at = index + 1
    if at < size:
        parts.append(jnp.zeros((size - at, size), F32))
    return jnp.concatenate(parts, axis=0)


def turn(field):
    return field.reshape(field.shape[0] * field.shape[1], field.shape[2]).T


def shifted(field, axis, back):
    size = field.shape[axis]
    return pltpu.roll(field, size - 1 if back else 1, axis)


def bring_kernel(count, *refs):
    copies = [pltpu.make_async_copy(refs[i], refs[count + i], refs[-1].at[i]) for i in range(count)]
    for copy in copies:
        copy.start()
    for copy in copies:
        copy.wait()


def bring(arrays, memories, room, name):
    return pl.pallas_call(
        functools.partial(bring_kernel, len(arrays)),
        out_shape=tuple(memory(x.shape, x.dtype) for x, memory in zip(arrays, memories)),
        in_specs=[HBM] * len(arrays),
        out_specs=tuple(VMEM if memory is pltpu.VMEM else SMEM for memory in memories),
        scratch_shapes=[pltpu.SemaphoreType.DMA((len(arrays),))],
        compiler_params=pltpu.CompilerParams(vmem_limit_bytes=room),
        cost_estimate=pl.CostEstimate(flops=2**20, bytes_accessed=2**22, transcendentals=0),
        name=name,
    )(*arrays)


def first_kernel(partner_ref, theta_ref, vel_ref, diff_ref, atm_ref, out_ref, bulk_ref):
    here = Place()
    levels, rows, cols = theta_ref.shape
    each = KINDS * levels // TILE
    firsts = [
        [jnp.where(upward, 0, each) - (here.n < n).astype(jnp.int32) for n in range(here.block_rows)]
        for upward in (here.even, jnp.logical_not(here.even))
    ]
    coef_refs = [vel_ref.at[0], vel_ref.at[1], diff_ref]
    tiles = levels // TILE
    for side, step in enumerate((-1, 1)):
        edge = rows - 1 if step < 0 else 0
        outer, t, inner = [theta_ref[:, edge + k * step, :] for k in range(3)]
        north, south = (outer, inner) if step < 0 else (inner, outer)
        coef = [ref[:, edge + step, :] for ref in coef_refs]
        tend = tendency(t, shifted(t, 1, True), shifted(t, 1, False), north, south, *coef)
        for kind, field in enumerate((outer, t, tend, *[ref[:, edge, :] for ref in coef_refs])):
            bulk_ref[pl.ds(side * each + kind * tiles, tiles)] = field.reshape(tiles, TILE, cols)
    bulk_ref[2 * each] = jnp.zeros((TILE, cols), F32)
    turned = turn(theta_ref[...])
    lane = lax.broadcasted_iota(jnp.int32, (1, cols), 1)
    second = jnp.where(lane == 1, partner_ref[0].astype(F32), turned[1:2])
    columns = [turned[0:1], second, turned[cols - 2 : cols - 1], turned[cols - 1 : cols]]
    atm = atm_ref[...].astype(F32)
    begin = jnp.concatenate(columns + [atm[: TILE - 4]], axis=0)
    own = jnp.concatenate([atm[TILE - 4 :], jnp.zeros((2 * TILE - 4 - atm.shape[0], cols), F32)], axis=0)
    for target in range(here.devices):
        e, n = target % here.count, target // here.count
        order = (e % here.half) * (here.block_rows - 1) + n
        start = firsts[e // here.half][n]
        tile = bulk_ref[start + min(order, each)]
        out_ref[target] = jnp.concatenate([begin, jnp.where(here.n == n, own, tile)], axis=0).astype(BF16)


def side_kernel(
    mask_ref, theta_ref, vel_ref, diff_ref, points_ref, columns_ref, rims_ref, start_ref
):
    levels, rows, cols = theta_ref.shape
    last = rows - 1
    wet = mask_ref[0, 0].astype(F32)
    u, v, d = wet * vel_ref[0], wet * vel_ref[1], wet * diff_ref[...]
    turned = [turn(u), turn(v), turn(d)]
    for side, at in enumerate((0, cols - 1)):
        for k in range(3):
            columns_ref[side, k : k + 1, :] = turned[k][at : at + 1]
    center, east, west, north, south = 1.0 - 4.0 * d, d - 0.5 * u, d + 0.5 * u, d - 0.5 * v, d + 0.5 * v
    for k, field in enumerate((center, east, west, north, south)):
        points_ref[k] = field
    t = theta_ref[...]
    lane = lax.broadcasted_iota(jnp.int32, t.shape, 2)
    line = lax.broadcasted_iota(jnp.int32, t.shape, 1)
    rims_ref[0] = jnp.where(lane == cols - 1, east, jnp.where(lane == 0, west, 0.0))
    rims_ref[1] = jnp.where(line == last, north, jnp.where(line == 0, south, 0.0))
    inner = center * t
    inner = inner + east * jnp.where(lane == cols - 1, 0.0, shifted(t, 2, True))
    inner = inner + west * jnp.where(lane == 0, 0.0, shifted(t, 2, False))
    inner = inner + north * jnp.where(line == last, 0.0, shifted(t, 1, True))
    inner = inner + south * jnp.where(line == 0, 0.0, shifted(t, 1, False))
    start_ref[...] = inner


def middle_kernel(
    mask_ref, partner_ref, src_ref, columns_ref, rims_ref, start_ref, weights_ref, recv_ref,
    total_ref, force_ref, next_ref, ends_ref, out_ref,
):
    here = Place()
    levels, rows, cols = start_ref.shape
    fields = total_ref.shape[0]
    last = rows - 1
    wet = mask_ref[0, 0].astype(F32)

    pairs, cells, points = weights_ref.shape
    chosen = [recv_ref[here.slot(src_ref[0, pair], here.n)][4 : 4 + fields] for pair in range(pairs)]
    weights = weights_ref[...].reshape(pairs * cells, points)
    total = jnp.dot(jnp.concatenate(chosen, axis=1), weights, preferred_element_type=F32)
    total_ref[...] = total
    force = jnp.zeros((1, points), F32)
    for k in range(fields):
        force = force + COEFS[k] * total[k : k + 1]
    force = jnp.concatenate([force[:, r * cols : (r + 1) * cols] for r in range(rows)], axis=0)
    force = wet * (0.1 * force)
    force_ref[...] = force

    shape = start_ref.shape
    line = lax.broadcasted_iota(jnp.int32, shape, 1)
    level = lax.broadcasted_iota(jnp.int32, shape, 0)

    def got(e, n):
        return recv_ref[here.slot(e, n)].astype(F32)

    sides = fill(cols, {0: got(here.west, here.n)[3:4], cols - 1: got(here.east, here.n)[0:1]}).T.reshape(shape)
    fold, over, under = got(partner_ref[0], here.n), got(here.e, here.above), got(here.e, here.below)
    spots = (0, 1, cols - 2, cols - 1)
    beyond = {spot: jnp.where(here.is_top, fold[3 - i : 4 - i], over[i : i + 1]) for i, spot in enumerate(spots)}
    beyond.update({spot + (2 if i < 2 else -2): under[i : i + 1] for i, spot in enumerate(spots)})
    beyond = fill(cols, beyond).T.reshape(shape)
    flat = lax.broadcasted_iota(jnp.int32, (levels, cols), 1)
    above = jnp.where(here.is_top, beyond[:, last, :], beyond[:, 0, :])
    above = jnp.where((flat < 2) | (flat >= cols - 2), above, 0.0)
    below = beyond[:, last, :]
    below = jnp.where(
        flat < 2, pltpu.roll(below, cols - 2, 1), jnp.where(flat >= cols - 2, pltpu.roll(below, 2, 1), 0.0)
    )
    below = jnp.where(here.has_south, below, 0.0)
    across = jnp.where(line == last, above[:, None, :], below[:, None, :])
    t = start_ref[...] + rims_ref[0] * sides + rims_ref[1] * across
    next_ref[...] = t + jnp.where(level == 0, force[None], 0.0)

    held = [got(m, here.top) for m in range(here.count)]
    size = -(-here.count * TILE // cols) * cols
    tiles = [block[TILE:] for block in held] + [jnp.zeros((size - here.count * TILE, cols), F32)] * (size > here.count * TILE)
    tiles = jnp.concatenate(tiles, axis=0).astype(BF16)
    partners = jnp.concatenate([jnp.broadcast_to(block[1:2, 1:2], (TILE, 1)) for block in held], axis=0)
    wanted = TILE * partners + lax.rem(lax.broadcasted_iota(jnp.int32, partners.shape, 0), TILE).astype(F32)
    pick = lax.broadcasted_iota(jnp.int32, (here.count * TILE, size), 1).astype(F32) == wanted
    folded = jnp.dot(pick.astype(F32).astype(BF16), tiles, preferred_element_type=F32)

    turned = turn(t) + jnp.concatenate([force, jnp.zeros((cols - rows, cols), F32)], axis=0).T
    ends = jnp.concatenate([turned[0:1], turned[cols - 1 : cols], jnp.zeros((TILE - 2, cols), F32)], axis=0)
    lane = lax.broadcasted_iota(jnp.int32, (TILE, cols), 1)
    forces = jnp.concatenate([force, jnp.zeros((cols - rows, cols), F32)], axis=0).T
    forces = jnp.concatenate([forces[0:1], forces[cols - 1 : cols], jnp.zeros((TILE - 2, cols), F32)], axis=0)
    ends_ref[...] = ends
    marks = jnp.take_along_axis(forces, lane // 8, axis=1)
    slot = lax.rem(lane, 8)
    marks = jnp.where(slot == FORCE_SLOT, marks, jnp.where(slot == WET_SLOT, wet, 0.0))
    slot = slot[0:1]

    def corners(shifts, mark):
        row = mark
        for index, shift in enumerate(shifts):
            moved = pltpu.roll(ends, shift % cols, 1) if shift else ends
            row = jnp.where(slot == index, moved[index // 2 : index // 2 + 1], row)
        return row

    up, down = (-last, 2 - last, 2 - last, 4 - last), (0, 0, 2, 2)
    low_mark, high_mark = marks[0:1], marks[1:2]
    low_coef, high_coef = columns_ref[0], columns_ref[1]
    high_force, low_force = [force[last : last + 1], force[last - 1 : last]], [force[0:1], force[1:2]]
    low, high = [turned[0:1], turned[1:2]], [turned[cols - 1 : cols], turned[cols - 2 : cols - 1]]
    base = jnp.concatenate([corners(up, low_mark)] + high_force + low + [low_coef], axis=0)
    to_east = jnp.concatenate([corners(up, high_mark)] + high_force + high + [high_coef], axis=0)
    to_below = jnp.concatenate([corners(down, low_mark)] + low_force + low + [low_coef], axis=0)
    first_half = here.e < here.half
    for target in range(here.devices):
        e, n = target % here.count, target // here.count
        begin = jnp.where(n == here.n - 1, to_below, jnp.where(e == here.east, to_east, base))
        pair = n + 1 if n % 2 == 0 else n - 1
        other = max(n - 1, 0) if n % 2 == 0 else min(n + 1, here.top)
        tile = got(e, jnp.where(first_half, pair, other))[TILE:]
        if n == here.top:
            tile = jnp.where(first_half, tile, folded[e * TILE : (e + 1) * TILE])
        out_ref[target] = jnp.concatenate([begin, tile], axis=0).astype(BF16)


def last_kernel(
    partner_ref, theta_ref, points_ref, total_ref, next_ref, ends_ref, force_ref, first_ref, second_ref,
    result_hbm, flux_hbm, result_ref, flux_ref, rim_ref, sems,
):
    here = Place()
    levels, rows, cols = theta_ref.shape
    last = rows - 1
    for k in range(flux_ref.shape[0]):
        for r in range(rows):
            flux_ref[k, r : r + 1, :] = total_ref[k : k + 1, r * cols : (r + 1) * cols]
    copies = [
        pltpu.make_async_copy(flux_ref, flux_hbm, sems.at[0]), pltpu.make_async_copy(result_ref, result_hbm, sems.at[1])
    ]
    copies[0].start()
    partner = partner_ref[0]
    is_top, has_south = here.is_top, here.has_south

    def got(e, n):
        return second_ref[here.slot(e, n)].astype(F32)

    west, east = got(here.west, here.n), got(here.east, here.n)
    over, under = got(here.e, here.above), got(here.e, here.below)
    fold = got(partner, here.n)
    fold_east = got(lax.rem(partner + 1, here.count), here.n)[0:1]
    fold_west = got(lax.rem(partner + here.count - 1, here.count), here.n)[0:1]
    over_west, over_east = got(here.west, here.above)[0:1], got(here.east, here.above)[0:1]
    under_west, under_east = got(here.west, here.below)[0:1], got(here.east, here.below)[0:1]
    first_west = first_ref[here.slot(here.west, here.n)].astype(F32)
    first_east = first_ref[here.slot(here.east, here.n)].astype(F32)

    def mark(block):
        return block[0:1, WET_SLOT : WET_SLOT + 1]

    tiles = KINDS * levels // TILE

    def gather(begin, source):
        found = []
        for k in range(tiles):
            e, order = k // (here.block_rows - 1), k % (here.block_rows - 1)
            found.append(got(begin + e, order + (source <= order).astype(jnp.int32))[TILE:])
        return jnp.concatenate(found, axis=0)

    near, far = gather(0, here.pair), gather(here.half, here.other)
    south = jnp.where(has_south, jnp.where(here.even, far, near), 0.0)
    north = jnp.where(here.even, near, far)
    mirror = cols - 1 - lax.broadcasted_iota(jnp.int32, north.shape, 1)
    north = jnp.where(is_top, jnp.take_along_axis(north, mirror, axis=1), north)

    def kinds(bulk, wet, sign):
        t, inner, tend, u, v, d = [bulk[kind * levels : (kind + 1) * levels] for kind in range(KINDS)]
        return t, inner, inner + wet * tend, (sign * wet) * u, (sign * wet) * v, wet * d

    north = kinds(north, jnp.where(is_top, mark(fold), mark(over)), jnp.where(is_top, -1.0, 1.0))
    south = kinds(south, mark(under), 1.0)

    top_west, top_east = jnp.zeros((1, cols), F32), jnp.zeros((1, cols), F32)
    for s in range(here.count):
        row = got(s, here.n)[0:1]
        top_west = jnp.where(first_west[1:2, 1:2] == float(s), row, top_west)
        top_east = jnp.where(first_east[1:2, 1:2] == float(s), row, top_east)
    moved = [fold[0:1], over[0:1], under[0:1], fold_west, over_west, under_west, top_east]
    moved = jnp.concatenate(moved + [jnp.zeros((1, cols), F32)], axis=0)
    moved = pltpu.roll(moved, cols - 2, 1)
    def pair(low, high):
        return jnp.concatenate([low, high, jnp.zeros((TILE - 2, cols), F32)], axis=0)

    along = lax.broadcasted_iota(jnp.int32, (TILE, cols), 1)
    place = lax.rem(along, rows)
    side = pair(west[3:4], east[3:4])
    corner = pair(jnp.where(is_top, top_west, moved[4:5]), jnp.where(is_top, moved[6:7], over_east))
    side_north = jnp.where(place == last, pltpu.roll(corner, last, 1), shifted(side, 1, True))
    corner = jnp.where(has_south, pair(moved[5:6], under_east), 0.0)
    side_south = jnp.where(place == 0, corner, shifted(side, 1, False))
    side_force = jnp.take_along_axis(pair(west[0:1], east[0:1]), jnp.where(along < rows, 8 * along, 0) + FORCE_SLOT, axis=1)
    side_next = stencil(
        side, pair(ends_ref[0:1], east[4:5]), pair(west[4:5], ends_ref[1:2]), side_north, side_south,
        *[pair(west[k : k + 1], east[k : k + 1]) for k in (5, 6, 7)],
    ) + jnp.where(along < rows, side_force, 0.0)

    listed = [
        (west[3:4], east[3:4]),
        (side_next[0:1], side_next[1:2]),
        (jnp.where(is_top, moved[0:1], over[0:1]), jnp.where(is_top, fold[0:1], moved[1:2])),
        (under[0:1], moved[2:3]),
        (jnp.where(is_top, fold_east, moved[4:5]), jnp.where(is_top, moved[3:4], over_east)),
        (moved[5:6], under_east),
    ]
    lanes = {}
    for q, (low, high) in enumerate(listed):
        lanes[2 * q], lanes[(2 * q - 1) % cols] = low, high
    rim = fill(cols, lanes).T.reshape(theta_ref.shape)
    rim_ref[...] = rim

    def listing(q, field):
        return pltpu.roll(field, cols - 2 * q, field.ndim - 1) if q else field

    edges, inners = rim_ref[:, 0, :], rim_ref[:, 1, :]
    lane = lax.broadcasted_iota(jnp.int32, (levels, cols), 1)
    level = lax.broadcasted_iota(jnp.int32, (levels, cols), 0)
    ends = (lane == 0) | (lane == cols - 1)

    def forced(row, force):
        return row + jnp.where(level == 0, force, 0.0)

    flip = cols - 1 - lax.broadcasted_iota(jnp.int32, (8, cols), 1)
    flipped = jnp.take_along_axis(fold[:TILE], flip, axis=1)
    north_force = [jnp.where(is_top, flipped[k : k + 1], over[k : k + 1]) for k in (1, 2)]
    south_force = [under[1:2], under[2:3]]

    def beyond(rows_of, inside, outward, force, q):
        edge_row = stencil(
            rows_of[0], shifted(rows_of[0], 1, True), shifted(rows_of[0], 1, False),
            rows_of[1] if outward else inside, inside if outward else rows_of[1], *rows_of[3:],
        )
        edge_row = jnp.where(ends, listing(q, edges), forced(edge_row, force[0]))
        return edge_row, jnp.where(ends, listing(q, inners), forced(rows_of[2], force[1]))

    north_one, north_two = beyond(north, theta_ref[:, last, :], True, north_force, 2)
    south_one, south_two = beyond(south, theta_ref[:, 0, :], False, south_force, 3)
    south_one, south_two = jnp.where(has_south, south_one, 0.0), jnp.where(has_south, south_two, 0.0)
    shape = theta_ref.shape
    wide = lax.broadcasted_iota(jnp.int32, shape, 2)
    line = lax.broadcasted_iota(jnp.int32, shape, 1)
    force = jnp.where(lax.broadcasted_iota(jnp.int32, shape, 0) == 0, force_ref[...][None], 0.0)
    inside = (lane >= 2) & (lane < cols - 2)
    top_row = next_ref[:, last, :] + jnp.where(inside, points_ref[3, :, last, :] * north[0], 0.0)
    bottom_row = next_ref[:, 0, :] + jnp.where(inside, points_ref[4, :, 0, :] * south[0], 0.0)
    t = jnp.where(line == last, top_row[:, None, :], jnp.where(line == 0, bottom_row[:, None, :], next_ref[...]))

    def outer(row, further, inside, outward, rows_of, force_row, diagonal):
        result = stencil(
            row, jnp.where(lane == cols - 1, diagonal, shifted(row, 1, True)),
            jnp.where(lane == 0, diagonal, shifted(row, 1, False)),
            further if outward else inside, inside if outward else further, *rows_of[3:],
        )
        return forced(result, force_row)

    north_next = outer(north_one, north_two, top_row, True, north, north_force[0], listing(4, edges))
    south_next = outer(south_one, south_two, bottom_row, False, south, south_force[0], listing(5, edges))
    south_next = jnp.where(has_south, south_next, 0.0)

    def advance(t, sides, above, below):
        east = jnp.where(wide == cols - 1, sides, shifted(t, 2, True))
        west = jnp.where(wide == 0, sides, shifted(t, 2, False))
        north = jnp.where(line == last, above[:, None, :], shifted(t, 1, True))
        south = jnp.where(line == 0, below[:, None, :], shifted(t, 1, False))
        result = force
        for k, field in enumerate((t, east, west, north, south)):
            result = result + points_ref[k] * field
        return result

    t = advance(t, rim, north_one, south_one)
    result_ref[...] = advance(t, listing(1, rim), north_next, south_next)
    copies[1].start()
    for copy in copies:
        copy.wait()


def exchange(blocks):
    return lax.all_to_all(blocks, ("ns", "ew"), split_axis=0, concat_axis=0, tiled=True)


def local(theta, velocity, diffusivity, land_mask, fold_partner, atm_flux, remap_src, remap_weights):
    levels, rows, cols = theta.shape
    fields = atm_flux.shape[2]
    shape = jax.ShapeDtypeStruct
    devices = lax.axis_size("ew") * lax.axis_size("ns")
    blocks = (devices, BLOCK, cols)
    room = 60 * 2**20 - 2 * max(0, 2 * devices * BLOCK * cols - 2**20)
    weights = remap_weights[0, 0]
    field, velocity, diffusivity, flux = bring(
        [theta, velocity, diffusivity, atm_flux[0, 0]], [pltpu.VMEM] * 4, room, "bring"
    )
    out = pl.pallas_call(
        first_kernel,
        out_shape=pltpu.VMEM(blocks, BF16),
        in_specs=[SMEM] + [VMEM] * 4,
        out_specs=VMEM,
        scratch_shapes=[pltpu.VMEM((2 * KINDS * levels // TILE + 1, TILE, cols), F32)],
        compiler_params=PARAMS,
        name="first",
    )(fold_partner, field, velocity, diffusivity, flux)
    first = exchange(out)
    sources, weights = bring([remap_src[0], weights], [pltpu.SMEM, pltpu.VMEM], room, "load")
    points, columns, rims, start = pl.pallas_call(
        side_kernel,
        out_shape=(
            pltpu.VMEM((5,) + theta.shape, F32), pltpu.VMEM((2, 3, cols), F32), pltpu.VMEM((2,) + theta.shape, F32),
            pltpu.VMEM(theta.shape, F32),
        ),
        in_specs=[SMEM] + [VMEM] * 3,
        out_specs=(VMEM,) * 4,
        compiler_params=PARAMS,
        cost_estimate=pl.CostEstimate(flops=2**20, bytes_accessed=2**20, transcendentals=0),
        name="side",
    )(land_mask, field, velocity, diffusivity)
    total, force, after, ends, out = pl.pallas_call(
        middle_kernel,
        out_shape=(
            pltpu.VMEM((fields, rows * cols), F32), pltpu.VMEM((rows, cols), F32), pltpu.VMEM(theta.shape, F32),
            pltpu.VMEM((TILE, cols), F32), pltpu.VMEM(blocks, BF16),
        ),
        in_specs=[SMEM] * 3 + [VMEM] * 5,
        out_specs=(VMEM,) * 5,
        compiler_params=PARAMS,
        name="middle",
    )(land_mask, fold_partner, sources, columns, rims, start, weights, first)
    second = exchange(out)
    field, flux = pl.pallas_call(
        last_kernel,
        out_shape=(shape(theta.shape, F32), shape((fields, rows, cols), F32)),
        in_specs=[SMEM] + [VMEM] * 8,
        out_specs=(HBM, HBM),
        scratch_shapes=[
            pltpu.VMEM(theta.shape, F32), pltpu.VMEM((fields, rows, cols), F32), pltpu.VMEM(theta.shape, F32),
            pltpu.SemaphoreType.DMA((2,)),
        ],
        compiler_params=PARAMS,
        name="last",
    )(fold_partner, field, points, total, after, ends, force, first, second)
    return field, flux.reshape(1, 1, fields, rows * cols)


def solution(mesh):
    return jax.shard_map(
        local,
        mesh=mesh,
        in_specs=(
            P(None, "ns", "ew"),
            P(None, None, "ns", "ew"),
            P(None, "ns", "ew"),
            P("ns", "ew"),
            P("ew"),
            P("ns", "ew", None, None),
            P("ns", "ew", None),
            P("ns", "ew", None, None, None),
        ),
        out_specs=(P(None, "ns", "ew"), P("ns", "ew", None, None)),
        check_vma=False,
    )
```

```python
import functools

import jax
import jax.numpy as jnp
from jax import lax
from jax.experimental import pallas as pl
from jax.experimental.pallas import tpu as pltpu
from jax.sharding import PartitionSpec as P

COEFS = (0.5, -0.3, 0.2, 0.4, -0.25, 0.35)
VMEM = pl.BlockSpec(memory_space=pltpu.VMEM)
SMEM = pl.BlockSpec(memory_space=pltpu.SMEM)
HBM = pl.BlockSpec(memory_space=pltpu.HBM)
PARAMS = pltpu.CompilerParams(vmem_limit_bytes=16 * 1024 * 1024)
F32 = jnp.float32
BF16 = jnp.bfloat16
KINDS = 6
TILE = 8
FORCE_SLOT, WET_SLOT, PARTNER_SLOT = 4, 5, 4


def tendency(t, east, west, north, south, u, v, d):
    return d * (east + west + north + south - 4.0 * t) - 0.5 * (u * (east - west) + v * (north - south))


def stencil(t, *others):
    return t + tendency(t, *others)


class Place:
    def __init__(self):
        self.count, self.block_rows = lax.axis_size("ew"), lax.axis_size("ns")
        self.devices = self.count * self.block_rows
        self.e, self.n = lax.axis_index("ew"), lax.axis_index("ns")
        self.top = self.block_rows - 1
        self.is_top = self.n == self.top
        self.has_south = self.n > 0
        self.even = lax.rem(self.n, 2) == 0
        self.east = lax.rem(self.e + 1, self.count)
        self.west = lax.rem(self.e + self.count - 1, self.count)
        self.above = jnp.minimum(self.n + 1, self.top)
        self.below = jnp.maximum(self.n - 1, 0)
        self.pair = jnp.where(self.even, self.n + 1, self.n - 1)
        self.other = jnp.where(self.even, self.below, self.above)

    def slot(self, e, n):
        return n * self.count + e


def relays(row, block_rows):
    is_top = row == block_rows - 1
    first = jnp.where((row % 2 == 0) | is_top, jnp.maximum(row - 2, 0), row + 2)
    return first, jnp.where(is_top, jnp.maximum(row - 3, 0), row + 1 - 2 * (row % 2)), jnp.where(is_top, 0, 2)


def fill(size, rows):
    parts, at = [], 0
    for index in sorted(rows):
        if index > at:
            parts.append(jnp.zeros((index - at, size), F32))
        parts.append(rows[index])
        at = index + 1
    if at < size:
        parts.append(jnp.zeros((size - at, size), F32))
    return jnp.concatenate(parts, axis=0)


def turn(field):
    return field.reshape(field.shape[0] * field.shape[1], field.shape[2]).T


def row_of(ref, row):
    levels, rows, cols = ref.shape
    return ref.reshape(levels * rows, cols), pl.ds(row, levels, stride=rows)


def read_row(ref, row):
    flat, at = row_of(ref, row)
    return flat[at, :]


def write_row(ref, row, values):
    flat, at = row_of(ref, row)
    flat[at, :] = values


def shifted(field, axis, back):
    size = field.shape[axis]
    return pltpu.roll(field, size - 1 if back else 1, axis)


def bring_kernel(count, *refs):
    copies = [pltpu.make_async_copy(refs[i], refs[count + i], refs[-1].at[i]) for i in range(count)]
    for copy in copies:
        copy.start()
    for copy in copies:
        copy.wait()


def bring(arrays, memories, room, name):
    return pl.pallas_call(
        functools.partial(bring_kernel, len(arrays)),
        out_shape=tuple(memory(x.shape, x.dtype) for x, memory in zip(arrays, memories)),
        in_specs=[HBM] * len(arrays),
        out_specs=tuple(VMEM if memory is pltpu.VMEM else SMEM for memory in memories),
        scratch_shapes=[pltpu.SemaphoreType.DMA((len(arrays),))],
        compiler_params=pltpu.CompilerParams(vmem_limit_bytes=room),
        cost_estimate=pl.CostEstimate(flops=2**20, bytes_accessed=2**22, transcendentals=0),
        name=name,
    )(*arrays)


def first_kernel(partner_ref, theta_ref, vel_ref, diff_ref, atm_ref, out_ref, near_ref, bulk_ref):
    here = Place()
    levels, rows, cols = theta_ref.shape
    tiles = levels // TILE
    each = KINDS * tiles
    coef_refs = [vel_ref.at[0], vel_ref.at[1], diff_ref]
    strips = []
    for step in (1, -1):
        edge = rows - 1 if step < 0 else 0
        outer, t, inner = [read_row(theta_ref, edge + k * step) for k in range(3)]
        north, south = (outer, inner) if step < 0 else (inner, outer)
        coef = [read_row(ref, edge + step) for ref in coef_refs]
        tend = tendency(t, shifted(t, 1, True), shifted(t, 1, False), north, south, *coef)
        strips.append([outer, t, tend] + [read_row(ref, edge) for ref in coef_refs])
    for kind, (low, high) in enumerate(zip(*strips)):
        near_ref[kind] = jnp.where(here.even, high, low)
        far = jnp.where(here.even, low, high)
        bulk_ref[pl.ds(kind * tiles, tiles)] = far.reshape(tiles, TILE, cols)
    partner = partner_ref[0].astype(F32)

    @pl.when(here.is_top)
    def _():
        for kind in range(KINDS):
            write_row(bulk_ref, kind, strips[1][kind])
        write_row(bulk_ref, KINDS, jnp.full((levels, cols), partner))
        write_row(bulk_ref, KINDS + 1, jnp.zeros((levels, cols), F32))

    turned = turn(theta_ref[...])
    lane = lax.broadcasted_iota(jnp.int32, (TILE, cols), 1)
    slot = lax.rem(lane, 8)
    spots = [turned[0:1], turned[1:2], turned[cols - 2 : cols - 1], turned[cols - 1 : cols]]
    spots = jnp.concatenate(spots + [jnp.zeros((TILE - 4, cols), F32)], axis=0)
    spots = jnp.where(here.even, spots, pltpu.roll(spots, cols - rows + 1, 1))
    corner = jnp.where(slot[0:1] == PARTNER_SLOT, partner, 0.0)
    for k in range(4):
        moved = pltpu.roll(spots, k, 1) if k else spots
        corner = jnp.where(slot[0:1] == k, moved[k : k + 1], corner)
    atm = atm_ref[...].astype(F32)
    to_west = jnp.concatenate([corner, turned[0:1], atm], axis=0)
    to_east = jnp.concatenate([corner, turned[cols - 1 : cols], atm], axis=0)
    column = jnp.where(here.is_top, partner_ref[0], here.e)
    first, _, skip = relays(jnp.where(here.is_top, here.top, here.other), here.block_rows)
    for e in range(here.count):
        ahead = lax.rem(e - column + here.count, here.count)
        whole, some = jnp.minimum(ahead, TILE - 1), jnp.clip(ahead + TILE - skip, 0, levels - 1)
        own = jnp.where(e == here.east, to_east, to_west)
        for n in range(here.block_rows):
            tile = bulk_ref[jnp.where(first == n, whole, some)]
            owed = (here.n == n) | ((here.other == n) & (here.e == e))
            out_ref[n * here.count + e] = jnp.where(owed, own, tile).astype(BF16)


def side_kernel(
    mask_ref, theta_ref, vel_ref, diff_ref, points_ref, columns_ref, start_ref
):
    levels, rows, cols = theta_ref.shape
    last = rows - 1
    wet = mask_ref[0, 0].astype(F32)
    u, v, d = wet * vel_ref[0], wet * vel_ref[1], wet * diff_ref[...]
    turned = [turn(u), turn(v), turn(d)]
    for side, at in enumerate((0, cols - 1)):
        for k in range(3):
            columns_ref[side, k : k + 1, :] = turned[k][at : at + 1]
    center, east, west, north, south = 1.0 - 4.0 * d, d - 0.5 * u, d + 0.5 * u, d - 0.5 * v, d + 0.5 * v
    for k, field in enumerate((center, east, west, north, south)):
        points_ref[k] = field
    t = theta_ref[...]
    lane = lax.broadcasted_iota(jnp.int32, t.shape, 2)
    line = lax.broadcasted_iota(jnp.int32, t.shape, 1)
    inner = center * t
    inner = inner + east * jnp.where(lane == cols - 1, 0.0, shifted(t, 2, True))
    inner = inner + west * jnp.where(lane == 0, 0.0, shifted(t, 2, False))
    inner = inner + north * jnp.where(line == last, 0.0, shifted(t, 1, True))
    inner = inner + south * jnp.where(line == 0, 0.0, shifted(t, 1, False))
    start_ref[...] = inner


def middle_kernel(
    mask_ref, partner_ref, src_ref, columns_ref, points_ref, start_ref, weights_ref, recv_ref, near_ref,
    total_ref, force_ref, next_ref, ends_ref, out_ref, beyond_ref, plain_ref,
):
    here = Place()
    levels, rows, cols = start_ref.shape
    fields = total_ref.shape[0]
    last = rows - 1
    wet = mask_ref[0, 0].astype(F32)

    pairs, cells, points = weights_ref.shape
    chosen = [recv_ref[here.slot(src_ref[0, pair], here.n)][TILE - fields :] for pair in range(pairs)]
    weights = weights_ref[...].reshape(pairs * cells, points)
    total = jnp.dot(jnp.concatenate(chosen, axis=1), weights, preferred_element_type=F32)
    total_ref[...] = total
    force = jnp.zeros((1, points), F32)
    for k in range(fields):
        force = force + COEFS[k] * total[k : k + 1]
    force = jnp.concatenate([force[:, r * cols : (r + 1) * cols] for r in range(rows)], axis=0)
    force = wet * (0.1 * force)
    force_ref[...] = force

    shape = start_ref.shape
    level = lax.broadcasted_iota(jnp.int32, shape, 0)

    def got(e, n):
        return recv_ref[here.slot(e, n)].astype(F32)

    sides = fill(cols, {0: got(here.west, here.n)[1:2], cols - 1: got(here.east, here.n)[1:2]}).T.reshape(shape)
    from_fold, over, under = got(partner_ref[0], here.n)[0:1], got(here.e, here.above)[0:1], got(here.e, here.below)[0:1]
    facing = jnp.where(here.is_top, from_fold, jnp.where(here.even, under, over))
    facing = jnp.broadcast_to(facing, (TILE, cols))
    facing = [facing[0:1]] + [pltpu.roll(facing, cols - k, 1)[0:1] for k in range(1, 4)]
    facing = [jnp.where(here.is_top, facing[3 - k], facing[k]) for k in range(4)]
    spots = (0, 1, cols - 2, cols - 1)
    beyond_ref[...] = fill(cols, dict(zip(spots, facing))).T.reshape(shape)
    far = read_row(beyond_ref, 0)
    above = jnp.where(here.even, near_ref[0], far)
    below = jnp.where(here.has_south, jnp.where(here.even, far, near_ref[0]), 0.0)
    lane = lax.broadcasted_iota(jnp.int32, shape, 2)
    rim = jnp.where(lane == cols - 1, points_ref[1], jnp.where(lane == 0, points_ref[2], 0.0))
    plain_ref[...] = start_ref[...] + rim * sides
    write_row(plain_ref, last, read_row(plain_ref, last) + read_row(points_ref.at[3], last) * above)
    write_row(plain_ref, 0, read_row(plain_ref, 0) + read_row(points_ref.at[4], 0) * below)
    t = plain_ref[...]
    next_ref[...] = t + jnp.where(level == 0, force[None], 0.0)

    held = [got(m, here.top) for m in range(here.count)]
    size = -(-here.count * TILE // cols) * cols
    tiles = held + [jnp.zeros((size - here.count * TILE, cols), F32)] * (size > here.count * TILE)
    tiles = jnp.concatenate(tiles, axis=0).astype(BF16)
    partners = jnp.concatenate([jnp.broadcast_to(block[KINDS : KINDS + 1, 0:1], (TILE, 1)) for block in held], axis=0)
    wanted = TILE * partners + lax.rem(lax.broadcasted_iota(jnp.int32, partners.shape, 0), TILE).astype(F32)
    pick = lax.broadcasted_iota(jnp.int32, (here.count * TILE, size), 1).astype(F32) == wanted
    folded = jnp.dot(pick.astype(F32).astype(BF16), tiles, preferred_element_type=F32)

    turned = turn(t) + jnp.concatenate([force, jnp.zeros((cols - rows, cols), F32)], axis=0).T
    ends = jnp.concatenate([turned[0:1], turned[cols - 1 : cols], jnp.zeros((TILE - 2, cols), F32)], axis=0)
    lane = lax.broadcasted_iota(jnp.int32, (TILE, cols), 1)
    forces = jnp.concatenate([force, jnp.zeros((cols - rows, cols), F32)], axis=0).T
    forces = jnp.concatenate([forces[0:1], forces[cols - 1 : cols], jnp.zeros((TILE - 2, cols), F32)], axis=0)
    ends_ref[...] = ends
    marks = jnp.take_along_axis(forces, lane // 8, axis=1)
    slot = lax.rem(lane, 8)
    marks = jnp.where(slot == FORCE_SLOT, marks, jnp.where(slot == WET_SLOT, wet, 0.0))
    slot = slot[0:1]

    def corners(shifts, mark):
        row = mark
        for index, shift in enumerate(shifts):
            moved = pltpu.roll(ends, shift % cols, 1) if shift else ends
            row = jnp.where(slot == index, moved[index // 2 : index // 2 + 1], row)
        return row

    up, down = (-last, 2 - last, 2 - last, 4 - last), (0, 0, 2, 2)
    low_mark, high_mark = marks[0:1], marks[1:2]
    low_coef, high_coef = columns_ref[0], columns_ref[1]
    high_force, low_force = [force[last : last + 1], force[last - 1 : last]], [force[0:1], force[1:2]]
    low, high = [turned[0:1], turned[1:2]], [turned[cols - 1 : cols], turned[cols - 2 : cols - 1]]
    base = jnp.concatenate([corners(up, low_mark)] + high_force + low + [low_coef], axis=0)
    to_east = jnp.concatenate([corners(up, high_mark)] + high_force + high + [high_coef], axis=0)
    to_below = jnp.concatenate([corners(down, low_mark)] + low_force + low + [low_coef], axis=0)
    for e in range(here.count):
        ahead = lax.rem(e - here.e + here.count, here.count)
        close = (ahead <= 1) | (ahead == here.count - 1)
        for n in range(here.block_rows):
            begin = jnp.where(n == here.n - 1, to_below, jnp.where(e == here.east, to_east, base))
            owed = (n == here.n) | (close & ((n == here.n - 1) | (n == here.n + 1)))
            if n == here.top:
                tile = folded[e * TILE : (e + 1) * TILE]
            else:
                tile = got(e, max(n - 1, 0) if n % 2 == 0 else n + 1)
            out_ref[n * here.count + e] = jnp.where(owed, begin, tile).astype(BF16)


def last_kernel(
    partner_ref, theta_ref, points_ref, total_ref, next_ref, ends_ref, force_ref, first_ref, second_ref, near_ref,
    result_hbm, flux_hbm, result_ref, flux_ref, rim_ref, tall_ref, tile_ref, sems,
):
    here = Place()
    levels, rows, cols = theta_ref.shape
    last = rows - 1
    for k in range(flux_ref.shape[0]):
        for r in range(rows):
            flux_ref[k, r : r + 1, :] = total_ref[k : k + 1, r * cols : (r + 1) * cols]
    copies = [
        pltpu.make_async_copy(flux_ref, flux_hbm, sems.at[0]), pltpu.make_async_copy(result_ref, result_hbm, sems.at[1])
    ]
    copies[0].start()
    partner = partner_ref[0]
    is_top, has_south = here.is_top, here.has_south

    def got(e, n):
        return second_ref[here.slot(e, n)].astype(F32)

    west, east = got(here.west, here.n), got(here.east, here.n)
    over, under = got(here.e, here.above), got(here.e, here.below)
    fold = got(partner, here.n)
    fold_east = got(lax.rem(partner + 1, here.count), here.n)[0:1]
    fold_west = got(lax.rem(partner + here.count - 1, here.count), here.n)[0:1]
    over_west, over_east = got(here.west, here.above)[0:1], got(here.east, here.above)[0:1]
    under_west, under_east = got(here.west, here.below)[0:1], got(here.east, here.below)[0:1]
    first_west = first_ref[here.slot(here.west, here.n)].astype(F32)
    first_east = first_ref[here.slot(here.east, here.n)].astype(F32)

    def mark(block):
        return block[0:1, WET_SLOT : WET_SLOT + 1]

    first, second, skip = relays(here.n, here.block_rows)
    for k in range(levels):
        ahead, row = (k, first) if k < TILE else (k - TILE + skip, second)
        tile_ref[k] = got(lax.rem(here.e + ahead, here.count), row)
    tiles = levels // TILE
    far = [tile_ref[pl.ds(kind * tiles, tiles)].reshape(levels, cols) for kind in range(KINDS)]
    far = jnp.concatenate(far, axis=0)
    mirrored = jnp.concatenate([read_row(tile_ref, kind) for kind in range(KINDS)], axis=0)
    mirror = cols - 1 - lax.broadcasted_iota(jnp.int32, far.shape, 1)
    far = jnp.where(is_top, jnp.take_along_axis(mirrored, mirror, axis=1), far)
    far = [far[kind * levels : (kind + 1) * levels] for kind in range(KINDS)]
    near = [near_ref[kind] for kind in range(KINDS)]
    north = [jnp.where(here.even, a, b) for a, b in zip(near, far)]
    south = [jnp.where(has_south, jnp.where(here.even, b, a), 0.0) for a, b in zip(near, far)]

    def kinds(strip, wet, sign):
        t, inner, tend, u, v, d = strip
        return t, inner, inner + wet * tend, (sign * wet) * u, (sign * wet) * v, wet * d

    north = kinds(north, jnp.where(is_top, mark(fold), mark(over)), jnp.where(is_top, -1.0, 1.0))
    south = kinds(south, mark(under), 1.0)

    top_west, top_east = jnp.zeros((1, cols), F32), jnp.zeros((1, cols), F32)
    for s in range(here.count):
        row = got(s, here.n)[0:1]
        top_west = jnp.where(first_west[0:1, PARTNER_SLOT : PARTNER_SLOT + 1] == float(s), row, top_west)
        top_east = jnp.where(first_east[0:1, PARTNER_SLOT : PARTNER_SLOT + 1] == float(s), row, top_east)
    moved = [fold[0:1], over[0:1], under[0:1], fold_west, over_west, under_west, top_east]
    moved = jnp.concatenate(moved + [jnp.zeros((1, cols), F32)], axis=0)
    moved = pltpu.roll(moved, cols - 2, 1)
    def pair(low, high):
        return jnp.concatenate([low, high, jnp.zeros((TILE - 2, cols), F32)], axis=0)

    along = lax.broadcasted_iota(jnp.int32, (TILE, cols), 1)
    place = lax.rem(along, rows)
    side = pair(west[3:4], east[3:4])
    corner = pair(jnp.where(is_top, top_west, moved[4:5]), jnp.where(is_top, moved[6:7], over_east))
    side_north = jnp.where(place == last, pltpu.roll(corner, last, 1), shifted(side, 1, True))
    corner = jnp.where(has_south, pair(moved[5:6], under_east), 0.0)
    side_south = jnp.where(place == 0, corner, shifted(side, 1, False))
    side_force = jnp.take_along_axis(pair(west[0:1], east[0:1]), jnp.where(along < rows, 8 * along, 0) + FORCE_SLOT, axis=1)
    side_next = stencil(
        side, pair(ends_ref[0:1], east[4:5]), pair(west[4:5], ends_ref[1:2]), side_north, side_south,
        *[pair(west[k : k + 1], east[k : k + 1]) for k in (5, 6, 7)],
    ) + jnp.where(along < rows, side_force, 0.0)

    listed = [
        (west[3:4], east[3:4]),
        (side_next[0:1], side_next[1:2]),
        (jnp.where(is_top, moved[0:1], over[0:1]), jnp.where(is_top, fold[0:1], moved[1:2])),
        (under[0:1], moved[2:3]),
        (jnp.where(is_top, fold_east, moved[4:5]), jnp.where(is_top, moved[3:4], over_east)),
        (moved[5:6], under_east),
    ]
    lanes = {}
    for q, (low, high) in enumerate(listed):
        lanes[2 * q], lanes[(2 * q - 1) % cols] = low, high
    rim = fill(cols, lanes).T.reshape(theta_ref.shape)
    rim_ref[...] = rim

    def listing(q, field):
        return pltpu.roll(field, cols - 2 * q, field.ndim - 1) if q else field

    edges, inners = read_row(rim_ref, 0), read_row(rim_ref, 1)
    lane = lax.broadcasted_iota(jnp.int32, (levels, cols), 1)
    level = lax.broadcasted_iota(jnp.int32, (levels, cols), 0)
    ends = (lane == 0) | (lane == cols - 1)

    def forced(row, force):
        return row + jnp.where(level == 0, force, 0.0)

    flip = cols - 1 - lax.broadcasted_iota(jnp.int32, (8, cols), 1)
    flipped = jnp.take_along_axis(fold[:TILE], flip, axis=1)
    north_force = [jnp.where(is_top, flipped[k : k + 1], over[k : k + 1]) for k in (1, 2)]
    south_force = [under[1:2], under[2:3]]

    def beyond(rows_of, inside, outward, force, q):
        edge_row = stencil(
            rows_of[0], shifted(rows_of[0], 1, True), shifted(rows_of[0], 1, False),
            rows_of[1] if outward else inside, inside if outward else rows_of[1], *rows_of[3:],
        )
        edge_row = jnp.where(ends, listing(q, edges), forced(edge_row, force[0]))
        return edge_row, jnp.where(ends, listing(q, inners), forced(rows_of[2], force[1]))

    north_one, north_two = beyond(north, read_row(theta_ref, last), True, north_force, 2)
    south_one, south_two = beyond(south, read_row(theta_ref, 0), False, south_force, 3)
    south_one, south_two = jnp.where(has_south, south_one, 0.0), jnp.where(has_south, south_two, 0.0)
    shape = theta_ref.shape
    wide = lax.broadcasted_iota(jnp.int32, shape, 2)
    force = jnp.where(lax.broadcasted_iota(jnp.int32, shape, 0) == 0, force_ref[...][None], 0.0)
    inside = (lane >= 2) & (lane < cols - 2)
    more_north, more_south = inside & jnp.logical_not(here.even), inside & here.even
    top_row = read_row(next_ref, last) + jnp.where(more_north, read_row(points_ref.at[3], last) * north[0], 0.0)
    bottom_row = read_row(next_ref, 0) + jnp.where(more_south, read_row(points_ref.at[4], 0) * south[0], 0.0)
    tall_ref[:, TILE : 2 * TILE, :] = next_ref[...]
    write_row(tall_ref, TILE + last, top_row)
    write_row(tall_ref, TILE, bottom_row)

    def outer(row, further, inside, outward, rows_of, force_row, diagonal):
        result = stencil(
            row, jnp.where(lane == cols - 1, diagonal, shifted(row, 1, True)),
            jnp.where(lane == 0, diagonal, shifted(row, 1, False)),
            further if outward else inside, inside if outward else further, *rows_of[3:],
        )
        return forced(result, force_row)

    north_next = outer(north_one, north_two, top_row, True, north, north_force[0], listing(4, edges))
    south_next = outer(south_one, south_two, bottom_row, False, south, south_force[0], listing(5, edges))
    south_next = jnp.where(has_south, south_next, 0.0)

    def advance(sides, above, below):
        write_row(tall_ref, 2 * TILE, above)
        write_row(tall_ref, TILE - 1, below)
        t = tall_ref[:, TILE : 2 * TILE, :]
        east = jnp.where(wide == cols - 1, sides, shifted(t, 2, True))
        west = jnp.where(wide == 0, sides, shifted(t, 2, False))
        north, south = tall_ref[:, TILE + 1 : 2 * TILE + 1, :], tall_ref[:, TILE - 1 : 2 * TILE - 1, :]
        result = force
        for k, field in enumerate((t, east, west, north, south)):
            result = result + points_ref[k] * field
        return result

    tall_ref[:, TILE : 2 * TILE, :] = advance(rim, north_one, south_one)
    result_ref[...] = advance(listing(1, rim), north_next, south_next)
    copies[1].start()
    for copy in copies:
        copy.wait()


def exchange(blocks):
    return lax.all_to_all(blocks, ("ns", "ew"), split_axis=0, concat_axis=0, tiled=True)


def swap(rows):
    pairs = [(i, i + 1) for i in range(0, lax.axis_size("ns"), 2)]
    return lax.ppermute(rows, "ns", pairs + [(b, a) for a, b in pairs])


def local(theta, velocity, diffusivity, land_mask, fold_partner, atm_flux, remap_src, remap_weights):
    levels, rows, cols = theta.shape
    fields = atm_flux.shape[2]
    shape = jax.ShapeDtypeStruct
    devices = lax.axis_size("ew") * lax.axis_size("ns")
    blocks = (devices, TILE, cols)
    room = 60 * 2**20 - 2 * max(0, 4 * devices * TILE * cols - 2**20)
    weights = remap_weights[0, 0]
    field, velocity, diffusivity, flux = bring(
        [theta, velocity, diffusivity, atm_flux[0, 0]], [pltpu.VMEM] * 4, room, "bring"
    )
    out, near = pl.pallas_call(
        first_kernel,
        out_shape=(pltpu.VMEM(blocks, BF16), pltpu.VMEM((KINDS, levels, cols), F32)),
        in_specs=[SMEM] + [VMEM] * 4,
        out_specs=(VMEM,) * 2,
        scratch_shapes=[pltpu.VMEM((levels, TILE, cols), F32)],
        compiler_params=PARAMS,
        name="first",
    )(fold_partner, field, velocity, diffusivity, flux)
    first, near = exchange(out), swap(near)
    sources, weights = bring([remap_src[0], weights], [pltpu.SMEM, pltpu.VMEM], room, "load")
    points, columns, start = pl.pallas_call(
        side_kernel,
        out_shape=(
            pltpu.VMEM((5,) + theta.shape, F32), pltpu.VMEM((2, 3, cols), F32), pltpu.VMEM(theta.shape, F32),
        ),
        in_specs=[SMEM] + [VMEM] * 3,
        out_specs=(VMEM,) * 3,
        compiler_params=PARAMS,
        cost_estimate=pl.CostEstimate(flops=2**20, bytes_accessed=2**20, transcendentals=0),
        name="side",
    )(land_mask, field, velocity, diffusivity)
    total, force, after, ends, out = pl.pallas_call(
        middle_kernel,
        out_shape=(
            pltpu.VMEM((fields, rows * cols), F32), pltpu.VMEM((rows, cols), F32), pltpu.VMEM(theta.shape, F32),
            pltpu.VMEM((TILE, cols), F32), pltpu.VMEM(blocks, BF16),
        ),
        in_specs=[SMEM] * 3 + [VMEM] * 6,
        out_specs=(VMEM,) * 5,
        scratch_shapes=[pltpu.VMEM(theta.shape, F32)] * 2,
        compiler_params=PARAMS,
        name="middle",
    )(land_mask, fold_partner, sources, columns, points, start, weights, first, near)
    second = exchange(out)
    field, flux = pl.pallas_call(
        last_kernel,
        out_shape=(shape(theta.shape, F32), shape((fields, rows, cols), F32)),
        in_specs=[SMEM] + [VMEM] * 9,
        out_specs=(HBM, HBM),
        scratch_shapes=[
            pltpu.VMEM(theta.shape, F32), pltpu.VMEM((fields, rows, cols), F32), pltpu.VMEM(theta.shape, F32),
            pltpu.VMEM((levels, 3 * TILE, cols), F32), pltpu.VMEM((levels, TILE, cols), F32),
            pltpu.SemaphoreType.DMA((2,)),
        ],
        compiler_params=PARAMS,
        name="last",
    )(fold_partner, field, points, total, after, ends, force, first, second, near)
    return field, flux.reshape(1, 1, fields, rows * cols)


def solution(mesh):
    return jax.shard_map(
        local,
        mesh=mesh,
        in_specs=(
            P(None, "ns", "ew"),
            P(None, None, "ns", "ew"),
            P(None, "ns", "ew"),
            P("ns", "ew"),
            P("ew"),
            P("ns", "ew", None, None),
            P("ns", "ew", None),
            P("ns", "ew", None, None, None),
        ),
        out_specs=(P(None, "ns", "ew"), P("ns", "ew", None, None)),
        check_vma=False,
    )
```

```python
import functools

import jax
import jax.numpy as jnp
from jax import lax
from jax.experimental import pallas as pl
from jax.experimental.pallas import tpu as pltpu
from jax.sharding import PartitionSpec as P

COEFS = (0.5, -0.3, 0.2, 0.4, -0.25, 0.35)
VMEM = pl.BlockSpec(memory_space=pltpu.VMEM)
SMEM = pl.BlockSpec(memory_space=pltpu.SMEM)
HBM = pl.BlockSpec(memory_space=pltpu.HBM)
PARAMS = pltpu.CompilerParams(vmem_limit_bytes=16 * 1024 * 1024)
F32 = jnp.float32
BF16 = jnp.bfloat16
KINDS = 6
TILE = 8
FORCE_SLOT, WET_SLOT, PARTNER_SLOT = 4, 5, 4


def tendency(t, east, west, north, south, u, v, d):
    return d * (east + west + north + south - 4.0 * t) - 0.5 * (u * (east - west) + v * (north - south))


def stencil(t, *others):
    return t + tendency(t, *others)


class Place:
    def __init__(self):
        self.count, self.block_rows = lax.axis_size("ew"), lax.axis_size("ns")
        self.devices = self.count * self.block_rows
        self.e, self.n = lax.axis_index("ew"), lax.axis_index("ns")
        self.top = self.block_rows - 1
        self.is_top = self.n == self.top
        self.has_south = self.n > 0
        self.even = lax.rem(self.n, 2) == 0
        self.east = lax.rem(self.e + 1, self.count)
        self.west = lax.rem(self.e + self.count - 1, self.count)
        self.above = jnp.minimum(self.n + 1, self.top)
        self.below = jnp.maximum(self.n - 1, 0)
        self.pair = jnp.where(self.even, self.n + 1, self.n - 1)
        self.other = jnp.where(self.even, self.below, self.above)

    def slot(self, e, n):
        return n * self.count + e


def relays(row, block_rows):
    is_top = row == block_rows - 1
    first = jnp.where((row % 2 == 0) | is_top, jnp.maximum(row - 2, 0), row + 2)
    return first, jnp.where(is_top, jnp.maximum(row - 3, 0), row + 1 - 2 * (row % 2)), jnp.where(is_top, 0, 2)


def fill(size, rows):
    parts, at = [], 0
    for index in sorted(rows):
        if index > at:
            parts.append(jnp.zeros((index - at, size), F32))
        parts.append(rows[index])
        at = index + 1
    if at < size:
        parts.append(jnp.zeros((size - at, size), F32))
    return jnp.concatenate(parts, axis=0)


def turn(field):
    return field.reshape(field.shape[0] * field.shape[1], field.shape[2]).T


def row_of(ref, row):
    levels, rows, cols = ref.shape
    return ref.reshape(levels * rows, cols), pl.ds(row, levels, stride=rows)


def read_row(ref, row):
    flat, at = row_of(ref, row)
    return flat[at, :]


def write_row(ref, row, values):
    flat, at = row_of(ref, row)
    flat[at, :] = values


def shifted(field, axis, back):
    size = field.shape[axis]
    return pltpu.roll(field, size - 1 if back else 1, axis)


def bring_kernel(count, *refs):
    copies = [pltpu.make_async_copy(refs[i], refs[count + i], refs[-1].at[i]) for i in range(count)]
    for copy in copies:
        copy.start()
    for copy in copies:
        copy.wait()


def bring(arrays, memories, room, name):
    return pl.pallas_call(
        functools.partial(bring_kernel, len(arrays)),
        out_shape=tuple(memory(x.shape, x.dtype) for x, memory in zip(arrays, memories)),
        in_specs=[HBM] * len(arrays),
        out_specs=tuple(VMEM if memory is pltpu.VMEM else SMEM for memory in memories),
        scratch_shapes=[pltpu.SemaphoreType.DMA((len(arrays),))],
        compiler_params=pltpu.CompilerParams(vmem_limit_bytes=room),
        cost_estimate=pl.CostEstimate(flops=2**20, bytes_accessed=2**22, transcendentals=0),
        name=name,
    )(*arrays)


def first_kernel(partner_ref, theta_ref, vel_ref, diff_ref, atm_ref, out_ref, near_ref, bulk_ref):
    here = Place()
    levels, rows, cols = theta_ref.shape
    tiles = levels // TILE
    each = KINDS * tiles
    coef_refs = [vel_ref.at[0], vel_ref.at[1], diff_ref]
    turned = turn(theta_ref[...])
    strips = []
    for step in (1, -1):
        edge = rows - 1 if step < 0 else 0
        outer, t, inner = [read_row(theta_ref, edge + k * step) for k in range(3)]
        north, south = (outer, inner) if step < 0 else (inner, outer)
        coef = [read_row(ref, edge + step) for ref in coef_refs]
        tend = tendency(t, shifted(t, 1, True), shifted(t, 1, False), north, south, *coef)
        strips.append([outer, t, tend] + [read_row(ref, edge) for ref in coef_refs])
    for kind, (low, high) in enumerate(zip(*strips)):
        near_ref[kind] = jnp.where(here.even, high, low)
        far = jnp.where(here.even, low, high)
        bulk_ref[pl.ds(kind * tiles, tiles)] = far.reshape(tiles, TILE, cols)
    partner = partner_ref[0].astype(F32)
    fold_ref = bulk_ref.at[pl.ds(levels, levels)]
    for kind in range(KINDS):
        write_row(fold_ref, kind, strips[1][kind])
    write_row(fold_ref, KINDS, jnp.full((levels, cols), partner))
    write_row(fold_ref, KINDS + 1, jnp.zeros((levels, cols), F32))
    lane = lax.broadcasted_iota(jnp.int32, (TILE, cols), 1)
    slot = lax.rem(lane, 8)
    spots = [turned[0:1], turned[1:2], turned[cols - 2 : cols - 1], turned[cols - 1 : cols]]
    spots = jnp.concatenate(spots + [jnp.zeros((TILE - 4, cols), F32)], axis=0)
    spots = jnp.where(here.even, spots, pltpu.roll(spots, cols - rows + 1, 1))
    corner = jnp.where(slot[0:1] == PARTNER_SLOT, partner, 0.0)
    for k in range(4):
        moved = pltpu.roll(spots, k, 1) if k else spots
        corner = jnp.where(slot[0:1] == k, moved[k : k + 1], corner)
    atm = atm_ref[...].astype(F32)
    to_west = jnp.concatenate([corner, turned[0:1], atm], axis=0)
    to_east = jnp.concatenate([corner, turned[cols - 1 : cols], atm], axis=0)
    column = jnp.where(here.is_top, partner_ref[0], here.e)
    first, _, skip = relays(jnp.where(here.is_top, here.top, here.other), here.block_rows)
    begin = jnp.where(here.is_top, levels, 0)
    for e in range(here.count):
        ahead = lax.rem(e - column + here.count, here.count)
        whole = begin + jnp.minimum(ahead, TILE - 1)
        some = begin + jnp.clip(ahead + TILE - skip, 0, levels - 1)
        own = jnp.where(e == here.east, to_east, to_west)
        for n in range(here.block_rows):
            tile = bulk_ref[jnp.where(first == n, whole, some)]
            owed = (here.n == n) | ((here.other == n) & (here.e == e))
            out_ref[n * here.count + e] = jnp.where(owed, own, tile).astype(BF16)


def side_kernel(
    mask_ref, theta_ref, vel_ref, diff_ref, points_ref, columns_ref, start_ref
):
    levels, rows, cols = theta_ref.shape
    last = rows - 1
    wet = mask_ref[0, 0].astype(F32)
    u, v, d = wet * vel_ref[0], wet * vel_ref[1], wet * diff_ref[...]
    turned = [turn(u), turn(v), turn(d)]
    for side, at in enumerate((0, cols - 1)):
        for k in range(3):
            columns_ref[side, k : k + 1, :] = turned[k][at : at + 1]
    center, east, west, north, south = 1.0 - 4.0 * d, d - 0.5 * u, d + 0.5 * u, d - 0.5 * v, d + 0.5 * v
    for k, field in enumerate((center, east, west, north, south)):
        points_ref[k] = field
    t = theta_ref[...]
    lane = lax.broadcasted_iota(jnp.int32, t.shape, 2)
    line = lax.broadcasted_iota(jnp.int32, t.shape, 1)
    inner = center * t
    inner = inner + east * jnp.where(lane == cols - 1, 0.0, shifted(t, 2, True))
    inner = inner + west * jnp.where(lane == 0, 0.0, shifted(t, 2, False))
    inner = inner + north * jnp.where(line == last, 0.0, shifted(t, 1, True))
    inner = inner + south * jnp.where(line == 0, 0.0, shifted(t, 1, False))
    start_ref[...] = inner


def middle_kernel(
    mask_ref, partner_ref, src_ref, columns_ref, points_ref, start_ref, weights_ref, recv_ref, near_ref,
    total_ref, force_ref, next_ref, ends_ref, out_ref, beyond_ref, plain_ref,
):
    here = Place()
    levels, rows, cols = start_ref.shape
    fields = total_ref.shape[0]
    last = rows - 1
    wet = mask_ref[0, 0].astype(F32)

    pairs, cells, points = weights_ref.shape
    chosen = [recv_ref[here.slot(src_ref[0, pair], here.n)][TILE - fields :] for pair in range(pairs)]
    weights = weights_ref[...].reshape(pairs * cells, points)
    total = jnp.dot(jnp.concatenate(chosen, axis=1), weights, preferred_element_type=F32)
    total_ref[...] = total
    force = jnp.zeros((1, points), F32)
    for k in range(fields):
        force = force + COEFS[k] * total[k : k + 1]
    force = jnp.concatenate([force[:, r * cols : (r + 1) * cols] for r in range(rows)], axis=0)
    force = wet * (0.1 * force)
    force_ref[...] = force

    shape = start_ref.shape
    level = lax.broadcasted_iota(jnp.int32, shape, 0)

    def got(e, n):
        return recv_ref[here.slot(e, n)].astype(F32)

    sides = fill(cols, {0: got(here.west, here.n)[1:2], cols - 1: got(here.east, here.n)[1:2]}).T.reshape(shape)
    from_fold, over, under = got(partner_ref[0], here.n)[0:1], got(here.e, here.above)[0:1], got(here.e, here.below)[0:1]
    facing = jnp.where(here.is_top, from_fold, jnp.where(here.even, under, over))
    facing = jnp.broadcast_to(facing, (TILE, cols))
    facing = [facing[0:1]] + [pltpu.roll(facing, cols - k, 1)[0:1] for k in range(1, 4)]
    facing = [jnp.where(here.is_top, facing[3 - k], facing[k]) for k in range(4)]
    spots = (0, 1, cols - 2, cols - 1)
    beyond_ref[...] = fill(cols, dict(zip(spots, facing))).T.reshape(shape)
    far = read_row(beyond_ref, 0)
    above = jnp.where(here.even, near_ref[0], far)
    below = jnp.where(here.has_south, jnp.where(here.even, far, near_ref[0]), 0.0)
    lane = lax.broadcasted_iota(jnp.int32, shape, 2)
    rim = jnp.where(lane == cols - 1, points_ref[1], jnp.where(lane == 0, points_ref[2], 0.0))
    plain_ref[...] = start_ref[...] + rim * sides
    write_row(plain_ref, last, read_row(plain_ref, last) + read_row(points_ref.at[3], last) * above)
    write_row(plain_ref, 0, read_row(plain_ref, 0) + read_row(points_ref.at[4], 0) * below)
    t = plain_ref[...]
    next_ref[...] = t + jnp.where(level == 0, force[None], 0.0)

    held = [got(m, here.top) for m in range(here.count)]
    size = -(-here.count * TILE // cols) * cols
    tiles = held + [jnp.zeros((size - here.count * TILE, cols), F32)] * (size > here.count * TILE)
    tiles = jnp.concatenate(tiles, axis=0).astype(BF16)
    partners = jnp.concatenate([jnp.broadcast_to(block[KINDS : KINDS + 1, 0:1], (TILE, 1)) for block in held], axis=0)
    wanted = TILE * partners + lax.rem(lax.broadcasted_iota(jnp.int32, partners.shape, 0), TILE).astype(F32)
    pick = lax.broadcasted_iota(jnp.int32, (here.count * TILE, size), 1).astype(F32) == wanted
    folded = jnp.dot(pick.astype(F32).astype(BF16), tiles, preferred_element_type=F32)

    turned = turn(t) + jnp.concatenate([force, jnp.zeros((cols - rows, cols), F32)], axis=0).T
    ends = jnp.concatenate([turned[0:1], turned[cols - 1 : cols], jnp.zeros((TILE - 2, cols), F32)], axis=0)
    lane = lax.broadcasted_iota(jnp.int32, (TILE, cols), 1)
    forces = jnp.concatenate([force, jnp.zeros((cols - rows, cols), F32)], axis=0).T
    forces = jnp.concatenate([forces[0:1], forces[cols - 1 : cols], jnp.zeros((TILE - 2, cols), F32)], axis=0)
    ends_ref[...] = ends
    marks = jnp.take_along_axis(forces, lane // 8, axis=1)
    slot = lax.rem(lane, 8)
    marks = jnp.where(slot == FORCE_SLOT, marks, jnp.where(slot == WET_SLOT, wet, 0.0))
    slot = slot[0:1]

    def corners(shifts, mark):
        row = mark
        for index, shift in enumerate(shifts):
            moved = pltpu.roll(ends, shift % cols, 1) if shift else ends
            row = jnp.where(slot == index, moved[index // 2 : index // 2 + 1], row)
        return row

    up, down = (-last, 2 - last, 2 - last, 4 - last), (0, 0, 2, 2)
    low_mark, high_mark = marks[0:1], marks[1:2]
    low_coef, high_coef = columns_ref[0], columns_ref[1]
    high_force, low_force = [force[last : last + 1], force[last - 1 : last]], [force[0:1], force[1:2]]
    low, high = [turned[0:1], turned[1:2]], [turned[cols - 1 : cols], turned[cols - 2 : cols - 1]]
    base = jnp.concatenate([corners(up, low_mark)] + high_force + low + [low_coef], axis=0)
    to_east = jnp.concatenate([corners(up, high_mark)] + high_force + high + [high_coef], axis=0)
    to_below = jnp.concatenate([corners(down, low_mark)] + low_force + low + [low_coef], axis=0)
    for e in range(here.count):
        ahead = lax.rem(e - here.e + here.count, here.count)
        close = (ahead <= 1) | (ahead == here.count - 1)
        for n in range(here.block_rows):
            begin = jnp.where(n == here.n - 1, to_below, jnp.where(e == here.east, to_east, base))
            owed = (n == here.n) | (close & ((n == here.n - 1) | (n == here.n + 1)))
            if n == here.top:
                tile = folded[e * TILE : (e + 1) * TILE]
            else:
                tile = got(e, max(n - 1, 0) if n % 2 == 0 else n + 1)
            out_ref[n * here.count + e] = jnp.where(owed, begin, tile).astype(BF16)


def last_kernel(
    partner_ref, theta_ref, points_ref, total_ref, next_ref, ends_ref, force_ref, first_ref, second_ref, near_ref,
    result_hbm, flux_hbm, result_ref, flux_ref, rim_ref, tall_ref, tile_ref, sems,
):
    here = Place()
    levels, rows, cols = theta_ref.shape
    last = rows - 1
    for k in range(flux_ref.shape[0]):
        for r in range(rows):
            flux_ref[k, r : r + 1, :] = total_ref[k : k + 1, r * cols : (r + 1) * cols]
    copies = [
        pltpu.make_async_copy(flux_ref, flux_hbm, sems.at[0]), pltpu.make_async_copy(result_ref, result_hbm, sems.at[1])
    ]
    copies[0].start()
    partner = partner_ref[0]
    is_top, has_south = here.is_top, here.has_south

    def got(e, n):
        return second_ref[here.slot(e, n)].astype(F32)

    west, east = got(here.west, here.n), got(here.east, here.n)
    over, under = got(here.e, here.above), got(here.e, here.below)
    fold = got(partner, here.n)
    fold_east = got(lax.rem(partner + 1, here.count), here.n)[0:1]
    fold_west = got(lax.rem(partner + here.count - 1, here.count), here.n)[0:1]
    over_west, over_east = got(here.west, here.above)[0:1], got(here.east, here.above)[0:1]
    under_west, under_east = got(here.west, here.below)[0:1], got(here.east, here.below)[0:1]
    first_west = first_ref[here.slot(here.west, here.n)].astype(F32)
    first_east = first_ref[here.slot(here.east, here.n)].astype(F32)

    def mark(block):
        return block[0:1, WET_SLOT : WET_SLOT + 1]

    first, second, skip = relays(here.n, here.block_rows)
    for k in range(levels):
        ahead, row = (k, first) if k < TILE else (k - TILE + skip, second)
        tile_ref[k] = got(lax.rem(here.e + ahead, here.count), row)
    tiles = levels // TILE
    far = [tile_ref[pl.ds(kind * tiles, tiles)].reshape(levels, cols) for kind in range(KINDS)]
    far = jnp.concatenate(far, axis=0)
    mirrored = jnp.concatenate([read_row(tile_ref, kind) for kind in range(KINDS)], axis=0)
    mirror = cols - 1 - lax.broadcasted_iota(jnp.int32, far.shape, 1)
    far = jnp.where(is_top, jnp.take_along_axis(mirrored, mirror, axis=1), far)
    far = [far[kind * levels : (kind + 1) * levels] for kind in range(KINDS)]
    near = [near_ref[kind] for kind in range(KINDS)]
    north = [jnp.where(here.even, a, b) for a, b in zip(near, far)]
    south = [jnp.where(has_south, jnp.where(here.even, b, a), 0.0) for a, b in zip(near, far)]

    def kinds(strip, wet, sign):
        t, inner, tend, u, v, d = strip
        return t, inner, inner + wet * tend, (sign * wet) * u, (sign * wet) * v, wet * d

    north = kinds(north, jnp.where(is_top, mark(fold), mark(over)), jnp.where(is_top, -1.0, 1.0))
    south = kinds(south, mark(under), 1.0)

    top_west, top_east = jnp.zeros((1, cols), F32), jnp.zeros((1, cols), F32)
    for s in range(here.count):
        row = got(s, here.n)[0:1]
        top_west = jnp.where(first_west[0:1, PARTNER_SLOT : PARTNER_SLOT + 1] == float(s), row, top_west)
        top_east = jnp.where(first_east[0:1, PARTNER_SLOT : PARTNER_SLOT + 1] == float(s), row, top_east)
    moved = [fold[0:1], over[0:1], under[0:1], fold_west, over_west, under_west, top_east]
    moved = jnp.concatenate(moved + [jnp.zeros((1, cols), F32)], axis=0)
    moved = pltpu.roll(moved, cols - 2, 1)
    def pair(low, high):
        return jnp.concatenate([low, high, jnp.zeros((TILE - 2, cols), F32)], axis=0)

    along = lax.broadcasted_iota(jnp.int32, (TILE, cols), 1)
    place = lax.rem(along, rows)
    side = pair(west[3:4], east[3:4])
    corner = pair(jnp.where(is_top, top_west, moved[4:5]), jnp.where(is_top, moved[6:7], over_east))
    side_north = jnp.where(place == last, pltpu.roll(corner, last, 1), shifted(side, 1, True))
    corner = jnp.where(has_south, pair(moved[5:6], under_east), 0.0)
    side_south = jnp.where(place == 0, corner, shifted(side, 1, False))
    side_force = jnp.take_along_axis(pair(west[0:1], east[0:1]), jnp.where(along < rows, 8 * along, 0) + FORCE_SLOT, axis=1)
    side_next = stencil(
        side, pair(ends_ref[0:1], east[4:5]), pair(west[4:5], ends_ref[1:2]), side_north, side_south,
        *[pair(west[k : k + 1], east[k : k + 1]) for k in (5, 6, 7)],
    ) + jnp.where(along < rows, side_force, 0.0)

    listed = [
        (west[3:4], east[3:4]),
        (side_next[0:1], side_next[1:2]),
        (jnp.where(is_top, moved[0:1], over[0:1]), jnp.where(is_top, fold[0:1], moved[1:2])),
        (under[0:1], moved[2:3]),
        (jnp.where(is_top, fold_east, moved[4:5]), jnp.where(is_top, moved[3:4], over_east)),
        (moved[5:6], under_east),
    ]
    lanes = {}
    for q, (low, high) in enumerate(listed):
        lanes[2 * q], lanes[(2 * q - 1) % cols] = low, high
    rim = fill(cols, lanes).T.reshape(theta_ref.shape)
    rim_ref[...] = rim

    def listing(q, field):
        return pltpu.roll(field, cols - 2 * q, field.ndim - 1) if q else field

    edges, inners = read_row(rim_ref, 0), read_row(rim_ref, 1)
    lane = lax.broadcasted_iota(jnp.int32, (levels, cols), 1)
    level = lax.broadcasted_iota(jnp.int32, (levels, cols), 0)
    ends = (lane == 0) | (lane == cols - 1)

    def forced(row, force):
        return row + jnp.where(level == 0, force, 0.0)

    flip = cols - 1 - lax.broadcasted_iota(jnp.int32, (8, cols), 1)
    flipped = jnp.take_along_axis(fold[:TILE], flip, axis=1)
    north_force = [jnp.where(is_top, flipped[k : k + 1], over[k : k + 1]) for k in (1, 2)]
    south_force = [under[1:2], under[2:3]]

    def beyond(rows_of, inside, outward, force, q):
        edge_row = stencil(
            rows_of[0], shifted(rows_of[0], 1, True), shifted(rows_of[0], 1, False),
            rows_of[1] if outward else inside, inside if outward else rows_of[1], *rows_of[3:],
        )
        edge_row = jnp.where(ends, listing(q, edges), forced(edge_row, force[0]))
        return edge_row, jnp.where(ends, listing(q, inners), forced(rows_of[2], force[1]))

    north_one, north_two = beyond(north, read_row(theta_ref, last), True, north_force, 2)
    south_one, south_two = beyond(south, read_row(theta_ref, 0), False, south_force, 3)
    south_one, south_two = jnp.where(has_south, south_one, 0.0), jnp.where(has_south, south_two, 0.0)
    shape = theta_ref.shape
    wide = lax.broadcasted_iota(jnp.int32, shape, 2)
    force = jnp.where(lax.broadcasted_iota(jnp.int32, shape, 0) == 0, force_ref[...][None], 0.0)
    inside = (lane >= 2) & (lane < cols - 2)
    more_north, more_south = inside & jnp.logical_not(here.even), inside & here.even
    top_row = read_row(next_ref, last) + jnp.where(more_north, read_row(points_ref.at[3], last) * north[0], 0.0)
    bottom_row = read_row(next_ref, 0) + jnp.where(more_south, read_row(points_ref.at[4], 0) * south[0], 0.0)
    tall_ref[:, TILE : 2 * TILE, :] = next_ref[...]
    write_row(tall_ref, TILE + last, top_row)
    write_row(tall_ref, TILE, bottom_row)

    def outer(row, further, inside, outward, rows_of, force_row, diagonal):
        result = stencil(
            row, jnp.where(lane == cols - 1, diagonal, shifted(row, 1, True)),
            jnp.where(lane == 0, diagonal, shifted(row, 1, False)),
            further if outward else inside, inside if outward else further, *rows_of[3:],
        )
        return forced(result, force_row)

    north_next = outer(north_one, north_two, top_row, True, north, north_force[0], listing(4, edges))
    south_next = outer(south_one, south_two, bottom_row, False, south, south_force[0], listing(5, edges))
    south_next = jnp.where(has_south, south_next, 0.0)

    def advance(sides, above, below):
        write_row(tall_ref, 2 * TILE, above)
        write_row(tall_ref, TILE - 1, below)
        t = tall_ref[:, TILE : 2 * TILE, :]
        east = jnp.where(wide == cols - 1, sides, shifted(t, 2, True))
        west = jnp.where(wide == 0, sides, shifted(t, 2, False))
        north, south = tall_ref[:, TILE + 1 : 2 * TILE + 1, :], tall_ref[:, TILE - 1 : 2 * TILE - 1, :]
        result = force
        for k, field in enumerate((t, east, west, north, south)):
            result = result + points_ref[k] * field
        return result

    tall_ref[:, TILE : 2 * TILE, :] = advance(rim, north_one, south_one)
    result_ref[...] = advance(listing(1, rim), north_next, south_next)
    copies[1].start()
    for copy in copies:
        copy.wait()


def exchange(blocks):
    return lax.all_to_all(blocks, ("ns", "ew"), split_axis=0, concat_axis=0, tiled=True)


def swap(rows):
    pairs = [(i, i + 1) for i in range(0, lax.axis_size("ns"), 2)]
    return lax.ppermute(rows, "ns", pairs + [(b, a) for a, b in pairs])


def local(theta, velocity, diffusivity, land_mask, fold_partner, atm_flux, remap_src, remap_weights):
    levels, rows, cols = theta.shape
    fields = atm_flux.shape[2]
    shape = jax.ShapeDtypeStruct
    devices = lax.axis_size("ew") * lax.axis_size("ns")
    blocks = (devices, TILE, cols)
    room = 60 * 2**20 - 2 * max(0, 4 * devices * TILE * cols - 2**20)
    weights = remap_weights[0, 0]
    field, velocity, diffusivity, flux = bring(
        [theta, velocity, diffusivity, atm_flux[0, 0]], [pltpu.VMEM] * 4, room, "bring"
    )
    out, near = pl.pallas_call(
        first_kernel,
        out_shape=(pltpu.VMEM(blocks, BF16), pltpu.VMEM((KINDS, levels, cols), F32)),
        in_specs=[SMEM] + [VMEM] * 4,
        out_specs=(VMEM,) * 2,
        scratch_shapes=[pltpu.VMEM((2 * levels, TILE, cols), F32)],
        compiler_params=PARAMS,
        name="first",
    )(fold_partner, field, velocity, diffusivity, flux)
    first, near = exchange(out), swap(near)
    sources, weights = bring([remap_src[0], weights], [pltpu.SMEM, pltpu.VMEM], room, "load")
    points, columns, start = pl.pallas_call(
        side_kernel,
        out_shape=(
            pltpu.VMEM((5,) + theta.shape, F32), pltpu.VMEM((2, 3, cols), F32), pltpu.VMEM(theta.shape, F32),
        ),
        in_specs=[SMEM] + [VMEM] * 3,
        out_specs=(VMEM,) * 3,
        compiler_params=PARAMS,
        cost_estimate=pl.CostEstimate(flops=2**20, bytes_accessed=2**20, transcendentals=0),
        name="side",
    )(land_mask, field, velocity, diffusivity)
    total, force, after, ends, out = pl.pallas_call(
        middle_kernel,
        out_shape=(
            pltpu.VMEM((fields, rows * cols), F32), pltpu.VMEM((rows, cols), F32), pltpu.VMEM(theta.shape, F32),
            pltpu.VMEM((TILE, cols), F32), pltpu.VMEM(blocks, BF16),
        ),
        in_specs=[SMEM] * 3 + [VMEM] * 6,
        out_specs=(VMEM,) * 5,
        scratch_shapes=[pltpu.VMEM(theta.shape, F32)] * 2,
        compiler_params=PARAMS,
        name="middle",
    )(land_mask, fold_partner, sources, columns, points, start, weights, first, near)
    second = exchange(out)
    field, flux = pl.pallas_call(
        last_kernel,
        out_shape=(shape(theta.shape, F32), shape((fields, rows, cols), F32)),
        in_specs=[SMEM] + [VMEM] * 9,
        out_specs=(HBM, HBM),
        scratch_shapes=[
            pltpu.VMEM(theta.shape, F32), pltpu.VMEM((fields, rows, cols), F32), pltpu.VMEM(theta.shape, F32),
            pltpu.VMEM((levels, 3 * TILE, cols), F32), pltpu.VMEM((levels, TILE, cols), F32),
            pltpu.SemaphoreType.DMA((2,)),
        ],
        compiler_params=PARAMS,
        name="last",
    )(fold_partner, field, points, total, after, ends, force, first, second, near)
    return field, flux.reshape(1, 1, fields, rows * cols)


def solution(mesh):
    return jax.shard_map(
        local,
        mesh=mesh,
        in_specs=(
            P(None, "ns", "ew"),
            P(None, None, "ns", "ew"),
            P(None, "ns", "ew"),
            P("ns", "ew"),
            P("ew"),
            P("ns", "ew", None, None),
            P("ns", "ew", None),
            P("ns", "ew", None, None, None),
        ),
        out_specs=(P(None, "ns", "ew"), P("ns", "ew", None, None)),
        check_vma=False,
    )
```

```python
import functools

import jax
import jax.numpy as jnp
from jax import lax
from jax.experimental import pallas as pl
from jax.experimental.pallas import tpu as pltpu
from jax.sharding import PartitionSpec as P

COEFS = (0.5, -0.3, 0.2, 0.4, -0.25, 0.35)
VMEM = pl.BlockSpec(memory_space=pltpu.VMEM)
SMEM = pl.BlockSpec(memory_space=pltpu.SMEM)
HBM = pl.BlockSpec(memory_space=pltpu.HBM)
PARAMS = pltpu.CompilerParams(vmem_limit_bytes=16 * 1024 * 1024)
F32 = jnp.float32
BF16 = jnp.bfloat16
KINDS = 6
TILE = 8
FORCE_SLOT, WET_SLOT, PARTNER_SLOT = 4, 5, 4


def tendency(t, east, west, north, south, u, v, d):
    return d * (east + west + north + south - 4.0 * t) - 0.5 * (u * (east - west) + v * (north - south))


def stencil(t, *others):
    return t + tendency(t, *others)


class Place:
    def __init__(self):
        self.count, self.block_rows = lax.axis_size("ew"), lax.axis_size("ns")
        self.devices = self.count * self.block_rows
        self.e, self.n = lax.axis_index("ew"), lax.axis_index("ns")
        self.top = self.block_rows - 1
        self.is_top = self.n == self.top
        self.has_south = self.n > 0
        self.even = (self.n & 1) == 0
        self.east, self.west = self.wrap(self.e + 1), self.wrap(self.e + self.count - 1)
        self.above = jnp.minimum(self.n + 1, self.top)
        self.below = jnp.maximum(self.n - 1, 0)
        self.pair = jnp.where(self.even, self.n + 1, self.n - 1)
        self.other = jnp.where(self.even, self.below, self.above)

    def wrap(self, e):
        return jnp.where(e >= self.count, e - self.count, e)

    def slot(self, e, n):
        return n * self.count + e


def relays(row, block_rows):
    is_top = row == block_rows - 1
    odd = row & 1
    first = jnp.where((odd == 0) | is_top, jnp.maximum(row - 2, 0), row + 2)
    return first, jnp.where(is_top, jnp.maximum(row - 3, 0), row + 1 - 2 * odd), jnp.where(is_top, 0, 2)


def fill(size, rows):
    parts, at = [], 0
    for index in sorted(rows):
        if index > at:
            parts.append(jnp.zeros((index - at, size), F32))
        parts.append(rows[index])
        at = index + 1
    if at < size:
        parts.append(jnp.zeros((size - at, size), F32))
    return jnp.concatenate(parts, axis=0)


def turn(field):
    return field.reshape(field.shape[0] * field.shape[1], field.shape[2]).T


def row_of(ref, row):
    levels, rows, cols = ref.shape
    return ref.reshape(levels * rows, cols), pl.ds(row, levels, stride=rows)


def read_row(ref, row):
    flat, at = row_of(ref, row)
    return flat[at, :]


def write_row(ref, row, values):
    flat, at = row_of(ref, row)
    flat[at, :] = values


def shifted(field, axis, back):
    size = field.shape[axis]
    return pltpu.roll(field, size - 1 if back else 1, axis)


def bring_kernel(count, *refs):
    copies = [pltpu.make_async_copy(refs[i], refs[count + i], refs[-1].at[i]) for i in range(count)]
    for copy in copies:
        copy.start()
    for copy in copies:
        copy.wait()


def bring(arrays, memories, room, name):
    return pl.pallas_call(
        functools.partial(bring_kernel, len(arrays)),
        out_shape=tuple(memory(x.shape, x.dtype) for x, memory in zip(arrays, memories)),
        in_specs=[HBM] * len(arrays),
        out_specs=tuple(VMEM if memory is pltpu.VMEM else SMEM for memory in memories),
        scratch_shapes=[pltpu.SemaphoreType.DMA((len(arrays),))],
        compiler_params=pltpu.CompilerParams(vmem_limit_bytes=room),
        cost_estimate=pl.CostEstimate(flops=2**20, bytes_accessed=2**22, transcendentals=0),
        name=name,
    )(*arrays)


def first_kernel(partner_ref, theta_ref, vel_ref, diff_ref, atm_ref, out_ref, near_ref, bulk_ref):
    here = Place()
    levels, rows, cols = theta_ref.shape
    tiles = levels // TILE
    each = KINDS * tiles
    coef_refs = [vel_ref.at[0], vel_ref.at[1], diff_ref]
    turned = turn(theta_ref[...])
    strips = []
    for step in (1, -1):
        edge = rows - 1 if step < 0 else 0
        outer, t, inner = [read_row(theta_ref, edge + k * step) for k in range(3)]
        north, south = (outer, inner) if step < 0 else (inner, outer)
        coef = [read_row(ref, edge + step) for ref in coef_refs]
        tend = tendency(t, shifted(t, 1, True), shifted(t, 1, False), north, south, *coef)
        strips.append([outer, t, tend] + [read_row(ref, edge) for ref in coef_refs])
    for kind, (low, high) in enumerate(zip(*strips)):
        near_ref[kind] = jnp.where(here.even, high, low)
        far = jnp.where(here.even, low, high)
        bulk_ref[pl.ds(kind * tiles, tiles)] = far.reshape(tiles, TILE, cols)
    partner = partner_ref[0].astype(F32)
    fold_ref = bulk_ref.at[pl.ds(levels, levels)]
    for kind in range(KINDS):
        write_row(fold_ref, kind, strips[1][kind])
    write_row(fold_ref, KINDS, jnp.full((levels, cols), partner))
    write_row(fold_ref, KINDS + 1, jnp.zeros((levels, cols), F32))
    lane = lax.broadcasted_iota(jnp.int32, (TILE, cols), 1)
    slot = lane & 7
    spots = [turned[0:1], turned[1:2], turned[cols - 2 : cols - 1], turned[cols - 1 : cols]]
    spots = jnp.concatenate(spots + [jnp.zeros((TILE - 4, cols), F32)], axis=0)
    spots = jnp.where(here.even, spots, pltpu.roll(spots, cols - rows + 1, 1))
    corner = jnp.where(slot[0:1] == PARTNER_SLOT, partner, 0.0)
    for k in range(4):
        moved = pltpu.roll(spots, k, 1) if k else spots
        corner = jnp.where(slot[0:1] == k, moved[k : k + 1], corner)
    atm = atm_ref[...].astype(F32)
    to_west = jnp.concatenate([corner, turned[0:1], atm], axis=0)
    to_east = jnp.concatenate([corner, turned[cols - 1 : cols], atm], axis=0)
    column = jnp.where(here.is_top, partner_ref[0], here.e)
    first, second, skip = relays(jnp.where(here.is_top, here.top, here.other), here.block_rows)
    begin = jnp.where(here.is_top, levels, 0)
    for e in range(here.count):
        ahead = here.wrap(e - column + here.count)
        out_ref[here.slot(e, first)] = bulk_ref[begin + jnp.minimum(ahead, TILE - 1)].astype(BF16)
        out_ref[here.slot(e, second)] = bulk_ref[begin + jnp.minimum(ahead + TILE - skip, levels - 1)].astype(BF16)
    to_west, to_east = to_west.astype(BF16), to_east.astype(BF16)
    out_ref[here.slot(here.e, here.other)] = to_west
    for e in range(here.count):
        out_ref[here.slot(e, here.n)] = to_west
    out_ref[here.slot(here.east, here.n)] = to_east


def side_kernel(
    mask_ref, theta_ref, vel_ref, diff_ref, points_ref, columns_ref, start_ref
):
    levels, rows, cols = theta_ref.shape
    last = rows - 1
    wet = mask_ref[0, 0].astype(F32)
    u, v, d = wet * vel_ref[0], wet * vel_ref[1], wet * diff_ref[...]
    turned = [turn(u), turn(v), turn(d)]
    for side, at in enumerate((0, cols - 1)):
        for k in range(3):
            columns_ref[side, k : k + 1, :] = turned[k][at : at + 1]
    center, east, west, north, south = 1.0 - 4.0 * d, d - 0.5 * u, d + 0.5 * u, d - 0.5 * v, d + 0.5 * v
    for k, field in enumerate((center, east, west, north, south)):
        points_ref[k] = field
    t = theta_ref[...]
    lane = lax.broadcasted_iota(jnp.int32, t.shape, 2)
    line = lax.broadcasted_iota(jnp.int32, t.shape, 1)
    inner = center * t
    inner = inner + east * jnp.where(lane == cols - 1, 0.0, shifted(t, 2, True))
    inner = inner + west * jnp.where(lane == 0, 0.0, shifted(t, 2, False))
    inner = inner + north * jnp.where(line == last, 0.0, shifted(t, 1, True))
    inner = inner + south * jnp.where(line == 0, 0.0, shifted(t, 1, False))
    start_ref[...] = inner


def middle_kernel(
    mask_ref, partner_ref, src_ref, columns_ref, points_ref, start_ref, weights_ref, recv_ref, near_ref,
    total_ref, force_ref, next_ref, ends_ref, out_ref, beyond_ref, plain_ref,
):
    here = Place()
    levels, rows, cols = start_ref.shape
    fields = total_ref.shape[0]
    last = rows - 1
    wet = mask_ref[0, 0].astype(F32)

    pairs, cells, points = weights_ref.shape
    chosen = [recv_ref[here.slot(src_ref[0, pair], here.n)][TILE - fields :] for pair in range(pairs)]
    weights = weights_ref[...].reshape(pairs * cells, points)
    total = jnp.dot(jnp.concatenate(chosen, axis=1), weights, preferred_element_type=F32)
    total_ref[...] = total
    force = jnp.zeros((1, points), F32)
    for k in range(fields):
        force = force + COEFS[k] * total[k : k + 1]
    force = jnp.concatenate([force[:, r * cols : (r + 1) * cols] for r in range(rows)], axis=0)
    force = wet * (0.1 * force)
    force_ref[...] = force

    shape = start_ref.shape
    level = lax.broadcasted_iota(jnp.int32, shape, 0)

    def got(e, n):
        return recv_ref[here.slot(e, n)].astype(F32)

    sides = fill(cols, {0: got(here.west, here.n)[1:2], cols - 1: got(here.east, here.n)[1:2]}).T.reshape(shape)
    from_fold, over, under = got(partner_ref[0], here.n)[0:1], got(here.e, here.above)[0:1], got(here.e, here.below)[0:1]
    facing = jnp.where(here.is_top, from_fold, jnp.where(here.even, under, over))
    facing = jnp.broadcast_to(facing, (TILE, cols))
    facing = [facing[0:1]] + [pltpu.roll(facing, cols - k, 1)[0:1] for k in range(1, 4)]
    facing = [jnp.where(here.is_top, facing[3 - k], facing[k]) for k in range(4)]
    spots = (0, 1, cols - 2, cols - 1)
    beyond_ref[...] = fill(cols, dict(zip(spots, facing))).T.reshape(shape)
    far = read_row(beyond_ref, 0)
    above = jnp.where(here.even, near_ref[0], far)
    below = jnp.where(here.has_south, jnp.where(here.even, far, near_ref[0]), 0.0)
    lane = lax.broadcasted_iota(jnp.int32, shape, 2)
    rim = jnp.where(lane == cols - 1, points_ref[1], jnp.where(lane == 0, points_ref[2], 0.0))
    plain_ref[...] = start_ref[...] + rim * sides
    write_row(plain_ref, last, read_row(plain_ref, last) + read_row(points_ref.at[3], last) * above)
    write_row(plain_ref, 0, read_row(plain_ref, 0) + read_row(points_ref.at[4], 0) * below)
    t = plain_ref[...]
    next_ref[...] = t + jnp.where(level == 0, force[None], 0.0)

    held = [got(m, here.top) for m in range(here.count)]
    size = -(-here.count * TILE // cols) * cols
    tiles = held + [jnp.zeros((size - here.count * TILE, cols), F32)] * (size > here.count * TILE)
    tiles = jnp.concatenate(tiles, axis=0).astype(BF16)
    partners = jnp.concatenate([jnp.broadcast_to(block[KINDS : KINDS + 1, 0:1], (TILE, 1)) for block in held], axis=0)
    wanted = TILE * partners + (lax.broadcasted_iota(jnp.int32, partners.shape, 0) & (TILE - 1)).astype(F32)
    pick = lax.broadcasted_iota(jnp.int32, (here.count * TILE, size), 1).astype(F32) == wanted
    folded = jnp.dot(pick.astype(F32).astype(BF16), tiles, preferred_element_type=F32)

    turned = turn(t) + jnp.concatenate([force, jnp.zeros((cols - rows, cols), F32)], axis=0).T
    ends = jnp.concatenate([turned[0:1], turned[cols - 1 : cols], jnp.zeros((TILE - 2, cols), F32)], axis=0)
    lane = lax.broadcasted_iota(jnp.int32, (TILE, cols), 1)
    forces = jnp.concatenate([force, jnp.zeros((cols - rows, cols), F32)], axis=0).T
    forces = jnp.concatenate([forces[0:1], forces[cols - 1 : cols], jnp.zeros((TILE - 2, cols), F32)], axis=0)
    ends_ref[...] = ends
    marks = jnp.take_along_axis(forces, lane >> 3, axis=1)
    slot = lane & 7
    marks = jnp.where(slot == FORCE_SLOT, marks, jnp.where(slot == WET_SLOT, wet, 0.0))
    slot = slot[0:1]

    def corners(shifts, mark):
        row = mark
        for index, shift in enumerate(shifts):
            moved = pltpu.roll(ends, shift % cols, 1) if shift else ends
            row = jnp.where(slot == index, moved[index // 2 : index // 2 + 1], row)
        return row

    up, down = (-last, 2 - last, 2 - last, 4 - last), (0, 0, 2, 2)
    low_mark, high_mark = marks[0:1], marks[1:2]
    low_coef, high_coef = columns_ref[0], columns_ref[1]
    high_force, low_force = [force[last : last + 1], force[last - 1 : last]], [force[0:1], force[1:2]]
    low, high = [turned[0:1], turned[1:2]], [turned[cols - 1 : cols], turned[cols - 2 : cols - 1]]
    base = jnp.concatenate([corners(up, low_mark)] + high_force + low + [low_coef], axis=0)
    to_east = jnp.concatenate([corners(up, high_mark)] + high_force + high + [high_coef], axis=0)
    to_below = jnp.concatenate([corners(down, low_mark)] + low_force + low + [low_coef], axis=0)
    for e in range(here.count):
        close = (e == here.e) | (e == here.east) | (e == here.west)
        for n in range(here.block_rows):
            begin = jnp.where(n == here.n - 1, to_below, jnp.where(e == here.east, to_east, base))
            owed = (n == here.n) | (close & ((n == here.n - 1) | (n == here.n + 1)))
            if n == here.top:
                tile = folded[e * TILE : (e + 1) * TILE]
            else:
                tile = got(e, max(n - 1, 0) if n % 2 == 0 else n + 1)
            out_ref[n * here.count + e] = jnp.where(owed, begin, tile).astype(BF16)


def last_kernel(
    partner_ref, theta_ref, points_ref, total_ref, next_ref, ends_ref, force_ref, first_ref, second_ref, near_ref,
    result_hbm, flux_hbm, result_ref, flux_ref, rim_ref, tall_ref, tile_ref, sems,
):
    here = Place()
    levels, rows, cols = theta_ref.shape
    last = rows - 1
    for k in range(flux_ref.shape[0]):
        for r in range(rows):
            flux_ref[k, r : r + 1, :] = total_ref[k : k + 1, r * cols : (r + 1) * cols]
    copies = [
        pltpu.make_async_copy(flux_ref, flux_hbm, sems.at[0]), pltpu.make_async_copy(result_ref, result_hbm, sems.at[1])
    ]
    copies[0].start()
    partner = partner_ref[0]
    is_top, has_south = here.is_top, here.has_south

    def got(e, n):
        return second_ref[here.slot(e, n)].astype(F32)

    west, east = got(here.west, here.n), got(here.east, here.n)
    over, under = got(here.e, here.above), got(here.e, here.below)
    fold = got(partner, here.n)
    fold_east = got(here.wrap(partner + 1), here.n)[0:1]
    fold_west = got(here.wrap(partner + here.count - 1), here.n)[0:1]
    over_west, over_east = got(here.west, here.above)[0:1], got(here.east, here.above)[0:1]
    under_west, under_east = got(here.west, here.below)[0:1], got(here.east, here.below)[0:1]
    first_west = first_ref[here.slot(here.west, here.n)].astype(F32)
    first_east = first_ref[here.slot(here.east, here.n)].astype(F32)

    def mark(block):
        return block[0:1, WET_SLOT : WET_SLOT + 1]

    first, second, skip = relays(here.n, here.block_rows)
    for k in range(levels):
        ahead, row = (k, first) if k < TILE else (k - TILE + skip, second)
        tile_ref[k] = got(here.wrap(here.e + jnp.minimum(ahead, here.count - 1)), row)
    tiles = levels // TILE
    far = [tile_ref[pl.ds(kind * tiles, tiles)].reshape(levels, cols) for kind in range(KINDS)]
    far = jnp.concatenate(far, axis=0)
    mirrored = jnp.concatenate([read_row(tile_ref, kind) for kind in range(KINDS)], axis=0)
    mirror = cols - 1 - lax.broadcasted_iota(jnp.int32, far.shape, 1)
    far = jnp.where(is_top, jnp.take_along_axis(mirrored, mirror, axis=1), far)
    far = [far[kind * levels : (kind + 1) * levels] for kind in range(KINDS)]
    near = [near_ref[kind] for kind in range(KINDS)]
    north = [jnp.where(here.even, a, b) for a, b in zip(near, far)]
    south = [jnp.where(has_south, jnp.where(here.even, b, a), 0.0) for a, b in zip(near, far)]

    def kinds(strip, wet, sign):
        t, inner, tend, u, v, d = strip
        return t, inner, inner + wet * tend, (sign * wet) * u, (sign * wet) * v, wet * d

    north = kinds(north, jnp.where(is_top, mark(fold), mark(over)), jnp.where(is_top, -1.0, 1.0))
    south = kinds(south, mark(under), 1.0)

    top_west, top_east = jnp.zeros((1, cols), F32), jnp.zeros((1, cols), F32)
    for s in range(here.count):
        row = got(s, here.n)[0:1]
        top_west = jnp.where(first_west[0:1, PARTNER_SLOT : PARTNER_SLOT + 1] == float(s), row, top_west)
        top_east = jnp.where(first_east[0:1, PARTNER_SLOT : PARTNER_SLOT + 1] == float(s), row, top_east)
    moved = [fold[0:1], over[0:1], under[0:1], fold_west, over_west, under_west, top_east]
    moved = jnp.concatenate(moved + [jnp.zeros((1, cols), F32)], axis=0)
    moved = pltpu.roll(moved, cols - 2, 1)
    def pair(low, high):
        return jnp.concatenate([low, high, jnp.zeros((TILE - 2, cols), F32)], axis=0)

    along = lax.broadcasted_iota(jnp.int32, (TILE, cols), 1)
    place = along & 7
    side = pair(west[3:4], east[3:4])
    corner = pair(jnp.where(is_top, top_west, moved[4:5]), jnp.where(is_top, moved[6:7], over_east))
    side_north = jnp.where(place == last, pltpu.roll(corner, last, 1), shifted(side, 1, True))
    corner = jnp.where(has_south, pair(moved[5:6], under_east), 0.0)
    side_south = jnp.where(place == 0, corner, shifted(side, 1, False))
    side_force = jnp.take_along_axis(pair(west[0:1], east[0:1]), jnp.where(along < rows, 8 * along, 0) + FORCE_SLOT, axis=1)
    side_next = stencil(
        side, pair(ends_ref[0:1], east[4:5]), pair(west[4:5], ends_ref[1:2]), side_north, side_south,
        *[pair(west[k : k + 1], east[k : k + 1]) for k in (5, 6, 7)],
    ) + jnp.where(along < rows, side_force, 0.0)

    listed = [
        (west[3:4], east[3:4]),
        (side_next[0:1], side_next[1:2]),
        (jnp.where(is_top, moved[0:1], over[0:1]), jnp.where(is_top, fold[0:1], moved[1:2])),
        (under[0:1], moved[2:3]),
        (jnp.where(is_top, fold_east, moved[4:5]), jnp.where(is_top, moved[3:4], over_east)),
        (moved[5:6], under_east),
    ]
    lanes = {}
    for q, (low, high) in enumerate(listed):
        lanes[2 * q], lanes[(2 * q - 1) % cols] = low, high
    rim = fill(cols, lanes).T.reshape(theta_ref.shape)
    rim_ref[...] = rim

    def listing(q, field):
        return pltpu.roll(field, cols - 2 * q, field.ndim - 1) if q else field

    edges, inners = read_row(rim_ref, 0), read_row(rim_ref, 1)
    lane = lax.broadcasted_iota(jnp.int32, (levels, cols), 1)
    level = lax.broadcasted_iota(jnp.int32, (levels, cols), 0)
    ends = (lane == 0) | (lane == cols - 1)

    def forced(row, force):
        return row + jnp.where(level == 0, force, 0.0)

    flip = cols - 1 - lax.broadcasted_iota(jnp.int32, (8, cols), 1)
    flipped = jnp.take_along_axis(fold[:TILE], flip, axis=1)
    north_force = [jnp.where(is_top, flipped[k : k + 1], over[k : k + 1]) for k in (1, 2)]
    south_force = [under[1:2], under[2:3]]

    def beyond(rows_of, inside, outward, force, q):
        edge_row = stencil(
            rows_of[0], shifted(rows_of[0], 1, True), shifted(rows_of[0], 1, False),
            rows_of[1] if outward else inside, inside if outward else rows_of[1], *rows_of[3:],
        )
        edge_row = jnp.where(ends, listing(q, edges), forced(edge_row, force[0]))
        return edge_row, jnp.where(ends, listing(q, inners), forced(rows_of[2], force[1]))

    north_one, north_two = beyond(north, read_row(theta_ref, last), True, north_force, 2)
    south_one, south_two = beyond(south, read_row(theta_ref, 0), False, south_force, 3)
    south_one, south_two = jnp.where(has_south, south_one, 0.0), jnp.where(has_south, south_two, 0.0)
    shape = theta_ref.shape
    wide = lax.broadcasted_iota(jnp.int32, shape, 2)
    force = jnp.where(lax.broadcasted_iota(jnp.int32, shape, 0) == 0, force_ref[...][None], 0.0)
    inside = (lane >= 2) & (lane < cols - 2)
    more_north, more_south = inside & jnp.logical_not(here.even), inside & here.even
    top_row = read_row(next_ref, last) + jnp.where(more_north, read_row(points_ref.at[3], last) * north[0], 0.0)
    bottom_row = read_row(next_ref, 0) + jnp.where(more_south, read_row(points_ref.at[4], 0) * south[0], 0.0)
    tall_ref[:, TILE : 2 * TILE, :] = next_ref[...]
    write_row(tall_ref, TILE + last, top_row)
    write_row(tall_ref, TILE, bottom_row)

    def outer(row, further, inside, outward, rows_of, force_row, diagonal):
        result = stencil(
            row, jnp.where(lane == cols - 1, diagonal, shifted(row, 1, True)),
            jnp.where(lane == 0, diagonal, shifted(row, 1, False)),
            further if outward else inside, inside if outward else further, *rows_of[3:],
        )
        return forced(result, force_row)

    north_next = outer(north_one, north_two, top_row, True, north, north_force[0], listing(4, edges))
    south_next = outer(south_one, south_two, bottom_row, False, south, south_force[0], listing(5, edges))
    south_next = jnp.where(has_south, south_next, 0.0)

    def advance(sides, above, below):
        write_row(tall_ref, 2 * TILE, above)
        write_row(tall_ref, TILE - 1, below)
        t = tall_ref[:, TILE : 2 * TILE, :]
        east = jnp.where(wide == cols - 1, sides, shifted(t, 2, True))
        west = jnp.where(wide == 0, sides, shifted(t, 2, False))
        north, south = tall_ref[:, TILE + 1 : 2 * TILE + 1, :], tall_ref[:, TILE - 1 : 2 * TILE - 1, :]
        result = force
        for k, field in enumerate((t, east, west, north, south)):
            result = result + points_ref[k] * field
        return result

    tall_ref[:, TILE : 2 * TILE, :] = advance(rim, north_one, south_one)
    result_ref[...] = advance(listing(1, rim), north_next, south_next)
    copies[1].start()
    for copy in copies:
        copy.wait()


def exchange(blocks):
    return lax.all_to_all(blocks, ("ns", "ew"), split_axis=0, concat_axis=0, tiled=True)


def swap(rows):
    pairs = [(i, i + 1) for i in range(0, lax.axis_size("ns"), 2)]
    return lax.ppermute(rows, "ns", pairs + [(b, a) for a, b in pairs])


def local(theta, velocity, diffusivity, land_mask, fold_partner, atm_flux, remap_src, remap_weights):
    levels, rows, cols = theta.shape
    fields = atm_flux.shape[2]
    shape = jax.ShapeDtypeStruct
    devices = lax.axis_size("ew") * lax.axis_size("ns")
    blocks = (devices, TILE, cols)
    room = 60 * 2**20 - 2 * max(0, 4 * devices * TILE * cols - 2**20)
    weights = remap_weights[0, 0]
    field, velocity, diffusivity, flux = bring(
        [theta, velocity, diffusivity, atm_flux[0, 0]], [pltpu.VMEM] * 4, room, "bring"
    )
    out, near = pl.pallas_call(
        first_kernel,
        out_shape=(pltpu.VMEM(blocks, BF16), pltpu.VMEM((KINDS, levels, cols), F32)),
        in_specs=[SMEM] + [VMEM] * 4,
        out_specs=(VMEM,) * 2,
        scratch_shapes=[pltpu.VMEM((2 * levels, TILE, cols), F32)],
        compiler_params=PARAMS,
        name="first",
    )(fold_partner, field, velocity, diffusivity, flux)
    first, near = exchange(out), swap(near)
    sources, weights = bring([remap_src[0], weights], [pltpu.SMEM, pltpu.VMEM], room, "load")
    points, columns, start = pl.pallas_call(
        side_kernel,
        out_shape=(
            pltpu.VMEM((5,) + theta.shape, F32), pltpu.VMEM((2, 3, cols), F32), pltpu.VMEM(theta.shape, F32),
        ),
        in_specs=[SMEM] + [VMEM] * 3,
        out_specs=(VMEM,) * 3,
        compiler_params=PARAMS,
        cost_estimate=pl.CostEstimate(flops=2**20, bytes_accessed=2**20, transcendentals=0),
        name="side",
    )(land_mask, field, velocity, diffusivity)
    total, force, after, ends, out = pl.pallas_call(
        middle_kernel,
        out_shape=(
            pltpu.VMEM((fields, rows * cols), F32), pltpu.VMEM((rows, cols), F32), pltpu.VMEM(theta.shape, F32),
            pltpu.VMEM((TILE, cols), F32), pltpu.VMEM(blocks, BF16),
        ),
        in_specs=[SMEM] * 3 + [VMEM] * 6,
        out_specs=(VMEM,) * 5,
        scratch_shapes=[pltpu.VMEM(theta.shape, F32)] * 2,
        compiler_params=PARAMS,
        name="middle",
    )(land_mask, fold_partner, sources, columns, points, start, weights, first, near)
    second = exchange(out)
    field, flux = pl.pallas_call(
        last_kernel,
        out_shape=(shape(theta.shape, F32), shape((fields, rows, cols), F32)),
        in_specs=[SMEM] + [VMEM] * 9,
        out_specs=(HBM, HBM),
        scratch_shapes=[
            pltpu.VMEM(theta.shape, F32), pltpu.VMEM((fields, rows, cols), F32), pltpu.VMEM(theta.shape, F32),
            pltpu.VMEM((levels, 3 * TILE, cols), F32), pltpu.VMEM((levels, TILE, cols), F32),
            pltpu.SemaphoreType.DMA((2,)),
        ],
        compiler_params=PARAMS,
        name="last",
    )(fold_partner, field, points, total, after, ends, force, first, second, near)
    return field, flux.reshape(1, 1, fields, rows * cols)


def solution(mesh):
    return jax.shard_map(
        local,
        mesh=mesh,
        in_specs=(
            P(None, "ns", "ew"),
            P(None, None, "ns", "ew"),
            P(None, "ns", "ew"),
            P("ns", "ew"),
            P("ew"),
            P("ns", "ew", None, None),
            P("ns", "ew", None),
            P("ns", "ew", None, None, None),
        ),
        out_specs=(P(None, "ns", "ew"), P("ns", "ew", None, None)),
        check_vma=False,
    )
```

```python
import functools

import jax
import jax.numpy as jnp
from jax import lax
from jax.experimental import pallas as pl
from jax.experimental.pallas import tpu as pltpu
from jax.sharding import PartitionSpec as P

COEFS = (0.5, -0.3, 0.2, 0.4, -0.25, 0.35)
VMEM = pl.BlockSpec(memory_space=pltpu.VMEM)
SMEM = pl.BlockSpec(memory_space=pltpu.SMEM)
HBM = pl.BlockSpec(memory_space=pltpu.HBM)
PARAMS = pltpu.CompilerParams(vmem_limit_bytes=16 * 1024 * 1024)
F32 = jnp.float32
BF16 = jnp.bfloat16
KINDS = 6
TILE = 8
FORCE_SLOT, WET_SLOT, PARTNER_SLOT = 4, 5, 4


def tendency(t, east, west, north, south, u, v, d):
    return d * (east + west + north + south - 4.0 * t) - 0.5 * (u * (east - west) + v * (north - south))


def stencil(t, *others):
    return t + tendency(t, *others)


class Place:
    def __init__(self):
        self.count, self.block_rows = lax.axis_size("ew"), lax.axis_size("ns")
        self.devices = self.count * self.block_rows
        self.e, self.n = lax.axis_index("ew"), lax.axis_index("ns")
        self.top = self.block_rows - 1
        self.is_top = self.n == self.top
        self.has_south = self.n > 0
        self.even = (self.n & 1) == 0
        self.east, self.west = self.wrap(self.e + 1), self.wrap(self.e + self.count - 1)
        self.above = jnp.minimum(self.n + 1, self.top)
        self.below = jnp.maximum(self.n - 1, 0)
        self.pair = jnp.where(self.even, self.n + 1, self.n - 1)
        self.other = jnp.where(self.even, self.below, self.above)

    def wrap(self, e):
        return jnp.where(e >= self.count, e - self.count, e)

    def slot(self, e, n):
        return n * self.count + e


def relays(row, block_rows):
    is_top = row == block_rows - 1
    odd = row & 1
    first = jnp.where((odd == 0) | is_top, jnp.maximum(row - 2, 0), row + 2)
    return first, jnp.where(is_top, jnp.maximum(row - 3, 0), row + 1 - 2 * odd), jnp.where(is_top, 0, 2)


def fill(size, rows):
    parts, at = [], 0
    for index in sorted(rows):
        if index > at:
            parts.append(jnp.zeros((index - at, size), F32))
        parts.append(rows[index])
        at = index + 1
    if at < size:
        parts.append(jnp.zeros((size - at, size), F32))
    return jnp.concatenate(parts, axis=0)


def turn(field):
    return field.reshape(field.shape[0] * field.shape[1], field.shape[2]).T


def row_of(ref, row):
    levels, rows, cols = ref.shape
    return ref.reshape(levels * rows, cols), pl.ds(row, levels, stride=rows)


def read_row(ref, row):
    flat, at = row_of(ref, row)
    return flat[at, :]


def write_row(ref, row, values):
    flat, at = row_of(ref, row)
    flat[at, :] = values


def shifted(field, axis, back):
    size = field.shape[axis]
    return pltpu.roll(field, size - 1 if back else 1, axis)


def bring_kernel(count, skip, *refs):
    copies = [pltpu.make_async_copy(refs[i], refs[count + skip + i], refs[-1].at[i]) for i in range(count)]
    for copy in copies:
        copy.start()
    for copy in copies:
        copy.wait()


def bring(arrays, memories, room, name, after=()):
    return pl.pallas_call(
        functools.partial(bring_kernel, len(arrays), len(after)),
        out_shape=tuple(memory(x.shape, x.dtype) for x, memory in zip(arrays, memories)),
        in_specs=[HBM] * len(arrays) + [pl.BlockSpec(memory_space=pl.ANY)] * len(after),
        out_specs=tuple(VMEM if memory is pltpu.VMEM else SMEM for memory in memories),
        scratch_shapes=[pltpu.SemaphoreType.DMA((len(arrays),))],
        compiler_params=pltpu.CompilerParams(vmem_limit_bytes=room),
        cost_estimate=pl.CostEstimate(flops=2**20, bytes_accessed=2**22, transcendentals=0),
        name=name,
    )(*arrays, *after)


def first_kernel(
    partner_ref, theta_ref, vel_ref, diff_ref, atm_ref, out_ref, near_ref, number_ref, token_ref, bulk_ref
):
    here = Place()
    partner = jnp.max(partner_ref[...].astype(F32))
    partner_column = partner.astype(jnp.int32)
    number_ref[0] = partner_column
    token_ref[...] = jnp.zeros(token_ref.shape, F32)
    levels, rows, cols = theta_ref.shape
    tiles = levels // TILE
    each = KINDS * tiles
    coef_refs = [vel_ref.at[0], vel_ref.at[1], diff_ref]
    turned = turn(theta_ref[...])
    strips = []
    for step in (1, -1):
        edge = rows - 1 if step < 0 else 0
        outer, t, inner = [read_row(theta_ref, edge + k * step) for k in range(3)]
        north, south = (outer, inner) if step < 0 else (inner, outer)
        coef = [read_row(ref, edge + step) for ref in coef_refs]
        tend = tendency(t, shifted(t, 1, True), shifted(t, 1, False), north, south, *coef)
        strips.append([outer, t, tend] + [read_row(ref, edge) for ref in coef_refs])
    for kind, (low, high) in enumerate(zip(*strips)):
        near_ref[kind] = jnp.where(here.even, high, low)
        far = jnp.where(here.even, low, high)
        bulk_ref[pl.ds(kind * tiles, tiles)] = far.reshape(tiles, TILE, cols)
    fold_ref = bulk_ref.at[pl.ds(levels, levels)]
    for kind in range(KINDS):
        write_row(fold_ref, kind, strips[1][kind])
    write_row(fold_ref, KINDS, jnp.full((levels, cols), partner))
    write_row(fold_ref, KINDS + 1, jnp.zeros((levels, cols), F32))
    lane = lax.broadcasted_iota(jnp.int32, (TILE, cols), 1)
    slot = lane & 7
    spots = [turned[0:1], turned[1:2], turned[cols - 2 : cols - 1], turned[cols - 1 : cols]]
    spots = jnp.concatenate(spots + [jnp.zeros((TILE - 4, cols), F32)], axis=0)
    spots = jnp.where(here.even, spots, pltpu.roll(spots, cols - rows + 1, 1))
    corner = jnp.where(slot[0:1] == PARTNER_SLOT, partner, 0.0)
    for k in range(4):
        moved = pltpu.roll(spots, k, 1) if k else spots
        corner = jnp.where(slot[0:1] == k, moved[k : k + 1], corner)
    atm = atm_ref[...].astype(F32)
    to_west = jnp.concatenate([corner, turned[0:1], atm], axis=0)
    to_east = jnp.concatenate([corner, turned[cols - 1 : cols], atm], axis=0)
    column = jnp.where(here.is_top, partner_column, here.e)
    first, second, skip = relays(jnp.where(here.is_top, here.top, here.other), here.block_rows)
    begin = jnp.where(here.is_top, levels, 0)
    for e in range(here.count):
        ahead = here.wrap(e - column + here.count)
        out_ref[here.slot(e, first)] = bulk_ref[begin + jnp.minimum(ahead, TILE - 1)].astype(BF16)
        out_ref[here.slot(e, second)] = bulk_ref[begin + jnp.minimum(ahead + TILE - skip, levels - 1)].astype(BF16)
    to_west, to_east = to_west.astype(BF16), to_east.astype(BF16)
    out_ref[here.slot(here.e, here.other)] = to_west
    for e in range(here.count):
        out_ref[here.slot(e, here.n)] = to_west
    out_ref[here.slot(here.east, here.n)] = to_east


def side_kernel(
    mask_ref, theta_ref, vel_ref, diff_ref, _, points_ref, columns_ref, start_ref
):
    levels, rows, cols = theta_ref.shape
    last = rows - 1
    wet = mask_ref[0, 0].astype(F32)
    u, v, d = wet * vel_ref[0], wet * vel_ref[1], wet * diff_ref[...]
    turned = [turn(u), turn(v), turn(d)]
    for side, at in enumerate((0, cols - 1)):
        for k in range(3):
            columns_ref[side, k : k + 1, :] = turned[k][at : at + 1]
    center, east, west, north, south = 1.0 - 4.0 * d, d - 0.5 * u, d + 0.5 * u, d - 0.5 * v, d + 0.5 * v
    for k, field in enumerate((center, east, west, north, south)):
        points_ref[k] = field
    t = theta_ref[...]
    lane = lax.broadcasted_iota(jnp.int32, t.shape, 2)
    line = lax.broadcasted_iota(jnp.int32, t.shape, 1)
    inner = center * t
    inner = inner + east * jnp.where(lane == cols - 1, 0.0, shifted(t, 2, True))
    inner = inner + west * jnp.where(lane == 0, 0.0, shifted(t, 2, False))
    inner = inner + north * jnp.where(line == last, 0.0, shifted(t, 1, True))
    inner = inner + south * jnp.where(line == 0, 0.0, shifted(t, 1, False))
    start_ref[...] = inner


def middle_kernel(
    mask_ref, partner_ref, src_ref, columns_ref, points_ref, start_ref, weights_ref, recv_ref, near_ref,
    total_ref, force_ref, next_ref, ends_ref, out_ref, beyond_ref, plain_ref,
):
    here = Place()
    levels, rows, cols = start_ref.shape
    fields = total_ref.shape[0]
    last = rows - 1
    wet = mask_ref[0, 0].astype(F32)

    pairs, cells, points = weights_ref.shape
    chosen = [recv_ref[here.slot(src_ref[0, pair], here.n)][TILE - fields :] for pair in range(pairs)]
    weights = weights_ref[...].reshape(pairs * cells, points)
    total = jnp.dot(jnp.concatenate(chosen, axis=1), weights, preferred_element_type=F32)
    total_ref[...] = total
    force = jnp.zeros((1, points), F32)
    for k in range(fields):
        force = force + COEFS[k] * total[k : k + 1]
    force = jnp.concatenate([force[:, r * cols : (r + 1) * cols] for r in range(rows)], axis=0)
    force = wet * (0.1 * force)
    force_ref[...] = force

    shape = start_ref.shape
    level = lax.broadcasted_iota(jnp.int32, shape, 0)

    def got(e, n):
        return recv_ref[here.slot(e, n)].astype(F32)

    sides = fill(cols, {0: got(here.west, here.n)[1:2], cols - 1: got(here.east, here.n)[1:2]}).T.reshape(shape)
    from_fold, over, under = got(partner_ref[0], here.n)[0:1], got(here.e, here.above)[0:1], got(here.e, here.below)[0:1]
    facing = jnp.where(here.is_top, from_fold, jnp.where(here.even, under, over))
    facing = jnp.broadcast_to(facing, (TILE, cols))
    facing = [facing[0:1]] + [pltpu.roll(facing, cols - k, 1)[0:1] for k in range(1, 4)]
    facing = [jnp.where(here.is_top, facing[3 - k], facing[k]) for k in range(4)]
    spots = (0, 1, cols - 2, cols - 1)
    beyond_ref[...] = fill(cols, dict(zip(spots, facing))).T.reshape(shape)
    far = read_row(beyond_ref, 0)
    above = jnp.where(here.even, near_ref[0], far)
    below = jnp.where(here.has_south, jnp.where(here.even, far, near_ref[0]), 0.0)
    lane = lax.broadcasted_iota(jnp.int32, shape, 2)
    rim = jnp.where(lane == cols - 1, points_ref[1], jnp.where(lane == 0, points_ref[2], 0.0))
    plain_ref[...] = start_ref[...] + rim * sides
    write_row(plain_ref, last, read_row(plain_ref, last) + read_row(points_ref.at[3], last) * above)
    write_row(plain_ref, 0, read_row(plain_ref, 0) + read_row(points_ref.at[4], 0) * below)
    t = plain_ref[...]
    next_ref[...] = t + jnp.where(level == 0, force[None], 0.0)

    held = [got(m, here.top) for m in range(here.count)]
    size = -(-here.count * TILE // cols) * cols
    tiles = held + [jnp.zeros((size - here.count * TILE, cols), F32)] * (size > here.count * TILE)
    tiles = jnp.concatenate(tiles, axis=0).astype(BF16)
    partners = jnp.concatenate([jnp.broadcast_to(block[KINDS : KINDS + 1, 0:1], (TILE, 1)) for block in held], axis=0)
    wanted = TILE * partners + (lax.broadcasted_iota(jnp.int32, partners.shape, 0) & (TILE - 1)).astype(F32)
    pick = lax.broadcasted_iota(jnp.int32, (here.count * TILE, size), 1).astype(F32) == wanted
    folded = jnp.dot(pick.astype(F32).astype(BF16), tiles, preferred_element_type=F32)

    turned = turn(t) + jnp.concatenate([force, jnp.zeros((cols - rows, cols), F32)], axis=0).T
    ends = jnp.concatenate([turned[0:1], turned[cols - 1 : cols], jnp.zeros((TILE - 2, cols), F32)], axis=0)
    lane = lax.broadcasted_iota(jnp.int32, (TILE, cols), 1)
    forces = jnp.concatenate([force, jnp.zeros((cols - rows, cols), F32)], axis=0).T
    forces = jnp.concatenate([forces[0:1], forces[cols - 1 : cols], jnp.zeros((TILE - 2, cols), F32)], axis=0)
    ends_ref[...] = ends
    marks = jnp.take_along_axis(forces, lane >> 3, axis=1)
    slot = lane & 7
    marks = jnp.where(slot == FORCE_SLOT, marks, jnp.where(slot == WET_SLOT, wet, 0.0))
    slot = slot[0:1]

    def corners(shifts, mark):
        row = mark
        for index, shift in enumerate(shifts):
            moved = pltpu.roll(ends, shift % cols, 1) if shift else ends
            row = jnp.where(slot == index, moved[index // 2 : index // 2 + 1], row)
        return row

    up, down = (-last, 2 - last, 2 - last, 4 - last), (0, 0, 2, 2)
    low_mark, high_mark = marks[0:1], marks[1:2]
    low_coef, high_coef = columns_ref[0], columns_ref[1]
    high_force, low_force = [force[last : last + 1], force[last - 1 : last]], [force[0:1], force[1:2]]
    low, high = [turned[0:1], turned[1:2]], [turned[cols - 1 : cols], turned[cols - 2 : cols - 1]]
    base = jnp.concatenate([corners(up, low_mark)] + high_force + low + [low_coef], axis=0)
    to_east = jnp.concatenate([corners(up, high_mark)] + high_force + high + [high_coef], axis=0)
    to_below = jnp.concatenate([corners(down, low_mark)] + low_force + low + [low_coef], axis=0)
    for e in range(here.count):
        close = (e == here.e) | (e == here.east) | (e == here.west)
        for n in range(here.block_rows):
            begin = jnp.where(n == here.n - 1, to_below, jnp.where(e == here.east, to_east, base))
            owed = (n == here.n) | (close & ((n == here.n - 1) | (n == here.n + 1)))
            if n == here.top:
                tile = folded[e * TILE : (e + 1) * TILE]
            else:
                tile = got(e, max(n - 1, 0) if n % 2 == 0 else n + 1)
            out_ref[n * here.count + e] = jnp.where(owed, begin, tile).astype(BF16)


def last_kernel(
    partner_ref, theta_ref, points_ref, total_ref, next_ref, ends_ref, force_ref, first_ref, second_ref, near_ref,
    result_hbm, flux_hbm, result_ref, flux_ref, rim_ref, tall_ref, tile_ref, sems,
):
    here = Place()
    levels, rows, cols = theta_ref.shape
    last = rows - 1
    for k in range(flux_ref.shape[0]):
        for r in range(rows):
            flux_ref[k, r : r + 1, :] = total_ref[k : k + 1, r * cols : (r + 1) * cols]
    copies = [
        pltpu.make_async_copy(flux_ref, flux_hbm, sems.at[0]), pltpu.make_async_copy(result_ref, result_hbm, sems.at[1])
    ]
    copies[0].start()
    partner = partner_ref[0]
    is_top, has_south = here.is_top, here.has_south

    def got(e, n):
        return second_ref[here.slot(e, n)].astype(F32)

    west, east = got(here.west, here.n), got(here.east, here.n)
    over, under = got(here.e, here.above), got(here.e, here.below)
    fold = got(partner, here.n)
    fold_east = got(here.wrap(partner + 1), here.n)[0:1]
    fold_west = got(here.wrap(partner + here.count - 1), here.n)[0:1]
    over_west, over_east = got(here.west, here.above)[0:1], got(here.east, here.above)[0:1]
    under_west, under_east = got(here.west, here.below)[0:1], got(here.east, here.below)[0:1]
    first_west = first_ref[here.slot(here.west, here.n)].astype(F32)
    first_east = first_ref[here.slot(here.east, here.n)].astype(F32)

    def mark(block):
        return block[0:1, WET_SLOT : WET_SLOT + 1]

    first, second, skip = relays(here.n, here.block_rows)
    for k in range(levels):
        ahead, row = (k, first) if k < TILE else (k - TILE + skip, second)
        tile_ref[k] = got(here.wrap(here.e + jnp.minimum(ahead, here.count - 1)), row)
    tiles = levels // TILE
    far = [tile_ref[pl.ds(kind * tiles, tiles)].reshape(levels, cols) for kind in range(KINDS)]
    far = jnp.concatenate(far, axis=0)
    mirrored = jnp.concatenate([read_row(tile_ref, kind) for kind in range(KINDS)], axis=0)
    mirror = cols - 1 - lax.broadcasted_iota(jnp.int32, far.shape, 1)
    far = jnp.where(is_top, jnp.take_along_axis(mirrored, mirror, axis=1), far)
    far = [far[kind * levels : (kind + 1) * levels] for kind in range(KINDS)]
    near = [near_ref[kind] for kind in range(KINDS)]
    north = [jnp.where(here.even, a, b) for a, b in zip(near, far)]
    south = [jnp.where(has_south, jnp.where(here.even, b, a), 0.0) for a, b in zip(near, far)]

    def kinds(strip, wet, sign):
        t, inner, tend, u, v, d = strip
        return t, inner, inner + wet * tend, (sign * wet) * u, (sign * wet) * v, wet * d

    north = kinds(north, jnp.where(is_top, mark(fold), mark(over)), jnp.where(is_top, -1.0, 1.0))
    south = kinds(south, mark(under), 1.0)

    top_west, top_east = jnp.zeros((1, cols), F32), jnp.zeros((1, cols), F32)
    for s in range(here.count):
        row = got(s, here.n)[0:1]
        top_west = jnp.where(first_west[0:1, PARTNER_SLOT : PARTNER_SLOT + 1] == float(s), row, top_west)
        top_east = jnp.where(first_east[0:1, PARTNER_SLOT : PARTNER_SLOT + 1] == float(s), row, top_east)
    moved = [fold[0:1], over[0:1], under[0:1], fold_west, over_west, under_west, top_east]
    moved = jnp.concatenate(moved + [jnp.zeros((1, cols), F32)], axis=0)
    moved = pltpu.roll(moved, cols - 2, 1)
    def pair(low, high):
        return jnp.concatenate([low, high, jnp.zeros((TILE - 2, cols), F32)], axis=0)

    along = lax.broadcasted_iota(jnp.int32, (TILE, cols), 1)
    place = along & 7
    side = pair(west[3:4], east[3:4])
    corner = pair(jnp.where(is_top, top_west, moved[4:5]), jnp.where(is_top, moved[6:7], over_east))
    side_north = jnp.where(place == last, pltpu.roll(corner, last, 1), shifted(side, 1, True))
    corner = jnp.where(has_south, pair(moved[5:6], under_east), 0.0)
    side_south = jnp.where(place == 0, corner, shifted(side, 1, False))
    side_force = jnp.take_along_axis(pair(west[0:1], east[0:1]), jnp.where(along < rows, 8 * along, 0) + FORCE_SLOT, axis=1)
    side_next = stencil(
        side, pair(ends_ref[0:1], east[4:5]), pair(west[4:5], ends_ref[1:2]), side_north, side_south,
        *[pair(west[k : k + 1], east[k : k + 1]) for k in (5, 6, 7)],
    ) + jnp.where(along < rows, side_force, 0.0)

    listed = [
        (west[3:4], east[3:4]),
        (side_next[0:1], side_next[1:2]),
        (jnp.where(is_top, moved[0:1], over[0:1]), jnp.where(is_top, fold[0:1], moved[1:2])),
        (under[0:1], moved[2:3]),
        (jnp.where(is_top, fold_east, moved[4:5]), jnp.where(is_top, moved[3:4], over_east)),
        (moved[5:6], under_east),
    ]
    lanes = {}
    for q, (low, high) in enumerate(listed):
        lanes[2 * q], lanes[(2 * q - 1) % cols] = low, high
    rim = fill(cols, lanes).T.reshape(theta_ref.shape)
    rim_ref[...] = rim

    def listing(q, field):
        return pltpu.roll(field, cols - 2 * q, field.ndim - 1) if q else field

    edges, inners = read_row(rim_ref, 0), read_row(rim_ref, 1)
    lane = lax.broadcasted_iota(jnp.int32, (levels, cols), 1)
    level = lax.broadcasted_iota(jnp.int32, (levels, cols), 0)
    ends = (lane == 0) | (lane == cols - 1)

    def forced(row, force):
        return row + jnp.where(level == 0, force, 0.0)

    flip = cols - 1 - lax.broadcasted_iota(jnp.int32, (8, cols), 1)
    flipped = jnp.take_along_axis(fold[:TILE], flip, axis=1)
    north_force = [jnp.where(is_top, flipped[k : k + 1], over[k : k + 1]) for k in (1, 2)]
    south_force = [under[1:2], under[2:3]]

    def beyond(rows_of, inside, outward, force, q):
        edge_row = stencil(
            rows_of[0], shifted(rows_of[0], 1, True), shifted(rows_of[0], 1, False),
            rows_of[1] if outward else inside, inside if outward else rows_of[1], *rows_of[3:],
        )
        edge_row = jnp.where(ends, listing(q, edges), forced(edge_row, force[0]))
        return edge_row, jnp.where(ends, listing(q, inners), forced(rows_of[2], force[1]))

    north_one, north_two = beyond(north, read_row(theta_ref, last), True, north_force, 2)
    south_one, south_two = beyond(south, read_row(theta_ref, 0), False, south_force, 3)
    south_one, south_two = jnp.where(has_south, south_one, 0.0), jnp.where(has_south, south_two, 0.0)
    shape = theta_ref.shape
    wide = lax.broadcasted_iota(jnp.int32, shape, 2)
    force = jnp.where(lax.broadcasted_iota(jnp.int32, shape, 0) == 0, force_ref[...][None], 0.0)
    inside = (lane >= 2) & (lane < cols - 2)
    more_north, more_south = inside & jnp.logical_not(here.even), inside & here.even
    top_row = read_row(next_ref, last) + jnp.where(more_north, read_row(points_ref.at[3], last) * north[0], 0.0)
    bottom_row = read_row(next_ref, 0) + jnp.where(more_south, read_row(points_ref.at[4], 0) * south[0], 0.0)
    tall_ref[:, TILE : 2 * TILE, :] = next_ref[...]
    write_row(tall_ref, TILE + last, top_row)
    write_row(tall_ref, TILE, bottom_row)

    def outer(row, further, inside, outward, rows_of, force_row, diagonal):
        result = stencil(
            row, jnp.where(lane == cols - 1, diagonal, shifted(row, 1, True)),
            jnp.where(lane == 0, diagonal, shifted(row, 1, False)),
            further if outward else inside, inside if outward else further, *rows_of[3:],
        )
        return forced(result, force_row)

    north_next = outer(north_one, north_two, top_row, True, north, north_force[0], listing(4, edges))
    south_next = outer(south_one, south_two, bottom_row, False, south, south_force[0], listing(5, edges))
    south_next = jnp.where(has_south, south_next, 0.0)

    def advance(sides, above, below):
        write_row(tall_ref, 2 * TILE, above)
        write_row(tall_ref, TILE - 1, below)
        t = tall_ref[:, TILE : 2 * TILE, :]
        east = jnp.where(wide == cols - 1, sides, shifted(t, 2, True))
        west = jnp.where(wide == 0, sides, shifted(t, 2, False))
        north, south = tall_ref[:, TILE + 1 : 2 * TILE + 1, :], tall_ref[:, TILE - 1 : 2 * TILE - 1, :]
        result = force
        for k, field in enumerate((t, east, west, north, south)):
            result = result + points_ref[k] * field
        return result

    tall_ref[:, TILE : 2 * TILE, :] = advance(rim, north_one, south_one)
    result_ref[...] = advance(listing(1, rim), north_next, south_next)
    copies[1].start()
    for copy in copies:
        copy.wait()


def exchange(blocks):
    return lax.all_to_all(blocks, ("ns", "ew"), split_axis=0, concat_axis=0, tiled=True)


def swap(rows):
    pairs = [(i, i + 1) for i in range(0, lax.axis_size("ns"), 2)]
    return lax.ppermute(rows, "ns", pairs + [(b, a) for a, b in pairs])


def local(theta, velocity, diffusivity, land_mask, fold_partner, atm_flux, remap_src, remap_weights):
    levels, rows, cols = theta.shape
    fields = atm_flux.shape[2]
    shape = jax.ShapeDtypeStruct
    devices = lax.axis_size("ew") * lax.axis_size("ns")
    blocks = (devices, TILE, cols)
    room = 60 * 2**20 - 2 * max(0, 4 * devices * TILE * cols - 2**20)
    weights = remap_weights[0, 0]
    near_partner = swap(fold_partner).reshape(1, 1)
    field, velocity, diffusivity, flux = bring(
        [theta, velocity, diffusivity, atm_flux[0, 0]], [pltpu.VMEM] * 4, room, "bring"
    )
    out, near, partner, token = pl.pallas_call(
        first_kernel,
        out_shape=(
            pltpu.VMEM(blocks, BF16), pltpu.VMEM((KINDS, levels, cols), F32), pltpu.SMEM((1,), jnp.int32),
            pltpu.HBM((TILE, cols), F32),
        ),
        in_specs=[VMEM] * 5,
        out_specs=(VMEM, VMEM, SMEM, VMEM),
        scratch_shapes=[pltpu.VMEM((2 * levels, TILE, cols), F32)],
        compiler_params=PARAMS,
        name="first",
    )(near_partner, field, velocity, diffusivity, flux)
    first, near = exchange(out), swap(near)
    sources, weights = bring([remap_src[0], weights], [pltpu.SMEM, pltpu.VMEM], room, "load", (token,))
    points, columns, start = pl.pallas_call(
        side_kernel,
        out_shape=(
            pltpu.VMEM((5,) + theta.shape, F32), pltpu.VMEM((2, 3, cols), F32), pltpu.VMEM(theta.shape, F32),
        ),
        in_specs=[SMEM] + [VMEM] * 3 + [pl.BlockSpec(memory_space=pl.ANY)],
        out_specs=(VMEM,) * 3,
        compiler_params=PARAMS,
        cost_estimate=pl.CostEstimate(flops=2**20, bytes_accessed=2**20, transcendentals=0),
        name="side",
    )(land_mask, field, velocity, diffusivity, token)
    total, force, after, ends, out = pl.pallas_call(
        middle_kernel,
        out_shape=(
            pltpu.VMEM((fields, rows * cols), F32), pltpu.VMEM((rows, cols), F32), pltpu.VMEM(theta.shape, F32),
            pltpu.VMEM((TILE, cols), F32), pltpu.VMEM(blocks, BF16),
        ),
        in_specs=[SMEM] * 3 + [VMEM] * 6,
        out_specs=(VMEM,) * 5,
        scratch_shapes=[pltpu.VMEM(theta.shape, F32)] * 2,
        compiler_params=PARAMS,
        name="middle",
    )(land_mask, partner, sources, columns, points, start, weights, first, near)
    second = exchange(out)
    field, flux = pl.pallas_call(
        last_kernel,
        out_shape=(shape(theta.shape, F32), shape((fields, rows, cols), F32)),
        in_specs=[SMEM] + [VMEM] * 9,
        out_specs=(HBM, HBM),
        scratch_shapes=[
            pltpu.VMEM(theta.shape, F32), pltpu.VMEM((fields, rows, cols), F32), pltpu.VMEM(theta.shape, F32),
            pltpu.VMEM((levels, 3 * TILE, cols), F32), pltpu.VMEM((levels, TILE, cols), F32),
            pltpu.SemaphoreType.DMA((2,)),
        ],
        compiler_params=PARAMS,
        name="last",
    )(partner, field, points, total, after, ends, force, first, second, near)
    return field, flux.reshape(1, 1, fields, rows * cols)


def solution(mesh):
    return jax.shard_map(
        local,
        mesh=mesh,
        in_specs=(
            P(None, "ns", "ew"),
            P(None, None, "ns", "ew"),
            P(None, "ns", "ew"),
            P("ns", "ew"),
            P("ew"),
            P("ns", "ew", None, None),
            P("ns", "ew", None),
            P("ns", "ew", None, None, None),
        ),
        out_specs=(P(None, "ns", "ew"), P("ns", "ew", None, None)),
        check_vma=False,
    )
```

```python
import functools

import jax
import jax.numpy as jnp
from jax import lax
from jax.experimental import pallas as pl
from jax.experimental.pallas import tpu as pltpu
from jax.sharding import PartitionSpec as P

COEFS = (0.5, -0.3, 0.2, 0.4, -0.25, 0.35)
VMEM = pl.BlockSpec(memory_space=pltpu.VMEM)
SMEM = pl.BlockSpec(memory_space=pltpu.SMEM)
HBM = pl.BlockSpec(memory_space=pltpu.HBM)
PARAMS = pltpu.CompilerParams(vmem_limit_bytes=16 * 1024 * 1024)
F32 = jnp.float32
BF16 = jnp.bfloat16
KINDS = 6
TILE = 8
FORCE_SLOT, WET_SLOT, PARTNER_SLOT = 4, 5, 4


def tendency(t, east, west, north, south, u, v, d):
    return d * (east + west + north + south - 4.0 * t) - 0.5 * (u * (east - west) + v * (north - south))


def stencil(t, *others):
    return t + tendency(t, *others)


class Place:
    def __init__(self):
        self.count, self.block_rows = lax.axis_size("ew"), lax.axis_size("ns")
        self.devices = self.count * self.block_rows
        self.e, self.n = lax.axis_index("ew"), lax.axis_index("ns")
        self.top = self.block_rows - 1
        self.is_top = self.n == self.top
        self.has_south = self.n > 0
        self.even = (self.n & 1) == 0
        self.east, self.west = self.wrap(self.e + 1), self.wrap(self.e + self.count - 1)
        self.above = jnp.minimum(self.n + 1, self.top)
        self.below = jnp.maximum(self.n - 1, 0)
        self.pair = jnp.where(self.even, self.n + 1, self.n - 1)
        self.other = jnp.where(self.even, self.below, self.above)

    def wrap(self, e):
        return jnp.where(e >= self.count, e - self.count, e)

    def slot(self, e, n):
        return n * self.count + e


def relays(row, block_rows):
    is_top = row == block_rows - 1
    odd = row & 1
    first = jnp.where((odd == 0) | is_top, jnp.maximum(row - 2, 0), row + 2)
    return first, jnp.where(is_top, jnp.maximum(row - 3, 0), row + 1 - 2 * odd), jnp.where(is_top, 0, 2)


def fill(size, rows):
    parts, at = [], 0
    for index in sorted(rows):
        if index > at:
            parts.append(jnp.zeros((index - at, size), F32))
        parts.append(rows[index])
        at = index + 1
    if at < size:
        parts.append(jnp.zeros((size - at, size), F32))
    return jnp.concatenate(parts, axis=0)


def turn(field):
    return field.reshape(field.shape[0] * field.shape[1], field.shape[2]).T


def row_of(ref, row):
    levels, rows, cols = ref.shape
    return ref.reshape(levels * rows, cols), pl.ds(row, levels, stride=rows)


def read_row(ref, row):
    flat, at = row_of(ref, row)
    return flat[at, :]


def write_row(ref, row, values):
    flat, at = row_of(ref, row)
    flat[at, :] = values


def shifted(field, axis, back):
    size = field.shape[axis]
    return pltpu.roll(field, size - 1 if back else 1, axis)


def bring_kernel(count, *refs):
    copies = [pltpu.make_async_copy(refs[i], refs[count + i], refs[-1].at[i]) for i in range(count)]
    for copy in copies:
        copy.start()
    for copy in copies:
        copy.wait()


def bring(arrays, memories, room, name):
    return pl.pallas_call(
        functools.partial(bring_kernel, len(arrays)),
        out_shape=tuple(memory(x.shape, x.dtype) for x, memory in zip(arrays, memories)),
        in_specs=[HBM] * len(arrays),
        out_specs=tuple(VMEM if memory is pltpu.VMEM else SMEM for memory in memories),
        scratch_shapes=[pltpu.SemaphoreType.DMA((len(arrays),))],
        compiler_params=pltpu.CompilerParams(vmem_limit_bytes=room),
        cost_estimate=pl.CostEstimate(flops=2**20, bytes_accessed=2**22, transcendentals=0),
        name=name,
    )(*arrays)


def first_kernel(partner_ref, theta_ref, vel_ref, diff_ref, atm_ref, out_ref, near_ref, bulk_ref):
    here = Place()
    levels, rows, cols = theta_ref.shape
    tiles = levels // TILE
    each = KINDS * tiles
    coef_refs = [vel_ref.at[0], vel_ref.at[1], diff_ref]
    turned = turn(theta_ref[...])
    strips = []
    for step in (1, -1):
        edge = rows - 1 if step < 0 else 0
        outer, t, inner = [read_row(theta_ref, edge + k * step) for k in range(3)]
        north, south = (outer, inner) if step < 0 else (inner, outer)
        coef = [read_row(ref, edge + step) for ref in coef_refs]
        tend = tendency(t, shifted(t, 1, True), shifted(t, 1, False), north, south, *coef)
        strips.append([outer, t, tend] + [read_row(ref, edge) for ref in coef_refs])
    for kind, (low, high) in enumerate(zip(*strips)):
        near_ref[kind] = jnp.where(here.even, high, low)
        far = jnp.where(here.even, low, high)
        bulk_ref[pl.ds(kind * tiles, tiles)] = far.reshape(tiles, TILE, cols)
    partner = partner_ref[0].astype(F32)
    fold_ref = bulk_ref.at[pl.ds(levels, levels)]
    for kind in range(KINDS):
        write_row(fold_ref, kind, strips[1][kind])
    write_row(fold_ref, KINDS, jnp.full((levels, cols), partner))
    write_row(fold_ref, KINDS + 1, jnp.zeros((levels, cols), F32))
    lane = lax.broadcasted_iota(jnp.int32, (TILE, cols), 1)
    slot = lane & 7
    spots = [turned[0:1], turned[1:2], turned[cols - 2 : cols - 1], turned[cols - 1 : cols]]
    spots = jnp.concatenate(spots + [jnp.zeros((TILE - 4, cols), F32)], axis=0)
    spots = jnp.where(here.even, spots, pltpu.roll(spots, cols - rows + 1, 1))
    corner = jnp.where(slot[0:1] == PARTNER_SLOT, partner, 0.0)
    for k in range(4):
        moved = pltpu.roll(spots, k, 1) if k else spots
        corner = jnp.where(slot[0:1] == k, moved[k : k + 1], corner)
    atm = atm_ref[...].astype(F32)
    to_west = jnp.concatenate([corner, turned[0:1], atm], axis=0)
    to_east = jnp.concatenate([corner, turned[cols - 1 : cols], atm], axis=0)
    column = jnp.where(here.is_top, partner_ref[0], here.e)
    first, second, skip = relays(jnp.where(here.is_top, here.top, here.other), here.block_rows)
    begin = jnp.where(here.is_top, levels, 0)
    for e in range(here.count):
        ahead = here.wrap(e - column + here.count)
        out_ref[here.slot(e, first)] = bulk_ref[begin + jnp.minimum(ahead, TILE - 1)].astype(BF16)
        out_ref[here.slot(e, second)] = bulk_ref[begin + jnp.minimum(ahead + TILE - skip, levels - 1)].astype(BF16)
    to_west, to_east = to_west.astype(BF16), to_east.astype(BF16)
    out_ref[here.slot(here.e, here.other)] = to_west
    for e in range(here.count):
        out_ref[here.slot(e, here.n)] = to_west
    out_ref[here.slot(here.east, here.n)] = to_east


def side_kernel(
    mask_ref, theta_ref, vel_ref, diff_ref, points_ref, columns_ref, start_ref
):
    levels, rows, cols = theta_ref.shape
    last = rows - 1
    wet = mask_ref[0, 0].astype(F32)
    u, v, d = wet * vel_ref[0], wet * vel_ref[1], wet * diff_ref[...]
    turned = [turn(u), turn(v), turn(d)]
    for side, at in enumerate((0, cols - 1)):
        for k in range(3):
            columns_ref[side, k : k + 1, :] = turned[k][at : at + 1]
    center, east, west, north, south = 1.0 - 4.0 * d, d - 0.5 * u, d + 0.5 * u, d - 0.5 * v, d + 0.5 * v
    for k, field in enumerate((center, east, west, north, south)):
        points_ref[k] = field
    t = theta_ref[...]
    lane = lax.broadcasted_iota(jnp.int32, t.shape, 2)
    line = lax.broadcasted_iota(jnp.int32, t.shape, 1)
    inner = center * t
    inner = inner + east * jnp.where(lane == cols - 1, 0.0, shifted(t, 2, True))
    inner = inner + west * jnp.where(lane == 0, 0.0, shifted(t, 2, False))
    inner = inner + north * jnp.where(line == last, 0.0, shifted(t, 1, True))
    inner = inner + south * jnp.where(line == 0, 0.0, shifted(t, 1, False))
    start_ref[...] = inner


def middle_kernel(
    mask_ref, partner_ref, src_ref, columns_ref, points_ref, start_ref, weights_ref, recv_ref, near_ref,
    total_ref, force_ref, next_ref, ends_ref, out_ref, beyond_ref, plain_ref,
):
    here = Place()
    levels, rows, cols = start_ref.shape
    fields = total_ref.shape[0]
    last = rows - 1
    wet = mask_ref[0, 0].astype(F32)

    pairs, cells, points = weights_ref.shape
    chosen = [recv_ref[here.slot(src_ref[0, pair], here.n)][TILE - fields :] for pair in range(pairs)]
    weights = weights_ref[...].reshape(pairs * cells, points)
    total = jnp.dot(jnp.concatenate(chosen, axis=1), weights, preferred_element_type=F32)
    total_ref[...] = total
    force = jnp.zeros((1, points), F32)
    for k in range(fields):
        force = force + COEFS[k] * total[k : k + 1]
    force = jnp.concatenate([force[:, r * cols : (r + 1) * cols] for r in range(rows)], axis=0)
    force = wet * (0.1 * force)
    force_ref[...] = force

    shape = start_ref.shape
    level = lax.broadcasted_iota(jnp.int32, shape, 0)

    def got(e, n):
        return recv_ref[here.slot(e, n)].astype(F32)

    sides = fill(cols, {0: got(here.west, here.n)[1:2], cols - 1: got(here.east, here.n)[1:2]}).T.reshape(shape)
    from_fold, over, under = got(partner_ref[0], here.n)[0:1], got(here.e, here.above)[0:1], got(here.e, here.below)[0:1]
    facing = jnp.where(here.is_top, from_fold, jnp.where(here.even, under, over))
    facing = jnp.broadcast_to(facing, (TILE, cols))
    facing = [facing[0:1]] + [pltpu.roll(facing, cols - k, 1)[0:1] for k in range(1, 4)]
    facing = [jnp.where(here.is_top, facing[3 - k], facing[k]) for k in range(4)]
    spots = (0, 1, cols - 2, cols - 1)
    beyond_ref[...] = fill(cols, dict(zip(spots, facing))).T.reshape(shape)
    far = read_row(beyond_ref, 0)
    above = jnp.where(here.even, near_ref[0], far)
    below = jnp.where(here.has_south, jnp.where(here.even, far, near_ref[0]), 0.0)
    lane = lax.broadcasted_iota(jnp.int32, shape, 2)
    rim = jnp.where(lane == cols - 1, points_ref[1], jnp.where(lane == 0, points_ref[2], 0.0))
    plain_ref[...] = start_ref[...] + rim * sides
    write_row(plain_ref, last, read_row(plain_ref, last) + read_row(points_ref.at[3], last) * above)
    write_row(plain_ref, 0, read_row(plain_ref, 0) + read_row(points_ref.at[4], 0) * below)
    t = plain_ref[...]
    next_ref[...] = t + jnp.where(level == 0, force[None], 0.0)

    held = [got(m, here.top) for m in range(here.count)]
    size = -(-here.count * TILE // cols) * cols
    tiles = held + [jnp.zeros((size - here.count * TILE, cols), F32)] * (size > here.count * TILE)
    tiles = jnp.concatenate(tiles, axis=0).astype(BF16)
    partners = jnp.concatenate([jnp.broadcast_to(block[KINDS : KINDS + 1, 0:1], (TILE, 1)) for block in held], axis=0)
    wanted = TILE * partners + (lax.broadcasted_iota(jnp.int32, partners.shape, 0) & (TILE - 1)).astype(F32)
    pick = lax.broadcasted_iota(jnp.int32, (here.count * TILE, size), 1).astype(F32) == wanted
    folded = jnp.dot(pick.astype(F32).astype(BF16), tiles, preferred_element_type=F32)

    turned = turn(t) + jnp.concatenate([force, jnp.zeros((cols - rows, cols), F32)], axis=0).T
    ends = jnp.concatenate([turned[0:1], turned[cols - 1 : cols], jnp.zeros((TILE - 2, cols), F32)], axis=0)
    lane = lax.broadcasted_iota(jnp.int32, (TILE, cols), 1)
    forces = jnp.concatenate([force, jnp.zeros((cols - rows, cols), F32)], axis=0).T
    forces = jnp.concatenate([forces[0:1], forces[cols - 1 : cols], jnp.zeros((TILE - 2, cols), F32)], axis=0)
    ends_ref[...] = ends
    marks = jnp.take_along_axis(forces, lane >> 3, axis=1)
    slot = lane & 7
    marks = jnp.where(slot == FORCE_SLOT, marks, jnp.where(slot == WET_SLOT, wet, 0.0))
    slot = slot[0:1]

    def corners(shifts, mark):
        row = mark
        for index, shift in enumerate(shifts):
            moved = pltpu.roll(ends, shift % cols, 1) if shift else ends
            row = jnp.where(slot == index, moved[index // 2 : index // 2 + 1], row)
        return row

    up, down = (-last, 2 - last, 2 - last, 4 - last), (0, 0, 2, 2)
    low_mark, high_mark = marks[0:1], marks[1:2]
    low_coef, high_coef = columns_ref[0], columns_ref[1]
    high_force, low_force = [force[last : last + 1], force[last - 1 : last]], [force[0:1], force[1:2]]
    low, high = [turned[0:1], turned[1:2]], [turned[cols - 1 : cols], turned[cols - 2 : cols - 1]]
    base = jnp.concatenate([corners(up, low_mark)] + high_force + low + [low_coef], axis=0)
    to_east = jnp.concatenate([corners(up, high_mark)] + high_force + high + [high_coef], axis=0)
    to_below = jnp.concatenate([corners(down, low_mark)] + low_force + low + [low_coef], axis=0)
    for e in range(here.count):
        close = (e == here.e) | (e == here.east) | (e == here.west)
        for n in range(here.block_rows):
            begin = jnp.where(n == here.n - 1, to_below, jnp.where(e == here.east, to_east, base))
            owed = (n == here.n) | (close & ((n == here.n - 1) | (n == here.n + 1)))
            if n == here.top:
                tile = folded[e * TILE : (e + 1) * TILE]
            else:
                tile = got(e, max(n - 1, 0) if n % 2 == 0 else n + 1)
            out_ref[n * here.count + e] = jnp.where(owed, begin, tile).astype(BF16)


def last_kernel(
    partner_ref, theta_ref, points_ref, total_ref, next_ref, ends_ref, force_ref, first_ref, second_ref, near_ref,
    result_hbm, flux_hbm, result_ref, flux_ref, rim_ref, tall_ref, tile_ref, sems,
):
    here = Place()
    levels, rows, cols = theta_ref.shape
    last = rows - 1
    partner = partner_ref[0]
    is_top, has_south = here.is_top, here.has_south

    def got(e, n):
        return second_ref[here.slot(e, n)].astype(F32)

    west, east = got(here.west, here.n), got(here.east, here.n)
    over, under = got(here.e, here.above), got(here.e, here.below)
    fold = got(partner, here.n)
    fold_east = got(here.wrap(partner + 1), here.n)[0:1]
    fold_west = got(here.wrap(partner + here.count - 1), here.n)[0:1]
    over_west, over_east = got(here.west, here.above)[0:1], got(here.east, here.above)[0:1]
    under_west, under_east = got(here.west, here.below)[0:1], got(here.east, here.below)[0:1]
    first_west = first_ref[here.slot(here.west, here.n)].astype(F32)
    first_east = first_ref[here.slot(here.east, here.n)].astype(F32)

    def mark(block):
        return block[0:1, WET_SLOT : WET_SLOT + 1]

    first, second, skip = relays(here.n, here.block_rows)
    for k in range(levels):
        ahead, row = (k, first) if k < TILE else (k - TILE + skip, second)
        tile_ref[k] = got(here.wrap(here.e + jnp.minimum(ahead, here.count - 1)), row)
    tiles = levels // TILE
    far = [tile_ref[pl.ds(kind * tiles, tiles)].reshape(levels, cols) for kind in range(KINDS)]
    far = jnp.concatenate(far, axis=0)
    mirrored = jnp.concatenate([read_row(tile_ref, kind) for kind in range(KINDS)], axis=0)
    mirror = cols - 1 - lax.broadcasted_iota(jnp.int32, far.shape, 1)
    far = jnp.where(is_top, jnp.take_along_axis(mirrored, mirror, axis=1), far)
    far = [far[kind * levels : (kind + 1) * levels] for kind in range(KINDS)]
    near = [near_ref[kind] for kind in range(KINDS)]
    north = [jnp.where(here.even, a, b) for a, b in zip(near, far)]
    south = [jnp.where(has_south, jnp.where(here.even, b, a), 0.0) for a, b in zip(near, far)]

    def kinds(strip, wet, sign):
        t, inner, tend, u, v, d = strip
        return t, inner, inner + wet * tend, (sign * wet) * u, (sign * wet) * v, wet * d

    north = kinds(north, jnp.where(is_top, mark(fold), mark(over)), jnp.where(is_top, -1.0, 1.0))
    south = kinds(south, mark(under), 1.0)

    top_west, top_east = jnp.zeros((1, cols), F32), jnp.zeros((1, cols), F32)
    for s in range(here.count):
        row = got(s, here.n)[0:1]
        top_west = jnp.where(first_west[0:1, PARTNER_SLOT : PARTNER_SLOT + 1] == float(s), row, top_west)
        top_east = jnp.where(first_east[0:1, PARTNER_SLOT : PARTNER_SLOT + 1] == float(s), row, top_east)
    moved = [fold[0:1], over[0:1], under[0:1], fold_west, over_west, under_west, top_east]
    moved = jnp.concatenate(moved + [jnp.zeros((1, cols), F32)], axis=0)
    moved = pltpu.roll(moved, cols - 2, 1)
    def pair(low, high):
        return jnp.concatenate([low, high, jnp.zeros((TILE - 2, cols), F32)], axis=0)

    along = lax.broadcasted_iota(jnp.int32, (TILE, cols), 1)
    place = along & 7
    side = pair(west[3:4], east[3:4])
    corner = pair(jnp.where(is_top, top_west, moved[4:5]), jnp.where(is_top, moved[6:7], over_east))
    side_north = jnp.where(place == last, pltpu.roll(corner, last, 1), shifted(side, 1, True))
    corner = jnp.where(has_south, pair(moved[5:6], under_east), 0.0)
    side_south = jnp.where(place == 0, corner, shifted(side, 1, False))
    side_force = jnp.take_along_axis(pair(west[0:1], east[0:1]), jnp.where(along < rows, 8 * along, 0) + FORCE_SLOT, axis=1)
    side_next = stencil(
        side, pair(ends_ref[0:1], east[4:5]), pair(west[4:5], ends_ref[1:2]), side_north, side_south,
        *[pair(west[k : k + 1], east[k : k + 1]) for k in (5, 6, 7)],
    ) + jnp.where(along < rows, side_force, 0.0)

    listed = [
        (west[3:4], east[3:4]),
        (side_next[0:1], side_next[1:2]),
        (jnp.where(is_top, moved[0:1], over[0:1]), jnp.where(is_top, fold[0:1], moved[1:2])),
        (under[0:1], moved[2:3]),
        (jnp.where(is_top, fold_east, moved[4:5]), jnp.where(is_top, moved[3:4], over_east)),
        (moved[5:6], under_east),
    ]
    lanes = {}
    for q, (low, high) in enumerate(listed):
        lanes[2 * q], lanes[(2 * q - 1) % cols] = low, high
    rim = fill(cols, lanes).T.reshape(theta_ref.shape)
    rim_ref[...] = rim

    def listing(q, field):
        return pltpu.roll(field, cols - 2 * q, field.ndim - 1) if q else field

    edges, inners = read_row(rim_ref, 0), read_row(rim_ref, 1)
    lane = lax.broadcasted_iota(jnp.int32, (levels, cols), 1)
    level = lax.broadcasted_iota(jnp.int32, (levels, cols), 0)
    ends = (lane == 0) | (lane == cols - 1)

    def forced(row, force):
        return row + jnp.where(level == 0, force, 0.0)

    flip = cols - 1 - lax.broadcasted_iota(jnp.int32, (8, cols), 1)
    flipped = jnp.take_along_axis(fold[:TILE], flip, axis=1)
    north_force = [jnp.where(is_top, flipped[k : k + 1], over[k : k + 1]) for k in (1, 2)]
    south_force = [under[1:2], under[2:3]]

    def beyond(rows_of, inside, outward, force, q):
        edge_row = stencil(
            rows_of[0], shifted(rows_of[0], 1, True), shifted(rows_of[0], 1, False),
            rows_of[1] if outward else inside, inside if outward else rows_of[1], *rows_of[3:],
        )
        edge_row = jnp.where(ends, listing(q, edges), forced(edge_row, force[0]))
        return edge_row, jnp.where(ends, listing(q, inners), forced(rows_of[2], force[1]))

    north_one, north_two = beyond(north, read_row(theta_ref, last), True, north_force, 2)
    south_one, south_two = beyond(south, read_row(theta_ref, 0), False, south_force, 3)
    south_one, south_two = jnp.where(has_south, south_one, 0.0), jnp.where(has_south, south_two, 0.0)
    shape = theta_ref.shape
    wide = lax.broadcasted_iota(jnp.int32, shape, 2)
    force = jnp.where(lax.broadcasted_iota(jnp.int32, shape, 0) == 0, force_ref[...][None], 0.0)
    inside = (lane >= 2) & (lane < cols - 2)
    more_north, more_south = inside & jnp.logical_not(here.even), inside & here.even
    top_row = read_row(next_ref, last) + jnp.where(more_north, read_row(points_ref.at[3], last) * north[0], 0.0)
    bottom_row = read_row(next_ref, 0) + jnp.where(more_south, read_row(points_ref.at[4], 0) * south[0], 0.0)
    tall_ref[:, TILE : 2 * TILE, :] = next_ref[...]
    write_row(tall_ref, TILE + last, top_row)
    write_row(tall_ref, TILE, bottom_row)

    def outer(row, further, inside, outward, rows_of, force_row, diagonal):
        result = stencil(
            row, jnp.where(lane == cols - 1, diagonal, shifted(row, 1, True)),
            jnp.where(lane == 0, diagonal, shifted(row, 1, False)),
            further if outward else inside, inside if outward else further, *rows_of[3:],
        )
        return forced(result, force_row)

    north_next = outer(north_one, north_two, top_row, True, north, north_force[0], listing(4, edges))
    south_next = outer(south_one, south_two, bottom_row, False, south, south_force[0], listing(5, edges))
    south_next = jnp.where(has_south, south_next, 0.0)

    def advance(sides, above, below):
        write_row(tall_ref, 2 * TILE, above)
        write_row(tall_ref, TILE - 1, below)
        t = tall_ref[:, TILE : 2 * TILE, :]
        east = jnp.where(wide == cols - 1, sides, shifted(t, 2, True))
        west = jnp.where(wide == 0, sides, shifted(t, 2, False))
        north, south = tall_ref[:, TILE + 1 : 2 * TILE + 1, :], tall_ref[:, TILE - 1 : 2 * TILE - 1, :]
        result = force
        for k, field in enumerate((t, east, west, north, south)):
            result = result + points_ref[k] * field
        return result

    tall_ref[:, TILE : 2 * TILE, :] = advance(rim, north_one, south_one)
    result_ref[...] = advance(listing(1, rim), north_next, south_next)
    for k in range(flux_ref.shape[0]):
        for r in range(rows):
            flux_ref[k, r : r + 1, :] = total_ref[k : k + 1, r * cols : (r + 1) * cols]
    copies = [
        pltpu.make_async_copy(flux_ref, flux_hbm, sems.at[0]), pltpu.make_async_copy(result_ref, result_hbm, sems.at[1])
    ]
    for copy in copies:
        copy.start()
    for copy in copies:
        copy.wait()


def exchange(blocks):
    return lax.all_to_all(blocks, ("ns", "ew"), split_axis=0, concat_axis=0, tiled=True)


def swap(rows):
    pairs = [(i, i + 1) for i in range(0, lax.axis_size("ns"), 2)]
    return lax.ppermute(rows, "ns", pairs + [(b, a) for a, b in pairs])


def local(theta, velocity, diffusivity, land_mask, fold_partner, atm_flux, remap_src, remap_weights):
    levels, rows, cols = theta.shape
    fields = atm_flux.shape[2]
    shape = jax.ShapeDtypeStruct
    devices = lax.axis_size("ew") * lax.axis_size("ns")
    blocks = (devices, TILE, cols)
    room = 60 * 2**20 - 2 * max(0, 4 * devices * TILE * cols - 2**20)
    weights = remap_weights[0, 0]
    field, velocity, diffusivity, flux = bring(
        [theta, velocity, diffusivity, atm_flux[0, 0]], [pltpu.VMEM] * 4, room, "bring"
    )
    out, near = pl.pallas_call(
        first_kernel,
        out_shape=(pltpu.VMEM(blocks, BF16), pltpu.VMEM((KINDS, levels, cols), F32)),
        in_specs=[SMEM] + [VMEM] * 4,
        out_specs=(VMEM,) * 2,
        scratch_shapes=[pltpu.VMEM((2 * levels, TILE, cols), F32)],
        compiler_params=PARAMS,
        name="first",
    )(fold_partner, field, velocity, diffusivity, flux)
    first, near = exchange(out), swap(near)
    sources, weights = bring([remap_src[0], weights], [pltpu.SMEM, pltpu.VMEM], room, "load")
    points, columns, start = pl.pallas_call(
        side_kernel,
        out_shape=(
            pltpu.VMEM((5,) + theta.shape, F32), pltpu.VMEM((2, 3, cols), F32), pltpu.VMEM(theta.shape, F32),
        ),
        in_specs=[SMEM] + [VMEM] * 3,
        out_specs=(VMEM,) * 3,
        compiler_params=PARAMS,
        cost_estimate=pl.CostEstimate(flops=2**20, bytes_accessed=2**20, transcendentals=0),
        name="side",
    )(land_mask, field, velocity, diffusivity)
    total, force, after, ends, out = pl.pallas_call(
        middle_kernel,
        out_shape=(
            pltpu.VMEM((fields, rows * cols), F32), pltpu.VMEM((rows, cols), F32), pltpu.VMEM(theta.shape, F32),
            pltpu.VMEM((TILE, cols), F32), pltpu.VMEM(blocks, BF16),
        ),
        in_specs=[SMEM] * 3 + [VMEM] * 6,
        out_specs=(VMEM,) * 5,
        scratch_shapes=[pltpu.VMEM(theta.shape, F32)] * 2,
        compiler_params=PARAMS,
        name="middle",
    )(land_mask, fold_partner, sources, columns, points, start, weights, first, near)
    second = exchange(out)
    field, flux = pl.pallas_call(
        last_kernel,
        out_shape=(shape(theta.shape, F32), shape((fields, rows, cols), F32)),
        in_specs=[SMEM] + [VMEM] * 9,
        out_specs=(HBM, HBM),
        scratch_shapes=[
            pltpu.VMEM(theta.shape, F32), pltpu.VMEM((fields, rows, cols), F32), pltpu.VMEM(theta.shape, F32),
            pltpu.VMEM((levels, 3 * TILE, cols), F32), pltpu.VMEM((levels, TILE, cols), F32),
            pltpu.SemaphoreType.DMA((2,)),
        ],
        compiler_params=PARAMS,
        name="last",
    )(fold_partner, field, points, total, after, ends, force, first, second, near)
    return field, flux.reshape(1, 1, fields, rows * cols)


def solution(mesh):
    return jax.shard_map(
        local,
        mesh=mesh,
        in_specs=(
            P(None, "ns", "ew"),
            P(None, None, "ns", "ew"),
            P(None, "ns", "ew"),
            P("ns", "ew"),
            P("ew"),
            P("ns", "ew", None, None),
            P("ns", "ew", None),
            P("ns", "ew", None, None, None),
        ),
        out_specs=(P(None, "ns", "ew"), P("ns", "ew", None, None)),
        check_vma=False,
    )
```

```python
import functools

import jax
import jax.numpy as jnp
from jax import lax
from jax.experimental import pallas as pl
from jax.experimental.pallas import tpu as pltpu
from jax.sharding import PartitionSpec as P

COEFS = (0.5, -0.3, 0.2, 0.4, -0.25, 0.35)
VMEM = pl.BlockSpec(memory_space=pltpu.VMEM)
SMEM = pl.BlockSpec(memory_space=pltpu.SMEM)
HBM = pl.BlockSpec(memory_space=pltpu.HBM)
PARAMS = pltpu.CompilerParams(vmem_limit_bytes=16 * 1024 * 1024)
F32 = jnp.float32
BF16 = jnp.bfloat16
KINDS = 6
TILE = 8
FORCE_SLOT, WET_SLOT, PARTNER_SLOT = 4, 5, 4


def tendency(t, east, west, north, south, u, v, d):
    return d * (east + west + north + south - 4.0 * t) - 0.5 * (u * (east - west) + v * (north - south))


def stencil(t, *others):
    return t + tendency(t, *others)


class Place:
    def __init__(self):
        self.count, self.block_rows = lax.axis_size("ew"), lax.axis_size("ns")
        self.devices = self.count * self.block_rows
        self.e, self.n = lax.axis_index("ew"), lax.axis_index("ns")
        self.top = self.block_rows - 1
        self.is_top = self.n == self.top
        self.has_south = self.n > 0
        self.even = (self.n & 1) == 0
        self.east, self.west = self.wrap(self.e + 1), self.wrap(self.e + self.count - 1)
        self.above = jnp.minimum(self.n + 1, self.top)
        self.below = jnp.maximum(self.n - 1, 0)
        self.pair = jnp.where(self.even, self.n + 1, self.n - 1)
        self.other = jnp.where(self.even, self.below, self.above)

    def wrap(self, e):
        return jnp.where(e >= self.count, e - self.count, e)

    def slot(self, e, n):
        return n * self.count + e

    def second_slot(self, e, n):
        return e * self.block_rows + n


def relays(row, block_rows):
    is_top = row == block_rows - 1
    odd = row & 1
    first = jnp.where((odd == 0) | is_top, jnp.maximum(row - 2, 0), row + 2)
    return first, jnp.where(is_top, jnp.maximum(row - 3, 0), row + 1 - 2 * odd), jnp.where(is_top, 0, 2)


def fill(size, rows):
    parts, at = [], 0
    for index in sorted(rows):
        if index > at:
            parts.append(jnp.zeros((index - at, size), F32))
        parts.append(rows[index])
        at = index + 1
    if at < size:
        parts.append(jnp.zeros((size - at, size), F32))
    return jnp.concatenate(parts, axis=0)


def turn(field):
    return field.reshape(field.shape[0] * field.shape[1], field.shape[2]).T


def row_of(ref, row):
    levels, rows, cols = ref.shape
    return ref.reshape(levels * rows, cols), pl.ds(row, levels, stride=rows)


def read_row(ref, row):
    flat, at = row_of(ref, row)
    return flat[at, :]


def write_row(ref, row, values):
    flat, at = row_of(ref, row)
    flat[at, :] = values


def shifted(field, axis, back):
    size = field.shape[axis]
    return pltpu.roll(field, size - 1 if back else 1, axis)


def bring_kernel(count, *refs):
    copies = [pltpu.make_async_copy(refs[i], refs[count + i], refs[-1].at[i]) for i in range(count)]
    for copy in copies:
        copy.start()
    for copy in copies:
        copy.wait()


def bring(arrays, memories, room, name):
    return pl.pallas_call(
        functools.partial(bring_kernel, len(arrays)),
        out_shape=tuple(memory(x.shape, x.dtype) for x, memory in zip(arrays, memories)),
        in_specs=[HBM] * len(arrays),
        out_specs=tuple(VMEM if memory is pltpu.VMEM else SMEM for memory in memories),
        scratch_shapes=[pltpu.SemaphoreType.DMA((len(arrays),))],
        compiler_params=pltpu.CompilerParams(vmem_limit_bytes=room),
        cost_estimate=pl.CostEstimate(flops=2**20, bytes_accessed=2**22, transcendentals=0),
        name=name,
    )(*arrays)


def first_kernel(partner_ref, theta_ref, vel_ref, diff_ref, atm_ref, out_ref, near_ref, bulk_ref):
    here = Place()
    levels, rows, cols = theta_ref.shape
    tiles = levels // TILE
    each = KINDS * tiles
    coef_refs = [vel_ref.at[0], vel_ref.at[1], diff_ref]
    turned = turn(theta_ref[...])
    strips = []
    for step in (1, -1):
        edge = rows - 1 if step < 0 else 0
        outer, t, inner = [read_row(theta_ref, edge + k * step) for k in range(3)]
        north, south = (outer, inner) if step < 0 else (inner, outer)
        coef = [read_row(ref, edge + step) for ref in coef_refs]
        tend = tendency(t, shifted(t, 1, True), shifted(t, 1, False), north, south, *coef)
        strips.append([outer, t, tend] + [read_row(ref, edge) for ref in coef_refs])
    for kind, (low, high) in enumerate(zip(*strips)):
        near_ref[kind] = jnp.where(here.even, high, low)
        far = jnp.where(here.even, low, high)
        bulk_ref[pl.ds(kind * tiles, tiles)] = far.reshape(tiles, TILE, cols)
    partner = partner_ref[0].astype(F32)
    fold_ref = bulk_ref.at[pl.ds(levels, levels)]
    for kind in range(KINDS):
        write_row(fold_ref, kind, strips[1][kind])
    write_row(fold_ref, KINDS, jnp.full((levels, cols), partner))
    write_row(fold_ref, KINDS + 1, jnp.zeros((levels, cols), F32))
    lane = lax.broadcasted_iota(jnp.int32, (TILE, cols), 1)
    slot = lane & 7
    spots = [turned[0:1], turned[1:2], turned[cols - 2 : cols - 1], turned[cols - 1 : cols]]
    spots = jnp.concatenate(spots + [jnp.zeros((TILE - 4, cols), F32)], axis=0)
    spots = jnp.where(here.even, spots, pltpu.roll(spots, cols - rows + 1, 1))
    corner = jnp.where(slot[0:1] == PARTNER_SLOT, partner, 0.0)
    for k in range(4):
        moved = pltpu.roll(spots, k, 1) if k else spots
        corner = jnp.where(slot[0:1] == k, moved[k : k + 1], corner)
    atm = atm_ref[...].astype(F32)
    to_west = jnp.concatenate([corner, turned[0:1], atm], axis=0)
    to_east = jnp.concatenate([corner, turned[cols - 1 : cols], atm], axis=0)
    column = jnp.where(here.is_top, partner_ref[0], here.e)
    first, second, skip = relays(jnp.where(here.is_top, here.top, here.other), here.block_rows)
    begin = jnp.where(here.is_top, levels, 0)
    for e in range(here.count):
        ahead = here.wrap(e - column + here.count)
        out_ref[here.slot(e, first)] = bulk_ref[begin + jnp.minimum(ahead, TILE - 1)].astype(BF16)
        out_ref[here.slot(e, second)] = bulk_ref[begin + jnp.minimum(ahead + TILE - skip, levels - 1)].astype(BF16)
    to_west, to_east = to_west.astype(BF16), to_east.astype(BF16)
    out_ref[here.slot(here.e, here.other)] = to_west
    for e in range(here.count):
        out_ref[here.slot(e, here.n)] = to_west
    out_ref[here.slot(here.east, here.n)] = to_east


def side_kernel(
    mask_ref, theta_ref, vel_ref, diff_ref, points_ref, columns_ref, start_ref
):
    levels, rows, cols = theta_ref.shape
    last = rows - 1
    wet = mask_ref[0, 0].astype(F32)
    u, v, d = wet * vel_ref[0], wet * vel_ref[1], wet * diff_ref[...]
    turned = [turn(u), turn(v), turn(d)]
    for side, at in enumerate((0, cols - 1)):
        for k in range(3):
            columns_ref[side, k : k + 1, :] = turned[k][at : at + 1]
    center, east, west, north, south = 1.0 - 4.0 * d, d - 0.5 * u, d + 0.5 * u, d - 0.5 * v, d + 0.5 * v
    for k, field in enumerate((center, east, west, north, south)):
        points_ref[k] = field
    t = theta_ref[...]
    lane = lax.broadcasted_iota(jnp.int32, t.shape, 2)
    line = lax.broadcasted_iota(jnp.int32, t.shape, 1)
    inner = center * t
    inner = inner + east * jnp.where(lane == cols - 1, 0.0, shifted(t, 2, True))
    inner = inner + west * jnp.where(lane == 0, 0.0, shifted(t, 2, False))
    inner = inner + north * jnp.where(line == last, 0.0, shifted(t, 1, True))
    inner = inner + south * jnp.where(line == 0, 0.0, shifted(t, 1, False))
    start_ref[...] = inner


def middle_kernel(
    mask_ref, partner_ref, src_ref, columns_ref, points_ref, start_ref, weights_ref, recv_ref, near_ref,
    total_ref, force_ref, next_ref, ends_ref, out_ref, beyond_ref, plain_ref,
):
    here = Place()
    levels, rows, cols = start_ref.shape
    fields = total_ref.shape[0]
    last = rows - 1
    wet = mask_ref[0, 0].astype(F32)

    pairs, cells, points = weights_ref.shape
    chosen = [recv_ref[here.slot(src_ref[0, pair], here.n)][TILE - fields :] for pair in range(pairs)]
    weights = weights_ref[...].reshape(pairs * cells, points)
    total = jnp.dot(jnp.concatenate(chosen, axis=1), weights, preferred_element_type=F32)
    total_ref[...] = total
    force = jnp.zeros((1, points), F32)
    for k in range(fields):
        force = force + COEFS[k] * total[k : k + 1]
    force = jnp.concatenate([force[:, r * cols : (r + 1) * cols] for r in range(rows)], axis=0)
    force = wet * (0.1 * force)
    force_ref[...] = force

    shape = start_ref.shape
    level = lax.broadcasted_iota(jnp.int32, shape, 0)

    def got(e, n):
        return recv_ref[here.slot(e, n)].astype(F32)

    sides = fill(cols, {0: got(here.west, here.n)[1:2], cols - 1: got(here.east, here.n)[1:2]}).T.reshape(shape)
    from_fold, over, under = got(partner_ref[0], here.n)[0:1], got(here.e, here.above)[0:1], got(here.e, here.below)[0:1]
    facing = jnp.where(here.is_top, from_fold, jnp.where(here.even, under, over))
    facing = jnp.broadcast_to(facing, (TILE, cols))
    facing = [facing[0:1]] + [pltpu.roll(facing, cols - k, 1)[0:1] for k in range(1, 4)]
    facing = [jnp.where(here.is_top, facing[3 - k], facing[k]) for k in range(4)]
    spots = (0, 1, cols - 2, cols - 1)
    beyond_ref[...] = fill(cols, dict(zip(spots, facing))).T.reshape(shape)
    far = read_row(beyond_ref, 0)
    above = jnp.where(here.even, near_ref[0], far)
    below = jnp.where(here.has_south, jnp.where(here.even, far, near_ref[0]), 0.0)
    lane = lax.broadcasted_iota(jnp.int32, shape, 2)
    rim = jnp.where(lane == cols - 1, points_ref[1], jnp.where(lane == 0, points_ref[2], 0.0))
    plain_ref[...] = start_ref[...] + rim * sides
    write_row(plain_ref, last, read_row(plain_ref, last) + read_row(points_ref.at[3], last) * above)
    write_row(plain_ref, 0, read_row(plain_ref, 0) + read_row(points_ref.at[4], 0) * below)
    t = plain_ref[...]
    next_ref[...] = t + jnp.where(level == 0, force[None], 0.0)

    held = [got(m, here.top) for m in range(here.count)]
    size = -(-here.count * TILE // cols) * cols
    tiles = held + [jnp.zeros((size - here.count * TILE, cols), F32)] * (size > here.count * TILE)
    tiles = jnp.concatenate(tiles, axis=0).astype(BF16)
    partners = jnp.concatenate([jnp.broadcast_to(block[KINDS : KINDS + 1, 0:1], (TILE, 1)) for block in held], axis=0)
    wanted = TILE * partners + (lax.broadcasted_iota(jnp.int32, partners.shape, 0) & (TILE - 1)).astype(F32)
    pick = lax.broadcasted_iota(jnp.int32, (here.count * TILE, size), 1).astype(F32) == wanted
    folded = jnp.dot(pick.astype(F32).astype(BF16), tiles, preferred_element_type=F32)

    turned = turn(t) + jnp.concatenate([force, jnp.zeros((cols - rows, cols), F32)], axis=0).T
    ends = jnp.concatenate([turned[0:1], turned[cols - 1 : cols], jnp.zeros((TILE - 2, cols), F32)], axis=0)
    lane = lax.broadcasted_iota(jnp.int32, (TILE, cols), 1)
    forces = jnp.concatenate([force, jnp.zeros((cols - rows, cols), F32)], axis=0).T
    forces = jnp.concatenate([forces[0:1], forces[cols - 1 : cols], jnp.zeros((TILE - 2, cols), F32)], axis=0)
    ends_ref[...] = ends
    marks = jnp.take_along_axis(forces, lane >> 3, axis=1)
    slot = lane & 7
    marks = jnp.where(slot == FORCE_SLOT, marks, jnp.where(slot == WET_SLOT, wet, 0.0))
    slot = slot[0:1]

    def corners(shifts, mark):
        row = mark
        for index, shift in enumerate(shifts):
            moved = pltpu.roll(ends, shift % cols, 1) if shift else ends
            row = jnp.where(slot == index, moved[index // 2 : index // 2 + 1], row)
        return row

    up, down = (-last, 2 - last, 2 - last, 4 - last), (0, 0, 2, 2)
    low_mark, high_mark = marks[0:1], marks[1:2]
    low_coef, high_coef = columns_ref[0], columns_ref[1]
    high_force, low_force = [force[last : last + 1], force[last - 1 : last]], [force[0:1], force[1:2]]
    low, high = [turned[0:1], turned[1:2]], [turned[cols - 1 : cols], turned[cols - 2 : cols - 1]]
    base = jnp.concatenate([corners(up, low_mark)] + high_force + low + [low_coef], axis=0)
    to_east = jnp.concatenate([corners(up, high_mark)] + high_force + high + [high_coef], axis=0)
    to_below = jnp.concatenate([corners(down, low_mark)] + low_force + low + [low_coef], axis=0)
    for e in range(here.count):
        close = (e == here.e) | (e == here.east) | (e == here.west)
        for n in range(here.block_rows):
            begin = jnp.where(n == here.n - 1, to_below, jnp.where(e == here.east, to_east, base))
            owed = (n == here.n) | (close & ((n == here.n - 1) | (n == here.n + 1)))
            if n == here.top:
                tile = folded[e * TILE : (e + 1) * TILE]
            else:
                tile = got(e, max(n - 1, 0) if n % 2 == 0 else n + 1)
            out_ref[here.second_slot(e, n)] = jnp.where(owed, begin, tile).astype(BF16)


def last_kernel(
    partner_ref, theta_ref, points_ref, total_ref, next_ref, ends_ref, force_ref, first_ref, second_ref, near_ref,
    result_hbm, flux_hbm, result_ref, flux_ref, rim_ref, tall_ref, tile_ref, sems,
):
    here = Place()
    levels, rows, cols = theta_ref.shape
    last = rows - 1
    partner = partner_ref[0]
    is_top, has_south = here.is_top, here.has_south

    def got(e, n):
        return second_ref[here.second_slot(e, n)].astype(F32)

    west, east = got(here.west, here.n), got(here.east, here.n)
    over, under = got(here.e, here.above), got(here.e, here.below)
    fold = got(partner, here.n)
    fold_east = got(here.wrap(partner + 1), here.n)[0:1]
    fold_west = got(here.wrap(partner + here.count - 1), here.n)[0:1]
    over_west, over_east = got(here.west, here.above)[0:1], got(here.east, here.above)[0:1]
    under_west, under_east = got(here.west, here.below)[0:1], got(here.east, here.below)[0:1]
    first_west = first_ref[here.slot(here.west, here.n)].astype(F32)
    first_east = first_ref[here.slot(here.east, here.n)].astype(F32)

    def mark(block):
        return block[0:1, WET_SLOT : WET_SLOT + 1]

    first, second, skip = relays(here.n, here.block_rows)
    for k in range(levels):
        ahead, row = (k, first) if k < TILE else (k - TILE + skip, second)
        tile_ref[k] = got(here.wrap(here.e + jnp.minimum(ahead, here.count - 1)), row)
    tiles = levels // TILE
    far = [tile_ref[pl.ds(kind * tiles, tiles)].reshape(levels, cols) for kind in range(KINDS)]
    far = jnp.concatenate(far, axis=0)
    mirrored = jnp.concatenate([read_row(tile_ref, kind) for kind in range(KINDS)], axis=0)
    mirror = cols - 1 - lax.broadcasted_iota(jnp.int32, far.shape, 1)
    far = jnp.where(is_top, jnp.take_along_axis(mirrored, mirror, axis=1), far)
    far = [far[kind * levels : (kind + 1) * levels] for kind in range(KINDS)]
    near = [near_ref[kind] for kind in range(KINDS)]
    north = [jnp.where(here.even, a, b) for a, b in zip(near, far)]
    south = [jnp.where(has_south, jnp.where(here.even, b, a), 0.0) for a, b in zip(near, far)]

    def kinds(strip, wet, sign):
        t, inner, tend, u, v, d = strip
        return t, inner, inner + wet * tend, (sign * wet) * u, (sign * wet) * v, wet * d

    north = kinds(north, jnp.where(is_top, mark(fold), mark(over)), jnp.where(is_top, -1.0, 1.0))
    south = kinds(south, mark(under), 1.0)

    top_west, top_east = jnp.zeros((1, cols), F32), jnp.zeros((1, cols), F32)
    for s in range(here.count):
        row = got(s, here.n)[0:1]
        top_west = jnp.where(first_west[0:1, PARTNER_SLOT : PARTNER_SLOT + 1] == float(s), row, top_west)
        top_east = jnp.where(first_east[0:1, PARTNER_SLOT : PARTNER_SLOT + 1] == float(s), row, top_east)
    moved = [fold[0:1], over[0:1], under[0:1], fold_west, over_west, under_west, top_east]
    moved = jnp.concatenate(moved + [jnp.zeros((1, cols), F32)], axis=0)
    moved = pltpu.roll(moved, cols - 2, 1)
    def pair(low, high):
        return jnp.concatenate([low, high, jnp.zeros((TILE - 2, cols), F32)], axis=0)

    along = lax.broadcasted_iota(jnp.int32, (TILE, cols), 1)
    place = along & 7
    side = pair(west[3:4], east[3:4])
    corner = pair(jnp.where(is_top, top_west, moved[4:5]), jnp.where(is_top, moved[6:7], over_east))
    side_north = jnp.where(place == last, pltpu.roll(corner, last, 1), shifted(side, 1, True))
    corner = jnp.where(has_south, pair(moved[5:6], under_east), 0.0)
    side_south = jnp.where(place == 0, corner, shifted(side, 1, False))
    side_force = jnp.take_along_axis(pair(west[0:1], east[0:1]), jnp.where(along < rows, 8 * along, 0) + FORCE_SLOT, axis=1)
    side_next = stencil(
        side, pair(ends_ref[0:1], east[4:5]), pair(west[4:5], ends_ref[1:2]), side_north, side_south,
        *[pair(west[k : k + 1], east[k : k + 1]) for k in (5, 6, 7)],
    ) + jnp.where(along < rows, side_force, 0.0)

    listed = [
        (west[3:4], east[3:4]),
        (side_next[0:1], side_next[1:2]),
        (jnp.where(is_top, moved[0:1], over[0:1]), jnp.where(is_top, fold[0:1], moved[1:2])),
        (under[0:1], moved[2:3]),
        (jnp.where(is_top, fold_east, moved[4:5]), jnp.where(is_top, moved[3:4], over_east)),
        (moved[5:6], under_east),
    ]
    lanes = {}
    for q, (low, high) in enumerate(listed):
        lanes[2 * q], lanes[(2 * q - 1) % cols] = low, high
    rim = fill(cols, lanes).T.reshape(theta_ref.shape)
    rim_ref[...] = rim

    def listing(q, field):
        return pltpu.roll(field, cols - 2 * q, field.ndim - 1) if q else field

    edges, inners = read_row(rim_ref, 0), read_row(rim_ref, 1)
    lane = lax.broadcasted_iota(jnp.int32, (levels, cols), 1)
    level = lax.broadcasted_iota(jnp.int32, (levels, cols), 0)
    ends = (lane == 0) | (lane == cols - 1)

    def forced(row, force):
        return row + jnp.where(level == 0, force, 0.0)

    flip = cols - 1 - lax.broadcasted_iota(jnp.int32, (8, cols), 1)
    flipped = jnp.take_along_axis(fold[:TILE], flip, axis=1)
    north_force = [jnp.where(is_top, flipped[k : k + 1], over[k : k + 1]) for k in (1, 2)]
    south_force = [under[1:2], under[2:3]]

    def beyond(rows_of, inside, outward, force, q):
        edge_row = stencil(
            rows_of[0], shifted(rows_of[0], 1, True), shifted(rows_of[0], 1, False),
            rows_of[1] if outward else inside, inside if outward else rows_of[1], *rows_of[3:],
        )
        edge_row = jnp.where(ends, listing(q, edges), forced(edge_row, force[0]))
        return edge_row, jnp.where(ends, listing(q, inners), forced(rows_of[2], force[1]))

    north_one, north_two = beyond(north, read_row(theta_ref, last), True, north_force, 2)
    south_one, south_two = beyond(south, read_row(theta_ref, 0), False, south_force, 3)
    south_one, south_two = jnp.where(has_south, south_one, 0.0), jnp.where(has_south, south_two, 0.0)
    shape = theta_ref.shape
    wide = lax.broadcasted_iota(jnp.int32, shape, 2)
    force = jnp.where(lax.broadcasted_iota(jnp.int32, shape, 0) == 0, force_ref[...][None], 0.0)
    inside = (lane >= 2) & (lane < cols - 2)
    more_north, more_south = inside & jnp.logical_not(here.even), inside & here.even
    top_row = read_row(next_ref, last) + jnp.where(more_north, read_row(points_ref.at[3], last) * north[0], 0.0)
    bottom_row = read_row(next_ref, 0) + jnp.where(more_south, read_row(points_ref.at[4], 0) * south[0], 0.0)
    tall_ref[:, TILE : 2 * TILE, :] = next_ref[...]
    write_row(tall_ref, TILE + last, top_row)
    write_row(tall_ref, TILE, bottom_row)

    def outer(row, further, inside, outward, rows_of, force_row, diagonal):
        result = stencil(
            row, jnp.where(lane == cols - 1, diagonal, shifted(row, 1, True)),
            jnp.where(lane == 0, diagonal, shifted(row, 1, False)),
            further if outward else inside, inside if outward else further, *rows_of[3:],
        )
        return forced(result, force_row)

    north_next = outer(north_one, north_two, top_row, True, north, north_force[0], listing(4, edges))
    south_next = outer(south_one, south_two, bottom_row, False, south, south_force[0], listing(5, edges))
    south_next = jnp.where(has_south, south_next, 0.0)

    def advance(sides, above, below):
        write_row(tall_ref, 2 * TILE, above)
        write_row(tall_ref, TILE - 1, below)
        t = tall_ref[:, TILE : 2 * TILE, :]
        east = jnp.where(wide == cols - 1, sides, shifted(t, 2, True))
        west = jnp.where(wide == 0, sides, shifted(t, 2, False))
        north, south = tall_ref[:, TILE + 1 : 2 * TILE + 1, :], tall_ref[:, TILE - 1 : 2 * TILE - 1, :]
        result = force
        for k, field in enumerate((t, east, west, north, south)):
            result = result + points_ref[k] * field
        return result

    tall_ref[:, TILE : 2 * TILE, :] = advance(rim, north_one, south_one)
    result_ref[...] = advance(listing(1, rim), north_next, south_next)
    for k in range(flux_ref.shape[0]):
        for r in range(rows):
            flux_ref[k, r : r + 1, :] = total_ref[k : k + 1, r * cols : (r + 1) * cols]
    copies = [
        pltpu.make_async_copy(flux_ref, flux_hbm, sems.at[0]), pltpu.make_async_copy(result_ref, result_hbm, sems.at[1])
    ]
    for copy in copies:
        copy.start()
    for copy in copies:
        copy.wait()


def exchange(blocks, axes):
    return lax.all_to_all(blocks, axes, split_axis=0, concat_axis=0, tiled=True)


def swap(rows):
    pairs = [(i, i + 1) for i in range(0, lax.axis_size("ns"), 2)]
    return lax.ppermute(rows, "ns", pairs + [(b, a) for a, b in pairs])


def local(theta, velocity, diffusivity, land_mask, fold_partner, atm_flux, remap_src, remap_weights):
    levels, rows, cols = theta.shape
    fields = atm_flux.shape[2]
    shape = jax.ShapeDtypeStruct
    devices = lax.axis_size("ew") * lax.axis_size("ns")
    blocks = (devices, TILE, cols)
    room = 60 * 2**20 - 2 * max(0, 4 * devices * TILE * cols - 2**20)
    weights = remap_weights[0, 0]
    field, velocity, diffusivity, flux = bring(
        [theta, velocity, diffusivity, atm_flux[0, 0]], [pltpu.VMEM] * 4, room, "bring"
    )
    out, near = pl.pallas_call(
        first_kernel,
        out_shape=(pltpu.VMEM(blocks, BF16), pltpu.VMEM((KINDS, levels, cols), F32)),
        in_specs=[SMEM] + [VMEM] * 4,
        out_specs=(VMEM,) * 2,
        scratch_shapes=[pltpu.VMEM((2 * levels, TILE, cols), F32)],
        compiler_params=PARAMS,
        name="first",
    )(fold_partner, field, velocity, diffusivity, flux)
    first, near = exchange(out, ("ns", "ew")), swap(near)
    sources, weights = bring([remap_src[0], weights], [pltpu.SMEM, pltpu.VMEM], room, "load")
    points, columns, start = pl.pallas_call(
        side_kernel,
        out_shape=(
            pltpu.VMEM((5,) + theta.shape, F32), pltpu.VMEM((2, 3, cols), F32), pltpu.VMEM(theta.shape, F32),
        ),
        in_specs=[SMEM] + [VMEM] * 3,
        out_specs=(VMEM,) * 3,
        compiler_params=PARAMS,
        cost_estimate=pl.CostEstimate(flops=2**20, bytes_accessed=2**20, transcendentals=0),
        name="side",
    )(land_mask, field, velocity, diffusivity)
    total, force, after, ends, out = pl.pallas_call(
        middle_kernel,
        out_shape=(
            pltpu.VMEM((fields, rows * cols), F32), pltpu.VMEM((rows, cols), F32), pltpu.VMEM(theta.shape, F32),
            pltpu.VMEM((TILE, cols), F32), pltpu.VMEM(blocks, BF16),
        ),
        in_specs=[SMEM] * 3 + [VMEM] * 6,
        out_specs=(VMEM,) * 5,
        scratch_shapes=[pltpu.VMEM(theta.shape, F32)] * 2,
        compiler_params=PARAMS,
        name="middle",
    )(land_mask, fold_partner, sources, columns, points, start, weights, first, near)
    second = exchange(out, ("ew", "ns"))
    field, flux = pl.pallas_call(
        last_kernel,
        out_shape=(shape(theta.shape, F32), shape((fields, rows, cols), F32)),
        in_specs=[SMEM] + [VMEM] * 9,
        out_specs=(HBM, HBM),
        scratch_shapes=[
            pltpu.VMEM(theta.shape, F32), pltpu.VMEM((fields, rows, cols), F32), pltpu.VMEM(theta.shape, F32),
            pltpu.VMEM((levels, 3 * TILE, cols), F32), pltpu.VMEM((levels, TILE, cols), F32),
            pltpu.SemaphoreType.DMA((2,)),
        ],
        compiler_params=PARAMS,
        name="last",
    )(fold_partner, field, points, total, after, ends, force, first, second, near)
    return field, flux.reshape(1, 1, fields, rows * cols)


def solution(mesh):
    return jax.shard_map(
        local,
        mesh=mesh,
        in_specs=(
            P(None, "ns", "ew"),
            P(None, None, "ns", "ew"),
            P(None, "ns", "ew"),
            P("ns", "ew"),
            P("ew"),
            P("ns", "ew", None, None),
            P("ns", "ew", None),
            P("ns", "ew", None, None, None),
        ),
        out_specs=(P(None, "ns", "ew"), P("ns", "ew", None, None)),
        check_vma=False,
    )
```

```python
import functools

import jax
import jax.numpy as jnp
from jax import lax
from jax.experimental import pallas as pl
from jax.experimental.pallas import tpu as pltpu
from jax.sharding import PartitionSpec as P

COEFS = (0.5, -0.3, 0.2, 0.4, -0.25, 0.35)
VMEM = pl.BlockSpec(memory_space=pltpu.VMEM)
SMEM = pl.BlockSpec(memory_space=pltpu.SMEM)
HBM = pl.BlockSpec(memory_space=pltpu.HBM)
PARAMS = pltpu.CompilerParams(vmem_limit_bytes=16 * 1024 * 1024)
F32 = jnp.float32
BF16 = jnp.bfloat16
KINDS = 6
TILE = 8
FORCE_SLOT, WET_SLOT, PARTNER_SLOT = 4, 5, 4


def tendency(t, east, west, north, south, u, v, d):
    return d * (east + west + north + south - 4.0 * t) - 0.5 * (u * (east - west) + v * (north - south))


def stencil(t, *others):
    return t + tendency(t, *others)


class Place:
    def __init__(self):
        self.count, self.block_rows = lax.axis_size("ew"), lax.axis_size("ns")
        self.devices = self.count * self.block_rows
        self.e, self.n = lax.axis_index("ew"), lax.axis_index("ns")
        self.top = self.block_rows - 1
        self.is_top = self.n == self.top
        self.has_south = self.n > 0
        self.even = (self.n & 1) == 0
        self.east, self.west = self.wrap(self.e + 1), self.wrap(self.e + self.count - 1)
        self.above = jnp.minimum(self.n + 1, self.top)
        self.below = jnp.maximum(self.n - 1, 0)
        self.pair = jnp.where(self.even, self.n + 1, self.n - 1)
        self.other = jnp.where(self.even, self.below, self.above)

    def wrap(self, e):
        return jnp.where(e >= self.count, e - self.count, e)

    def slot(self, e, n):
        return n * self.count + e


def relays(row, block_rows):
    is_top = row == block_rows - 1
    odd = row & 1
    first = jnp.where((odd == 0) | is_top, jnp.maximum(row - 2, 0), row + 2)
    return first, jnp.where(is_top, jnp.maximum(row - 3, 0), row + 1 - 2 * odd), jnp.where(is_top, 0, 2)


def fill(size, rows):
    parts, at = [], 0
    for index in sorted(rows):
        if index > at:
            parts.append(jnp.zeros((index - at, size), F32))
        parts.append(rows[index])
        at = index + 1
    if at < size:
        parts.append(jnp.zeros((size - at, size), F32))
    return jnp.concatenate(parts, axis=0)


def turn(field):
    return field.reshape(field.shape[0] * field.shape[1], field.shape[2]).T


def row_of(ref, row):
    levels, rows, cols = ref.shape
    return ref.reshape(levels * rows, cols), pl.ds(row, levels, stride=rows)


def read_row(ref, row):
    flat, at = row_of(ref, row)
    return flat[at, :]


def write_row(ref, row, values):
    flat, at = row_of(ref, row)
    flat[at, :] = values


def shifted(field, axis, back):
    size = field.shape[axis]
    return pltpu.roll(field, size - 1 if back else 1, axis)


def bring_kernel(count, *refs):
    copies = [pltpu.make_async_copy(refs[i], refs[count + i], refs[-1].at[i]) for i in range(count)]
    for copy in copies:
        copy.start()
    for copy in copies:
        copy.wait()


def bring(arrays, memories, room, name):
    return pl.pallas_call(
        functools.partial(bring_kernel, len(arrays)),
        out_shape=tuple(memory(x.shape, x.dtype) for x, memory in zip(arrays, memories)),
        in_specs=[HBM] * len(arrays),
        out_specs=tuple(VMEM if memory is pltpu.VMEM else SMEM for memory in memories),
        scratch_shapes=[pltpu.SemaphoreType.DMA((len(arrays),))],
        compiler_params=pltpu.CompilerParams(vmem_limit_bytes=room),
        cost_estimate=pl.CostEstimate(flops=2**20, bytes_accessed=2**22, transcendentals=0),
        name=name,
    )(*arrays)


def first_kernel(partner_ref, theta_ref, vel_ref, diff_ref, atm_ref, out_ref, near_ref, bulk_ref):
    here = Place()
    levels, rows, cols = theta_ref.shape
    tiles = levels // TILE
    each = KINDS * tiles
    coef_refs = [vel_ref.at[0], vel_ref.at[1], diff_ref]
    turned = turn(theta_ref[...])
    strips = []
    for step in (1, -1):
        edge = rows - 1 if step < 0 else 0
        outer, t, inner = [read_row(theta_ref, edge + k * step) for k in range(3)]
        north, south = (outer, inner) if step < 0 else (inner, outer)
        coef = [read_row(ref, edge + step) for ref in coef_refs]
        tend = tendency(t, shifted(t, 1, True), shifted(t, 1, False), north, south, *coef)
        strips.append([outer, t, tend] + [read_row(ref, edge) for ref in coef_refs])
    for kind, (low, high) in enumerate(zip(*strips)):
        near_ref[kind] = jnp.where(here.even, high, low)
        far = jnp.where(here.even, low, high)
        bulk_ref[pl.ds(kind * tiles, tiles)] = far.reshape(tiles, TILE, cols)
    partner = partner_ref[0].astype(F32)
    fold_ref = bulk_ref.at[pl.ds(levels, levels)]
    for kind in range(KINDS):
        write_row(fold_ref, kind, strips[1][kind])
    write_row(fold_ref, KINDS, jnp.full((levels, cols), partner))
    write_row(fold_ref, KINDS + 1, jnp.zeros((levels, cols), F32))
    lane = lax.broadcasted_iota(jnp.int32, (TILE, cols), 1)
    slot = lane & 7
    spots = [turned[0:1], turned[1:2], turned[cols - 2 : cols - 1], turned[cols - 1 : cols]]
    spots = jnp.concatenate(spots + [jnp.zeros((TILE - 4, cols), F32)], axis=0)
    spots = jnp.where(here.even, spots, pltpu.roll(spots, cols - rows + 1, 1))
    corner = jnp.where(slot[0:1] == PARTNER_SLOT, partner, 0.0)
    for k in range(4):
        moved = pltpu.roll(spots, k, 1) if k else spots
        corner = jnp.where(slot[0:1] == k, moved[k : k + 1], corner)
    atm = atm_ref[...].astype(F32)
    to_west = jnp.concatenate([corner, turned[0:1], atm], axis=0)
    to_east = jnp.concatenate([corner, turned[cols - 1 : cols], atm], axis=0)
    column = jnp.where(here.is_top, partner_ref[0], here.e)
    first, second, skip = relays(jnp.where(here.is_top, here.top, here.other), here.block_rows)
    begin = jnp.where(here.is_top, levels, 0)
    for e in range(here.count):
        ahead = here.wrap(e - column + here.count)
        out_ref[here.slot(e, first)] = bulk_ref[begin + jnp.minimum(ahead, TILE - 1)].astype(BF16)
        out_ref[here.slot(e, second)] = bulk_ref[begin + jnp.minimum(ahead + TILE - skip, levels - 1)].astype(BF16)
    to_west, to_east = to_west.astype(BF16), to_east.astype(BF16)
    out_ref[here.slot(here.e, here.other)] = to_west
    for e in range(here.count):
        out_ref[here.slot(e, here.n)] = to_west
    out_ref[here.slot(here.east, here.n)] = to_east


def side_kernel(
    mask_ref, theta_ref, vel_ref, diff_ref, points_ref, columns_ref, start_ref
):
    levels, rows, cols = theta_ref.shape
    last = rows - 1
    wet = mask_ref[0, 0].astype(F32)
    u, v, d = wet * vel_ref[0], wet * vel_ref[1], wet * diff_ref[...]
    turned = [turn(u), turn(v), turn(d)]
    for side, at in enumerate((0, cols - 1)):
        for k in range(3):
            columns_ref[side, k : k + 1, :] = turned[k][at : at + 1]
    center, east, west, north, south = 1.0 - 4.0 * d, d - 0.5 * u, d + 0.5 * u, d - 0.5 * v, d + 0.5 * v
    for k, field in enumerate((center, east, west, north, south)):
        points_ref[k] = field
    t = theta_ref[...]
    lane = lax.broadcasted_iota(jnp.int32, t.shape, 2)
    line = lax.broadcasted_iota(jnp.int32, t.shape, 1)
    inner = center * t
    inner = inner + east * jnp.where(lane == cols - 1, 0.0, shifted(t, 2, True))
    inner = inner + west * jnp.where(lane == 0, 0.0, shifted(t, 2, False))
    inner = inner + north * jnp.where(line == last, 0.0, shifted(t, 1, True))
    inner = inner + south * jnp.where(line == 0, 0.0, shifted(t, 1, False))
    start_ref[...] = inner


def middle_kernel(
    mask_ref, partner_ref, src_ref, columns_ref, points_ref, start_ref, weights_ref, recv_ref, near_ref,
    total_ref, force_ref, next_ref, ends_ref, out_ref, beyond_ref, plain_ref,
):
    here = Place()
    levels, rows, cols = start_ref.shape
    fields = total_ref.shape[0]
    last = rows - 1
    wet = mask_ref[0, 0].astype(F32)

    pairs, cells, points = weights_ref.shape
    chosen = [recv_ref[here.slot(src_ref[0, pair], here.n)][TILE - fields :] for pair in range(pairs)]
    weights = weights_ref[...].reshape(pairs * cells, points)
    total = jnp.dot(jnp.concatenate(chosen, axis=1), weights, preferred_element_type=F32)
    total_ref[...] = total
    force = jnp.zeros((1, points), F32)
    for k in range(fields):
        force = force + COEFS[k] * total[k : k + 1]
    force = jnp.concatenate([force[:, r * cols : (r + 1) * cols] for r in range(rows)], axis=0)
    force = wet * (0.1 * force)
    force_ref[...] = force

    shape = start_ref.shape
    level = lax.broadcasted_iota(jnp.int32, shape, 0)

    def got(e, n):
        return recv_ref[here.slot(e, n)].astype(F32)

    sides = fill(cols, {0: got(here.west, here.n)[1:2], cols - 1: got(here.east, here.n)[1:2]}).T.reshape(shape)
    from_fold, over, under = got(partner_ref[0], here.n)[0:1], got(here.e, here.above)[0:1], got(here.e, here.below)[0:1]
    facing = jnp.where(here.is_top, from_fold, jnp.where(here.even, under, over))
    facing = jnp.broadcast_to(facing, (TILE, cols))
    facing = [facing[0:1]] + [pltpu.roll(facing, cols - k, 1)[0:1] for k in range(1, 4)]
    facing = [jnp.where(here.is_top, facing[3 - k], facing[k]) for k in range(4)]
    spots = (0, 1, cols - 2, cols - 1)
    beyond_ref[...] = fill(cols, dict(zip(spots, facing))).T.reshape(shape)
    far = read_row(beyond_ref, 0)
    above = jnp.where(here.even, near_ref[0], far)
    below = jnp.where(here.has_south, jnp.where(here.even, far, near_ref[0]), 0.0)
    lane = lax.broadcasted_iota(jnp.int32, shape, 2)
    rim = jnp.where(lane == cols - 1, points_ref[1], jnp.where(lane == 0, points_ref[2], 0.0))
    plain_ref[...] = start_ref[...] + rim * sides
    write_row(plain_ref, last, read_row(plain_ref, last) + read_row(points_ref.at[3], last) * above)
    write_row(plain_ref, 0, read_row(plain_ref, 0) + read_row(points_ref.at[4], 0) * below)
    t = plain_ref[...]
    next_ref[...] = t + jnp.where(level == 0, force[None], 0.0)

    held = [got(m, here.top) for m in range(here.count)]
    size = -(-here.count * TILE // cols) * cols
    tiles = held + [jnp.zeros((size - here.count * TILE, cols), F32)] * (size > here.count * TILE)
    tiles = jnp.concatenate(tiles, axis=0).astype(BF16)
    partners = jnp.concatenate([jnp.broadcast_to(block[KINDS : KINDS + 1, 0:1], (TILE, 1)) for block in held], axis=0)
    wanted = TILE * partners + (lax.broadcasted_iota(jnp.int32, partners.shape, 0) & (TILE - 1)).astype(F32)
    pick = lax.broadcasted_iota(jnp.int32, (here.count * TILE, size), 1).astype(F32) == wanted
    folded = jnp.dot(pick.astype(F32).astype(BF16), tiles, preferred_element_type=F32)

    turned = turn(t) + jnp.concatenate([force, jnp.zeros((cols - rows, cols), F32)], axis=0).T
    ends = jnp.concatenate([turned[0:1], turned[cols - 1 : cols], jnp.zeros((TILE - 2, cols), F32)], axis=0)
    lane = lax.broadcasted_iota(jnp.int32, (TILE, cols), 1)
    forces = jnp.concatenate([force, jnp.zeros((cols - rows, cols), F32)], axis=0).T
    forces = jnp.concatenate([forces[0:1], forces[cols - 1 : cols], jnp.zeros((TILE - 2, cols), F32)], axis=0)
    ends_ref[...] = ends
    marks = jnp.take_along_axis(forces, lane >> 3, axis=1)
    slot = lane & 7
    marks = jnp.where(slot == FORCE_SLOT, marks, jnp.where(slot == WET_SLOT, wet, 0.0))
    slot = slot[0:1]

    def corners(shifts, mark):
        row = mark
        for index, shift in enumerate(shifts):
            moved = pltpu.roll(ends, shift % cols, 1) if shift else ends
            row = jnp.where(slot == index, moved[index // 2 : index // 2 + 1], row)
        return row

    up, down = (-last, 2 - last, 2 - last, 4 - last), (0, 0, 2, 2)
    low_mark, high_mark = marks[0:1], marks[1:2]
    low_coef, high_coef = columns_ref[0], columns_ref[1]
    high_force, low_force = [force[last : last + 1], force[last - 1 : last]], [force[0:1], force[1:2]]
    low, high = [turned[0:1], turned[1:2]], [turned[cols - 1 : cols], turned[cols - 2 : cols - 1]]
    base = jnp.concatenate([corners(up, low_mark)] + high_force + low + [low_coef], axis=0)
    to_east = jnp.concatenate([corners(up, high_mark)] + high_force + high + [high_coef], axis=0)
    to_below = jnp.concatenate([corners(down, low_mark)] + low_force + low + [low_coef], axis=0)
    for e in range(here.count):
        close = (e == here.e) | (e == here.east) | (e == here.west)
        for n in range(here.block_rows):
            begin = jnp.where(n == here.n - 1, to_below, jnp.where(e == here.east, to_east, base))
            owed = (n == here.n) | (close & ((n == here.n - 1) | (n == here.n + 1)))
            if n == here.top:
                tile = folded[e * TILE : (e + 1) * TILE]
            else:
                tile = got(e, max(n - 1, 0) if n % 2 == 0 else n + 1)
            out_ref[n * here.count + e] = jnp.where(owed, begin, tile).astype(BF16)


def last_kernel(
    partner_ref, theta_ref, points_ref, total_ref, next_ref, ends_ref, force_ref, first_ref, second_ref, near_ref,
    result_hbm, flux_hbm, result_ref, flux_ref, rim_ref, tall_ref, tile_ref, sems,
):
    here = Place()
    levels, rows, cols = theta_ref.shape
    last = rows - 1
    partner = partner_ref[0]
    is_top, has_south = here.is_top, here.has_south

    def got(e, n):
        return second_ref[here.slot(e, n)].astype(F32)

    west, east = got(here.west, here.n), got(here.east, here.n)
    over, under = got(here.e, here.above), got(here.e, here.below)
    fold = got(partner, here.n)
    fold_east = got(here.wrap(partner + 1), here.n)[0:1]
    fold_west = got(here.wrap(partner + here.count - 1), here.n)[0:1]
    over_west, over_east = got(here.west, here.above)[0:1], got(here.east, here.above)[0:1]
    under_west, under_east = got(here.west, here.below)[0:1], got(here.east, here.below)[0:1]
    first_west = first_ref[here.slot(here.west, here.n)].astype(F32)
    first_east = first_ref[here.slot(here.east, here.n)].astype(F32)

    def mark(block):
        return block[0:1, WET_SLOT : WET_SLOT + 1]

    first, second, skip = relays(here.n, here.block_rows)
    for k in range(levels):
        ahead, row = (k, first) if k < TILE else (k - TILE + skip, second)
        tile_ref[k] = got(here.wrap(here.e + jnp.minimum(ahead, here.count - 1)), row)
    tiles = levels // TILE
    far = [tile_ref[pl.ds(kind * tiles, tiles)].reshape(levels, cols) for kind in range(KINDS)]
    far = jnp.concatenate(far, axis=0)
    mirrored = jnp.concatenate([read_row(tile_ref, kind) for kind in range(KINDS)], axis=0)
    mirror = cols - 1 - lax.broadcasted_iota(jnp.int32, far.shape, 1)
    far = jnp.where(is_top, jnp.take_along_axis(mirrored, mirror, axis=1), far)
    far = [far[kind * levels : (kind + 1) * levels] for kind in range(KINDS)]
    near = [near_ref[kind] for kind in range(KINDS)]
    north = [jnp.where(here.even, a, b) for a, b in zip(near, far)]
    south = [jnp.where(has_south, jnp.where(here.even, b, a), 0.0) for a, b in zip(near, far)]

    def kinds(strip, wet, sign):
        t, inner, tend, u, v, d = strip
        return t, inner, inner + wet * tend, (sign * wet) * u, (sign * wet) * v, wet * d

    north = kinds(north, jnp.where(is_top, mark(fold), mark(over)), jnp.where(is_top, -1.0, 1.0))
    south = kinds(south, mark(under), 1.0)

    top_west, top_east = jnp.zeros((1, cols), F32), jnp.zeros((1, cols), F32)
    for s in range(here.count):
        row = got(s, here.n)[0:1]
        top_west = jnp.where(first_west[0:1, PARTNER_SLOT : PARTNER_SLOT + 1] == float(s), row, top_west)
        top_east = jnp.where(first_east[0:1, PARTNER_SLOT : PARTNER_SLOT + 1] == float(s), row, top_east)
    moved = [fold[0:1], over[0:1], under[0:1], fold_west, over_west, under_west, top_east]
    moved = jnp.concatenate(moved + [jnp.zeros((1, cols), F32)], axis=0)
    moved = pltpu.roll(moved, cols - 2, 1)
    def pair(low, high):
        return jnp.concatenate([low, high, jnp.zeros((TILE - 2, cols), F32)], axis=0)

    along = lax.broadcasted_iota(jnp.int32, (TILE, cols), 1)
    place = along & 7
    side = pair(west[3:4], east[3:4])
    corner = pair(jnp.where(is_top, top_west, moved[4:5]), jnp.where(is_top, moved[6:7], over_east))
    side_north = jnp.where(place == last, pltpu.roll(corner, last, 1), shifted(side, 1, True))
    corner = jnp.where(has_south, pair(moved[5:6], under_east), 0.0)
    side_south = jnp.where(place == 0, corner, shifted(side, 1, False))
    side_force = jnp.take_along_axis(pair(west[0:1], east[0:1]), jnp.where(along < rows, 8 * along, 0) + FORCE_SLOT, axis=1)
    side_next = stencil(
        side, pair(ends_ref[0:1], east[4:5]), pair(west[4:5], ends_ref[1:2]), side_north, side_south,
        *[pair(west[k : k + 1], east[k : k + 1]) for k in (5, 6, 7)],
    ) + jnp.where(along < rows, side_force, 0.0)

    listed = [
        (west[3:4], east[3:4]),
        (side_next[0:1], side_next[1:2]),
        (jnp.where(is_top, moved[0:1], over[0:1]), jnp.where(is_top, fold[0:1], moved[1:2])),
        (under[0:1], moved[2:3]),
        (jnp.where(is_top, fold_east, moved[4:5]), jnp.where(is_top, moved[3:4], over_east)),
        (moved[5:6], under_east),
    ]
    lanes = {}
    for q, (low, high) in enumerate(listed):
        lanes[2 * q], lanes[(2 * q - 1) % cols] = low, high
    rim = fill(cols, lanes).T.reshape(theta_ref.shape)
    rim_ref[...] = rim

    def listing(q, field):
        return pltpu.roll(field, cols - 2 * q, field.ndim - 1) if q else field

    edges, inners = read_row(rim_ref, 0), read_row(rim_ref, 1)
    lane = lax.broadcasted_iota(jnp.int32, (levels, cols), 1)
    level = lax.broadcasted_iota(jnp.int32, (levels, cols), 0)
    ends = (lane == 0) | (lane == cols - 1)

    def forced(row, force):
        return row + jnp.where(level == 0, force, 0.0)

    flip = cols - 1 - lax.broadcasted_iota(jnp.int32, (8, cols), 1)
    flipped = jnp.take_along_axis(fold[:TILE], flip, axis=1)
    north_force = [jnp.where(is_top, flipped[k : k + 1], over[k : k + 1]) for k in (1, 2)]
    south_force = [under[1:2], under[2:3]]

    def beyond(rows_of, inside, outward, force, q):
        edge_row = stencil(
            rows_of[0], shifted(rows_of[0], 1, True), shifted(rows_of[0], 1, False),
            rows_of[1] if outward else inside, inside if outward else rows_of[1], *rows_of[3:],
        )
        edge_row = jnp.where(ends, listing(q, edges), forced(edge_row, force[0]))
        return edge_row, jnp.where(ends, listing(q, inners), forced(rows_of[2], force[1]))

    north_one, north_two = beyond(north, read_row(theta_ref, last), True, north_force, 2)
    south_one, south_two = beyond(south, read_row(theta_ref, 0), False, south_force, 3)
    south_one, south_two = jnp.where(has_south, south_one, 0.0), jnp.where(has_south, south_two, 0.0)
    shape = theta_ref.shape
    wide = lax.broadcasted_iota(jnp.int32, shape, 2)
    force = jnp.where(lax.broadcasted_iota(jnp.int32, shape, 0) == 0, force_ref[...][None], 0.0)
    inside = (lane >= 2) & (lane < cols - 2)
    more_north, more_south = inside & jnp.logical_not(here.even), inside & here.even
    top_row = read_row(next_ref, last) + jnp.where(more_north, read_row(points_ref.at[3], last) * north[0], 0.0)
    bottom_row = read_row(next_ref, 0) + jnp.where(more_south, read_row(points_ref.at[4], 0) * south[0], 0.0)
    tall_ref[:, TILE : 2 * TILE, :] = next_ref[...]
    write_row(tall_ref, TILE + last, top_row)
    write_row(tall_ref, TILE, bottom_row)

    def outer(row, further, inside, outward, rows_of, force_row, diagonal):
        result = stencil(
            row, jnp.where(lane == cols - 1, diagonal, shifted(row, 1, True)),
            jnp.where(lane == 0, diagonal, shifted(row, 1, False)),
            further if outward else inside, inside if outward else further, *rows_of[3:],
        )
        return forced(result, force_row)

    north_next = outer(north_one, north_two, top_row, True, north, north_force[0], listing(4, edges))
    south_next = outer(south_one, south_two, bottom_row, False, south, south_force[0], listing(5, edges))
    south_next = jnp.where(has_south, south_next, 0.0)

    def advance(sides, above, below):
        write_row(tall_ref, 2 * TILE, above)
        write_row(tall_ref, TILE - 1, below)
        t = tall_ref[:, TILE : 2 * TILE, :]
        east = jnp.where(wide == cols - 1, sides, shifted(t, 2, True))
        west = jnp.where(wide == 0, sides, shifted(t, 2, False))
        north, south = tall_ref[:, TILE + 1 : 2 * TILE + 1, :], tall_ref[:, TILE - 1 : 2 * TILE - 1, :]
        result = force
        for k, field in enumerate((t, east, west, north, south)):
            result = result + points_ref[k] * field
        return result

    tall_ref[:, TILE : 2 * TILE, :] = advance(rim, north_one, south_one)
    for k in range(flux_ref.shape[0]):
        for r in range(rows):
            flux_ref[k, r : r + 1, :] = total_ref[k : k + 1, r * cols : (r + 1) * cols]
    copies = [pltpu.make_async_copy(flux_ref, flux_hbm, sems.at[0])]
    copies[0].start()
    t = advance(listing(1, rim), north_next, south_next)
    for half in range(2):
        part = pl.ds(half * (levels // 2), levels // 2)
        result_ref[part] = t[half * (levels // 2) : (half + 1) * (levels // 2)]
        copies.append(pltpu.make_async_copy(result_ref.at[part], result_hbm.at[part], sems.at[1 + half]))
        copies[-1].start()
    for copy in copies:
        copy.wait()


def exchange(blocks):
    return lax.all_to_all(blocks, ("ns", "ew"), split_axis=0, concat_axis=0, tiled=True)


def swap(rows):
    pairs = [(i, i + 1) for i in range(0, lax.axis_size("ns"), 2)]
    return lax.ppermute(rows, "ns", pairs + [(b, a) for a, b in pairs])


def local(theta, velocity, diffusivity, land_mask, fold_partner, atm_flux, remap_src, remap_weights):
    levels, rows, cols = theta.shape
    fields = atm_flux.shape[2]
    shape = jax.ShapeDtypeStruct
    devices = lax.axis_size("ew") * lax.axis_size("ns")
    blocks = (devices, TILE, cols)
    room = 60 * 2**20 - 2 * max(0, 4 * devices * TILE * cols - 2**20)
    weights = remap_weights[0, 0]
    field, velocity, diffusivity, flux = bring(
        [theta, velocity, diffusivity, atm_flux[0, 0]], [pltpu.VMEM] * 4, room, "bring"
    )
    out, near = pl.pallas_call(
        first_kernel,
        out_shape=(pltpu.VMEM(blocks, BF16), pltpu.VMEM((KINDS, levels, cols), F32)),
        in_specs=[SMEM] + [VMEM] * 4,
        out_specs=(VMEM,) * 2,
        scratch_shapes=[pltpu.VMEM((2 * levels, TILE, cols), F32)],
        compiler_params=PARAMS,
        name="first",
    )(fold_partner, field, velocity, diffusivity, flux)
    first, near = exchange(out), swap(near)
    sources, weights = bring([remap_src[0], weights], [pltpu.SMEM, pltpu.VMEM], room, "load")
    points, columns, start = pl.pallas_call(
        side_kernel,
        out_shape=(
            pltpu.VMEM((5,) + theta.shape, F32), pltpu.VMEM((2, 3, cols), F32), pltpu.VMEM(theta.shape, F32),
        ),
        in_specs=[SMEM] + [VMEM] * 3,
        out_specs=(VMEM,) * 3,
        compiler_params=PARAMS,
        cost_estimate=pl.CostEstimate(flops=2**20, bytes_accessed=2**20, transcendentals=0),
        name="side",
    )(land_mask, field, velocity, diffusivity)
    total, force, after, ends, out = pl.pallas_call(
        middle_kernel,
        out_shape=(
            pltpu.VMEM((fields, rows * cols), F32), pltpu.VMEM((rows, cols), F32), pltpu.VMEM(theta.shape, F32),
            pltpu.VMEM((TILE, cols), F32), pltpu.VMEM(blocks, BF16),
        ),
        in_specs=[SMEM] * 3 + [VMEM] * 6,
        out_specs=(VMEM,) * 5,
        scratch_shapes=[pltpu.VMEM(theta.shape, F32)] * 2,
        compiler_params=PARAMS,
        name="middle",
    )(land_mask, fold_partner, sources, columns, points, start, weights, first, near)
    second = exchange(out)
    field, flux = pl.pallas_call(
        last_kernel,
        out_shape=(shape(theta.shape, F32), shape((fields, rows, cols), F32)),
        in_specs=[SMEM] + [VMEM] * 9,
        out_specs=(HBM, HBM),
        scratch_shapes=[
            pltpu.VMEM(theta.shape, F32), pltpu.VMEM((fields, rows, cols), F32), pltpu.VMEM(theta.shape, F32),
            pltpu.VMEM((levels, 3 * TILE, cols), F32), pltpu.VMEM((levels, TILE, cols), F32),
            pltpu.SemaphoreType.DMA((3,)),
        ],
        compiler_params=PARAMS,
        name="last",
    )(fold_partner, field, points, total, after, ends, force, first, second, near)
    return field, flux.reshape(1, 1, fields, rows * cols)


def solution(mesh):
    return jax.shard_map(
        local,
        mesh=mesh,
        in_specs=(
            P(None, "ns", "ew"),
            P(None, None, "ns", "ew"),
            P(None, "ns", "ew"),
            P("ns", "ew"),
            P("ew"),
            P("ns", "ew", None, None),
            P("ns", "ew", None),
            P("ns", "ew", None, None, None),
        ),
        out_specs=(P(None, "ns", "ew"), P("ns", "ew", None, None)),
        check_vma=False,
    )
```

```python
import functools

import jax
import jax.numpy as jnp
from jax import lax
from jax.experimental import pallas as pl
from jax.experimental.pallas import tpu as pltpu
from jax.sharding import PartitionSpec as P

COEFS = (0.5, -0.3, 0.2, 0.4, -0.25, 0.35)
VMEM = pl.BlockSpec(memory_space=pltpu.VMEM)
SMEM = pl.BlockSpec(memory_space=pltpu.SMEM)
HBM = pl.BlockSpec(memory_space=pltpu.HBM)
PARAMS = pltpu.CompilerParams(vmem_limit_bytes=16 * 1024 * 1024)
F32 = jnp.float32
BF16 = jnp.bfloat16
KINDS = 6
TILE = 8
FORCE_SLOT, WET_SLOT, PARTNER_SLOT = 4, 5, 4


def tendency(t, east, west, north, south, u, v, d):
    return d * (east + west + north + south - 4.0 * t) - 0.5 * (u * (east - west) + v * (north - south))


def stencil(t, *others):
    return t + tendency(t, *others)


class Place:
    def __init__(self):
        self.count, self.block_rows = lax.axis_size("ew"), lax.axis_size("ns")
        self.devices = self.count * self.block_rows
        self.e, self.n = lax.axis_index("ew"), lax.axis_index("ns")
        self.top = self.block_rows - 1
        self.is_top = self.n == self.top
        self.has_south = self.n > 0
        self.even = (self.n & 1) == 0
        self.east, self.west = self.wrap(self.e + 1), self.wrap(self.e + self.count - 1)
        self.above = jnp.minimum(self.n + 1, self.top)
        self.below = jnp.maximum(self.n - 1, 0)
        self.pair = jnp.where(self.even, self.n + 1, self.n - 1)
        self.other = jnp.where(self.even, self.below, self.above)

    def wrap(self, e):
        return jnp.where(e >= self.count, e - self.count, e)

    def slot(self, e, n):
        return n * self.count + e


def relays(row, block_rows):
    is_top = row == block_rows - 1
    odd = row & 1
    first = jnp.where((odd == 0) | is_top, jnp.maximum(row - 2, 0), row + 2)
    return first, jnp.where(is_top, jnp.maximum(row - 3, 0), row + 1 - 2 * odd), jnp.where(is_top, 0, 2)


def fill(size, rows):
    parts, at = [], 0
    for index in sorted(rows):
        if index > at:
            parts.append(jnp.zeros((index - at, size), F32))
        parts.append(rows[index])
        at = index + 1
    if at < size:
        parts.append(jnp.zeros((size - at, size), F32))
    return jnp.concatenate(parts, axis=0)


def turn(field):
    return field.reshape(field.shape[0] * field.shape[1], field.shape[2]).T


def row_of(ref, row):
    levels, rows, cols = ref.shape
    return ref.reshape(levels * rows, cols), pl.ds(row, levels, stride=rows)


def read_row(ref, row):
    flat, at = row_of(ref, row)
    return flat[at, :]


def write_row(ref, row, values):
    flat, at = row_of(ref, row)
    flat[at, :] = values


def shifted(field, axis, back):
    size = field.shape[axis]
    return pltpu.roll(field, size - 1 if back else 1, axis)


def bring_kernel(count, *refs):
    copies = [pltpu.make_async_copy(refs[i], refs[count + i], refs[-1].at[i]) for i in range(count)]
    for copy in copies:
        copy.start()
    for copy in copies:
        copy.wait()


def bring(arrays, memories, room, name):
    return pl.pallas_call(
        functools.partial(bring_kernel, len(arrays)),
        out_shape=tuple(memory(x.shape, x.dtype) for x, memory in zip(arrays, memories)),
        in_specs=[HBM] * len(arrays),
        out_specs=tuple(VMEM if memory is pltpu.VMEM else SMEM for memory in memories),
        scratch_shapes=[pltpu.SemaphoreType.DMA((len(arrays),))],
        compiler_params=pltpu.CompilerParams(vmem_limit_bytes=room),
        cost_estimate=pl.CostEstimate(flops=2**20, bytes_accessed=2**22, transcendentals=0),
        name=name,
    )(*arrays)


def first_kernel(partner_ref, theta_ref, vel_ref, diff_ref, atm_ref, out_ref, near_ref, bulk_ref):
    here = Place()
    levels, rows, cols = theta_ref.shape
    tiles = levels // TILE
    each = KINDS * tiles
    coef_refs = [vel_ref.at[0], vel_ref.at[1], diff_ref]
    turned = turn(theta_ref[...])
    strips = []
    for step in (1, -1):
        edge = rows - 1 if step < 0 else 0
        outer, t, inner = [read_row(theta_ref, edge + k * step) for k in range(3)]
        north, south = (outer, inner) if step < 0 else (inner, outer)
        coef = [read_row(ref, edge + step) for ref in coef_refs]
        tend = tendency(t, shifted(t, 1, True), shifted(t, 1, False), north, south, *coef)
        strips.append([outer, t, tend] + [read_row(ref, edge) for ref in coef_refs])
    for kind, (low, high) in enumerate(zip(*strips)):
        near_ref[kind] = jnp.where(here.even, high, low)
        far = jnp.where(here.even, low, high)
        bulk_ref[pl.ds(kind * tiles, tiles)] = far.reshape(tiles, TILE, cols)
    partner = partner_ref[0].astype(F32)
    fold_ref = bulk_ref.at[pl.ds(levels, levels)]
    for kind in range(KINDS):
        write_row(fold_ref, kind, strips[1][kind])
    write_row(fold_ref, KINDS, jnp.full((levels, cols), partner))
    write_row(fold_ref, KINDS + 1, jnp.zeros((levels, cols), F32))
    lane = lax.broadcasted_iota(jnp.int32, (TILE, cols), 1)
    slot = lane & 7
    spots = [turned[0:1], turned[1:2], turned[cols - 2 : cols - 1], turned[cols - 1 : cols]]
    spots = jnp.concatenate(spots + [jnp.zeros((TILE - 4, cols), F32)], axis=0)
    spots = jnp.where(here.even, spots, pltpu.roll(spots, cols - rows + 1, 1))
    corner = jnp.where(slot[0:1] == PARTNER_SLOT, partner, 0.0)
    for k in range(4):
        moved = pltpu.roll(spots, k, 1) if k else spots
        corner = jnp.where(slot[0:1] == k, moved[k : k + 1], corner)
    atm = atm_ref[...].astype(F32)
    to_west = jnp.concatenate([corner, turned[0:1], atm], axis=0)
    to_east = jnp.concatenate([corner, turned[cols - 1 : cols], atm], axis=0)
    column = jnp.where(here.is_top, partner_ref[0], here.e)
    first, second, skip = relays(jnp.where(here.is_top, here.top, here.other), here.block_rows)
    begin = jnp.where(here.is_top, levels, 0)
    for e in range(here.count):
        ahead = here.wrap(e - column + here.count)
        out_ref[here.slot(e, first)] = bulk_ref[begin + jnp.minimum(ahead, TILE - 1)].astype(BF16)
        out_ref[here.slot(e, second)] = bulk_ref[begin + jnp.minimum(ahead + TILE - skip, levels - 1)].astype(BF16)
    to_west, to_east = to_west.astype(BF16), to_east.astype(BF16)
    out_ref[here.slot(here.e, here.other)] = to_west
    for e in range(here.count):
        out_ref[here.slot(e, here.n)] = to_west
    out_ref[here.slot(here.east, here.n)] = to_east


def side_kernel(
    mask_ref, theta_ref, vel_ref, diff_ref, points_ref, columns_ref, start_ref
):
    levels, rows, cols = theta_ref.shape
    last = rows - 1
    wet = mask_ref[0, 0].astype(F32)
    u, v, d = wet * vel_ref[0], wet * vel_ref[1], wet * diff_ref[...]
    turned = [turn(u), turn(v), turn(d)]
    for side, at in enumerate((0, cols - 1)):
        for k in range(3):
            columns_ref[side, k : k + 1, :] = turned[k][at : at + 1]
    center, east, west, north, south = 1.0 - 4.0 * d, d - 0.5 * u, d + 0.5 * u, d - 0.5 * v, d + 0.5 * v
    for k, field in enumerate((center, east, west, north, south)):
        points_ref[k] = field
    t = theta_ref[...]
    lane = lax.broadcasted_iota(jnp.int32, t.shape, 2)
    line = lax.broadcasted_iota(jnp.int32, t.shape, 1)
    inner = center * t
    inner = inner + east * jnp.where(lane == cols - 1, 0.0, shifted(t, 2, True))
    inner = inner + west * jnp.where(lane == 0, 0.0, shifted(t, 2, False))
    inner = inner + north * jnp.where(line == last, 0.0, shifted(t, 1, True))
    inner = inner + south * jnp.where(line == 0, 0.0, shifted(t, 1, False))
    start_ref[...] = inner


def middle_kernel(
    mask_ref, partner_ref, src_ref, columns_ref, points_ref, start_ref, weights_ref, recv_ref, near_ref,
    total_ref, force_ref, next_ref, ends_ref, out_ref, beyond_ref, plain_ref,
):
    here = Place()
    levels, rows, cols = start_ref.shape
    fields = total_ref.shape[0]
    last = rows - 1
    wet = mask_ref[0, 0].astype(F32)

    pairs, cells, points = weights_ref.shape
    chosen = [recv_ref[here.slot(src_ref[0, pair], here.n)][TILE - fields :] for pair in range(pairs)]
    weights = weights_ref[...].reshape(pairs * cells, points)
    total = jnp.dot(jnp.concatenate(chosen, axis=1), weights, preferred_element_type=F32)
    total_ref[...] = total
    force = jnp.zeros((1, points), F32)
    for k in range(fields):
        force = force + COEFS[k] * total[k : k + 1]
    force = jnp.concatenate([force[:, r * cols : (r + 1) * cols] for r in range(rows)], axis=0)
    force = wet * (0.1 * force)
    force_ref[...] = force

    shape = start_ref.shape
    level = lax.broadcasted_iota(jnp.int32, shape, 0)

    def got(e, n):
        return recv_ref[here.slot(e, n)].astype(F32)

    sides = fill(cols, {0: got(here.west, here.n)[1:2], cols - 1: got(here.east, here.n)[1:2]}).T.reshape(shape)
    from_fold, over, under = got(partner_ref[0], here.n)[0:1], got(here.e, here.above)[0:1], got(here.e, here.below)[0:1]
    facing = jnp.where(here.is_top, from_fold, jnp.where(here.even, under, over))
    facing = jnp.broadcast_to(facing, (TILE, cols))
    facing = [facing[0:1]] + [pltpu.roll(facing, cols - k, 1)[0:1] for k in range(1, 4)]
    facing = [jnp.where(here.is_top, facing[3 - k], facing[k]) for k in range(4)]
    spots = (0, 1, cols - 2, cols - 1)
    beyond_ref[...] = fill(cols, dict(zip(spots, facing))).T.reshape(shape)
    far = read_row(beyond_ref, 0)
    above = jnp.where(here.even, near_ref[0], far)
    below = jnp.where(here.has_south, jnp.where(here.even, far, near_ref[0]), 0.0)
    lane = lax.broadcasted_iota(jnp.int32, shape, 2)
    rim = jnp.where(lane == cols - 1, points_ref[1], jnp.where(lane == 0, points_ref[2], 0.0))
    plain_ref[...] = start_ref[...] + rim * sides
    write_row(plain_ref, last, read_row(plain_ref, last) + read_row(points_ref.at[3], last) * above)
    write_row(plain_ref, 0, read_row(plain_ref, 0) + read_row(points_ref.at[4], 0) * below)
    t = plain_ref[...]
    next_ref[...] = t + jnp.where(level == 0, force[None], 0.0)

    held = [got(m, here.top) for m in range(here.count)]
    size = -(-here.count * TILE // cols) * cols
    tiles = held + [jnp.zeros((size - here.count * TILE, cols), F32)] * (size > here.count * TILE)
    tiles = jnp.concatenate(tiles, axis=0).astype(BF16)
    partners = jnp.concatenate([jnp.broadcast_to(block[KINDS : KINDS + 1, 0:1], (TILE, 1)) for block in held], axis=0)
    wanted = TILE * partners + (lax.broadcasted_iota(jnp.int32, partners.shape, 0) & (TILE - 1)).astype(F32)
    pick = lax.broadcasted_iota(jnp.int32, (here.count * TILE, size), 1).astype(F32) == wanted
    folded = jnp.dot(pick.astype(F32).astype(BF16), tiles, preferred_element_type=F32)

    turned = turn(t) + jnp.concatenate([force, jnp.zeros((cols - rows, cols), F32)], axis=0).T
    ends = jnp.concatenate([turned[0:1], turned[cols - 1 : cols], jnp.zeros((TILE - 2, cols), F32)], axis=0)
    lane = lax.broadcasted_iota(jnp.int32, (TILE, cols), 1)
    forces = jnp.concatenate([force, jnp.zeros((cols - rows, cols), F32)], axis=0).T
    forces = jnp.concatenate([forces[0:1], forces[cols - 1 : cols], jnp.zeros((TILE - 2, cols), F32)], axis=0)
    ends_ref[...] = ends
    marks = jnp.take_along_axis(forces, lane >> 3, axis=1)
    slot = lane & 7
    marks = jnp.where(slot == FORCE_SLOT, marks, jnp.where(slot == WET_SLOT, wet, 0.0))
    slot = slot[0:1]

    def corners(shifts, mark):
        row = mark
        for index, shift in enumerate(shifts):
            moved = pltpu.roll(ends, shift % cols, 1) if shift else ends
            row = jnp.where(slot == index, moved[index // 2 : index // 2 + 1], row)
        return row

    up, down = (-last, 2 - last, 2 - last, 4 - last), (0, 0, 2, 2)
    low_mark, high_mark = marks[0:1], marks[1:2]
    low_coef, high_coef = columns_ref[0], columns_ref[1]
    high_force, low_force = [force[last : last + 1], force[last - 1 : last]], [force[0:1], force[1:2]]
    low, high = [turned[0:1], turned[1:2]], [turned[cols - 1 : cols], turned[cols - 2 : cols - 1]]
    base = jnp.concatenate([corners(up, low_mark)] + high_force + low + [low_coef], axis=0)
    to_east = jnp.concatenate([corners(up, high_mark)] + high_force + high + [high_coef], axis=0)
    to_below = jnp.concatenate([corners(down, low_mark)] + low_force + low + [low_coef], axis=0)
    for e in range(here.count):
        close = (e == here.e) | (e == here.east) | (e == here.west)
        for n in range(here.block_rows):
            begin = jnp.where(n == here.n - 1, to_below, jnp.where(e == here.east, to_east, base))
            owed = (n == here.n) | (close & ((n == here.n - 1) | (n == here.n + 1)))
            if n == here.top:
                tile = folded[e * TILE : (e + 1) * TILE]
            else:
                tile = got(e, max(n - 1, 0) if n % 2 == 0 else n + 1)
            out_ref[n * here.count + e] = jnp.where(owed, begin, tile).astype(BF16)


def last_kernel(
    partner_ref, theta_ref, points_ref, total_ref, next_ref, ends_ref, force_ref, first_ref, second_ref, near_ref,
    result_hbm, flux_hbm, result_ref, flux_ref, rim_ref, tall_ref, tile_ref, sems,
):
    here = Place()
    levels, rows, cols = theta_ref.shape
    last = rows - 1
    partner = partner_ref[0]
    is_top, has_south = here.is_top, here.has_south

    def got(e, n):
        return second_ref[here.slot(e, n)].astype(F32)

    west, east = got(here.west, here.n), got(here.east, here.n)
    over, under = got(here.e, here.above), got(here.e, here.below)
    fold = got(partner, here.n)
    fold_east = got(here.wrap(partner + 1), here.n)[0:1]
    fold_west = got(here.wrap(partner + here.count - 1), here.n)[0:1]
    over_west, over_east = got(here.west, here.above)[0:1], got(here.east, here.above)[0:1]
    under_west, under_east = got(here.west, here.below)[0:1], got(here.east, here.below)[0:1]
    first_west = first_ref[here.slot(here.west, here.n)].astype(F32)
    first_east = first_ref[here.slot(here.east, here.n)].astype(F32)

    def mark(block):
        return block[0:1, WET_SLOT : WET_SLOT + 1]

    first, second, skip = relays(here.n, here.block_rows)
    for k in range(levels):
        ahead, row = (k, first) if k < TILE else (k - TILE + skip, second)
        tile_ref[k] = got(here.wrap(here.e + jnp.minimum(ahead, here.count - 1)), row)
    tiles = levels // TILE
    far = [tile_ref[pl.ds(kind * tiles, tiles)].reshape(levels, cols) for kind in range(KINDS)]
    far = jnp.concatenate(far, axis=0)
    mirrored = jnp.concatenate([read_row(tile_ref, kind) for kind in range(KINDS)], axis=0)
    mirror = cols - 1 - lax.broadcasted_iota(jnp.int32, far.shape, 1)
    far = jnp.where(is_top, jnp.take_along_axis(mirrored, mirror, axis=1), far)
    far = [far[kind * levels : (kind + 1) * levels] for kind in range(KINDS)]
    near = [near_ref[kind] for kind in range(KINDS)]
    north = [jnp.where(here.even, a, b) for a, b in zip(near, far)]
    south = [jnp.where(has_south, jnp.where(here.even, b, a), 0.0) for a, b in zip(near, far)]

    def kinds(strip, wet, sign):
        t, inner, tend, u, v, d = strip
        return t, inner, inner + wet * tend, (sign * wet) * u, (sign * wet) * v, wet * d

    north = kinds(north, jnp.where(is_top, mark(fold), mark(over)), jnp.where(is_top, -1.0, 1.0))
    south = kinds(south, mark(under), 1.0)

    top_west, top_east = jnp.zeros((1, cols), F32), jnp.zeros((1, cols), F32)
    for s in range(here.count):
        row = got(s, here.n)[0:1]
        top_west = jnp.where(first_west[0:1, PARTNER_SLOT : PARTNER_SLOT + 1] == float(s), row, top_west)
        top_east = jnp.where(first_east[0:1, PARTNER_SLOT : PARTNER_SLOT + 1] == float(s), row, top_east)
    moved = [fold[0:1], over[0:1], under[0:1], fold_west, over_west, under_west, top_east]
    moved = jnp.concatenate(moved + [jnp.zeros((1, cols), F32)], axis=0)
    moved = pltpu.roll(moved, cols - 2, 1)
    def pair(low, high):
        return jnp.concatenate([low, high, jnp.zeros((TILE - 2, cols), F32)], axis=0)

    along = lax.broadcasted_iota(jnp.int32, (TILE, cols), 1)
    place = along & 7
    side = pair(west[3:4], east[3:4])
    corner = pair(jnp.where(is_top, top_west, moved[4:5]), jnp.where(is_top, moved[6:7], over_east))
    side_north = jnp.where(place == last, pltpu.roll(corner, last, 1), shifted(side, 1, True))
    corner = jnp.where(has_south, pair(moved[5:6], under_east), 0.0)
    side_south = jnp.where(place == 0, corner, shifted(side, 1, False))
    side_force = jnp.take_along_axis(pair(west[0:1], east[0:1]), jnp.where(along < rows, 8 * along, 0) + FORCE_SLOT, axis=1)
    side_next = stencil(
        side, pair(ends_ref[0:1], east[4:5]), pair(west[4:5], ends_ref[1:2]), side_north, side_south,
        *[pair(west[k : k + 1], east[k : k + 1]) for k in (5, 6, 7)],
    ) + jnp.where(along < rows, side_force, 0.0)

    listed = [
        (west[3:4], east[3:4]),
        (side_next[0:1], side_next[1:2]),
        (jnp.where(is_top, moved[0:1], over[0:1]), jnp.where(is_top, fold[0:1], moved[1:2])),
        (under[0:1], moved[2:3]),
        (jnp.where(is_top, fold_east, moved[4:5]), jnp.where(is_top, moved[3:4], over_east)),
        (moved[5:6], under_east),
    ]
    lanes = {}
    for q, (low, high) in enumerate(listed):
        lanes[2 * q], lanes[(2 * q - 1) % cols] = low, high
    rim = fill(cols, lanes).T.reshape(theta_ref.shape)
    rim_ref[...] = rim

    def listing(q, field):
        return pltpu.roll(field, cols - 2 * q, field.ndim - 1) if q else field

    edges, inners = read_row(rim_ref, 0), read_row(rim_ref, 1)
    lane = lax.broadcasted_iota(jnp.int32, (levels, cols), 1)
    level = lax.broadcasted_iota(jnp.int32, (levels, cols), 0)
    ends = (lane == 0) | (lane == cols - 1)

    def forced(row, force):
        return row + jnp.where(level == 0, force, 0.0)

    flip = cols - 1 - lax.broadcasted_iota(jnp.int32, (8, cols), 1)
    flipped = jnp.take_along_axis(fold[:TILE], flip, axis=1)
    north_force = [jnp.where(is_top, flipped[k : k + 1], over[k : k + 1]) for k in (1, 2)]
    south_force = [under[1:2], under[2:3]]

    def beyond(rows_of, inside, outward, force, q):
        edge_row = stencil(
            rows_of[0], shifted(rows_of[0], 1, True), shifted(rows_of[0], 1, False),
            rows_of[1] if outward else inside, inside if outward else rows_of[1], *rows_of[3:],
        )
        edge_row = jnp.where(ends, listing(q, edges), forced(edge_row, force[0]))
        return edge_row, jnp.where(ends, listing(q, inners), forced(rows_of[2], force[1]))

    north_one, north_two = beyond(north, read_row(theta_ref, last), True, north_force, 2)
    south_one, south_two = beyond(south, read_row(theta_ref, 0), False, south_force, 3)
    south_one, south_two = jnp.where(has_south, south_one, 0.0), jnp.where(has_south, south_two, 0.0)
    shape = theta_ref.shape
    wide = lax.broadcasted_iota(jnp.int32, shape, 2)
    force = jnp.where(lax.broadcasted_iota(jnp.int32, shape, 0) == 0, force_ref[...][None], 0.0)
    inside = (lane >= 2) & (lane < cols - 2)
    more_north, more_south = inside & jnp.logical_not(here.even), inside & here.even
    top_row = read_row(next_ref, last) + jnp.where(more_north, read_row(points_ref.at[3], last) * north[0], 0.0)
    bottom_row = read_row(next_ref, 0) + jnp.where(more_south, read_row(points_ref.at[4], 0) * south[0], 0.0)
    tall_ref[:, TILE : 2 * TILE, :] = next_ref[...]
    write_row(tall_ref, TILE + last, top_row)
    write_row(tall_ref, TILE, bottom_row)

    def outer(row, further, inside, outward, rows_of, force_row, diagonal):
        result = stencil(
            row, jnp.where(lane == cols - 1, diagonal, shifted(row, 1, True)),
            jnp.where(lane == 0, diagonal, shifted(row, 1, False)),
            further if outward else inside, inside if outward else further, *rows_of[3:],
        )
        return forced(result, force_row)

    north_next = outer(north_one, north_two, top_row, True, north, north_force[0], listing(4, edges))
    south_next = outer(south_one, south_two, bottom_row, False, south, south_force[0], listing(5, edges))
    south_next = jnp.where(has_south, south_next, 0.0)

    def advance(sides, above, below):
        write_row(tall_ref, 2 * TILE, above)
        write_row(tall_ref, TILE - 1, below)
        t = tall_ref[:, TILE : 2 * TILE, :]
        east = jnp.where(wide == cols - 1, sides, shifted(t, 2, True))
        west = jnp.where(wide == 0, sides, shifted(t, 2, False))
        north, south = tall_ref[:, TILE + 1 : 2 * TILE + 1, :], tall_ref[:, TILE - 1 : 2 * TILE - 1, :]
        result = force
        for k, field in enumerate((t, east, west, north, south)):
            result = result + points_ref[k] * field
        return result

    tall_ref[:, TILE : 2 * TILE, :] = advance(rim, north_one, south_one)
    for k in range(flux_ref.shape[0]):
        for r in range(rows):
            flux_ref[k, r : r + 1, :] = total_ref[k : k + 1, r * cols : (r + 1) * cols]
    copies = [pltpu.make_async_copy(flux_ref, flux_hbm, sems.at[0])]
    copies[0].start()
    t = advance(listing(1, rim), north_next, south_next)
    for half in range(2):
        part = pl.ds(half * (levels // 2), levels // 2)
        result_ref[part] = t[half * (levels // 2) : (half + 1) * (levels // 2)]
        copies.append(pltpu.make_async_copy(result_ref.at[part], result_hbm.at[part], sems.at[1 + half]))
        copies[-1].start()
    for copy in copies:
        copy.wait()


def exchange(blocks):
    return lax.all_to_all(blocks, ("ns", "ew"), split_axis=0, concat_axis=0, tiled=True)


def swap(rows):
    pairs = [(i, i + 1) for i in range(0, lax.axis_size("ns"), 2)]
    return lax.ppermute(rows, "ns", pairs + [(b, a) for a, b in pairs])


def local(theta, velocity, diffusivity, land_mask, fold_partner, atm_flux, remap_src, remap_weights):
    levels, rows, cols = theta.shape
    fields = atm_flux.shape[2]
    shape = jax.ShapeDtypeStruct
    devices = lax.axis_size("ew") * lax.axis_size("ns")
    blocks = (devices, TILE, cols)
    room = 60 * 2**20 - 2 * max(0, 4 * devices * TILE * cols - 2**20)
    weights = remap_weights[0, 0]
    velocity, field, diffusivity, flux = bring(
        [velocity, theta, diffusivity, atm_flux[0, 0]], [pltpu.VMEM] * 4, room, "bring"
    )
    out, near = pl.pallas_call(
        first_kernel,
        out_shape=(pltpu.VMEM(blocks, BF16), pltpu.VMEM((KINDS, levels, cols), F32)),
        in_specs=[SMEM] + [VMEM] * 4,
        out_specs=(VMEM,) * 2,
        scratch_shapes=[pltpu.VMEM((2 * levels, TILE, cols), F32)],
        compiler_params=PARAMS,
        name="first",
    )(fold_partner, field, velocity, diffusivity, flux)
    first, near = exchange(out), swap(near)
    sources, weights = bring([remap_src[0], weights], [pltpu.SMEM, pltpu.VMEM], room, "load")
    points, columns, start = pl.pallas_call(
        side_kernel,
        out_shape=(
            pltpu.VMEM((5,) + theta.shape, F32), pltpu.VMEM((2, 3, cols), F32), pltpu.VMEM(theta.shape, F32),
        ),
        in_specs=[SMEM] + [VMEM] * 3,
        out_specs=(VMEM,) * 3,
        compiler_params=PARAMS,
        cost_estimate=pl.CostEstimate(flops=2**20, bytes_accessed=2**20, transcendentals=0),
        name="side",
    )(land_mask, field, velocity, diffusivity)
    total, force, after, ends, out = pl.pallas_call(
        middle_kernel,
        out_shape=(
            pltpu.VMEM((fields, rows * cols), F32), pltpu.VMEM((rows, cols), F32), pltpu.VMEM(theta.shape, F32),
            pltpu.VMEM((TILE, cols), F32), pltpu.VMEM(blocks, BF16),
        ),
        in_specs=[SMEM] * 3 + [VMEM] * 6,
        out_specs=(VMEM,) * 5,
        scratch_shapes=[pltpu.VMEM(theta.shape, F32)] * 2,
        compiler_params=PARAMS,
        name="middle",
    )(land_mask, fold_partner, sources, columns, points, start, weights, first, near)
    second = exchange(out)
    field, flux = pl.pallas_call(
        last_kernel,
        out_shape=(shape(theta.shape, F32), shape((fields, rows, cols), F32)),
        in_specs=[SMEM] + [VMEM] * 9,
        out_specs=(HBM, HBM),
        scratch_shapes=[
            pltpu.VMEM(theta.shape, F32), pltpu.VMEM((fields, rows, cols), F32), pltpu.VMEM(theta.shape, F32),
            pltpu.VMEM((levels, 3 * TILE, cols), F32), pltpu.VMEM((levels, TILE, cols), F32),
            pltpu.SemaphoreType.DMA((3,)),
        ],
        compiler_params=PARAMS,
        name="last",
    )(fold_partner, field, points, total, after, ends, force, first, second, near)
    return field, flux.reshape(1, 1, fields, rows * cols)


def solution(mesh):
    return jax.shard_map(
        local,
        mesh=mesh,
        in_specs=(
            P(None, "ns", "ew"),
            P(None, None, "ns", "ew"),
            P(None, "ns", "ew"),
            P("ns", "ew"),
            P("ew"),
            P("ns", "ew", None, None),
            P("ns", "ew", None),
            P("ns", "ew", None, None, None),
        ),
        out_specs=(P(None, "ns", "ew"), P("ns", "ew", None, None)),
        check_vma=False,
    )
```
